32 devices in a mesh: ch: 16 (over z, y, core), fq: 2 (over x).
Axes of the slice: x: 2, y: 2, z: 4, core: 2. Of those that a mesh axis runs over, the one named last changes fastest.
Arguments:
- spectra: bfloat16 [2, 48, 128, 2048], P(None, None, 'fq', 'ch')
- band_ids: int32 [128], P('fq'), may hold values from 0 to 7, as said below
Outputs:
- coherence: float32 [2, 4, 8, 2048, 128], P(None, None, 'fq', 'ch')
The draws below stay inside these ranges and needn't reach their ends.
Inputs may be any that keep to these rules, and one draw needn't show every extreme that they name: band_ids never falls, every band has at least one bin, and the bins of the g-th run of 64 bins belong only to bands g * 4 to (g + 1) * 4 - 1.
All inputs are finite; a program needn't handle non-finite values.
Results may differ from the reference program's by a relative error of at most 0.004.
Values may be sent and summed in bfloat16 or wider, within the bound.
No kernel may reach another device: no remote copies, remote signals or barrier semaphores. Data moves between devices by JAX's collectives and lax.ppermute only.
A program may use at most 64 MiB of HBM per device.

```python
import math
import jax
import jax.numpy as jnp
from jax import lax

F = 128
BANDS = 8
C = 128
W = 48
ROUNDS = 4
SMOOTH = 4
NCH = 2048
FBIN_DEV = 64
BAND_DEV = 4
N_FQ = 2


def draw_spectra(key, part):
    key = jax.random.fold_in(key, 1)
    subkeys = jax.random.split(key, 4)
    noise_base = jax.random.normal(subkeys[0], (2, W, F, NCH), jnp.float32)
    chan_spread = math.log(10.0)
    chan_scale = jnp.exp(jax.random.uniform(subkeys[1], (NCH,), jnp.float32) * chan_spread) / 3.0
    bin_scale = jnp.exp(jax.random.uniform(subkeys[2], (F,), jnp.float32) * math.log(4.0))
    rough = jnp.exp(jax.random.uniform(subkeys[3], (F, NCH), jnp.float32) * math.log(3.0))
    scales = chan_scale[None, :] * bin_scale[:, None] * rough
    return (noise_base * scales[None, None]).astype(jnp.bfloat16)


def draw_band_ids(key, part):
    key = jax.random.fold_in(key, 2)
    subkeys = jax.random.split(key, N_FQ)

    def one_group(group_key, group):
        cut_points = jnp.sort(jax.random.permutation(group_key, FBIN_DEV - 1)[:BAND_DEV - 1] + 1)
        positions = jnp.arange(FBIN_DEV, dtype=jnp.int32)
        local_band = jnp.sum((positions[:, None] >= cut_points[None, :]).astype(jnp.int32), axis=1)
        return group * BAND_DEV + local_band
    groups = jax.vmap(one_group)(subkeys, jnp.arange(N_FQ, dtype=jnp.int32))
    return groups.reshape(F).astype(jnp.int32)


def setup_inputs(seed: int = 0) -> dict:
    keys = jax.random.split(jax.random.key(seed), 3)
    spectra = draw_spectra(jax.random.fold_in(keys[2], 71), 0)
    band_ids = draw_band_ids(jax.random.fold_in(keys[2], 71), 0)
    return {"spectra": spectra, "band_ids": band_ids}


EPS = 1e-06

def whiten(spectra):
    values = spectra.astype(jnp.float32)
    power = lax.optimization_barrier(jnp.mean(values[0] * values[0] + values[1] * values[1], axis=0))
    padded = jnp.pad(power, ((SMOOTH, SMOOTH), (0, 0)))
    inside = jnp.pad(jnp.ones((F,), jnp.float32), SMOOTH)
    total = padded[0:F]
    counts = inside[0:F]
    for offset in range(1, 2 * SMOOTH + 1):
        total = total + padded[offset:offset + F]
        counts = counts + inside[offset:offset + F]
    level = total / counts[:, None]
    return (values * lax.rsqrt(level + EPS)[None, None]).astype(jnp.bfloat16)

def band_cross(own_block, far_block, onehot, norms):
    own_vals = own_block.astype(jnp.float32)
    far_vals = far_block.astype(jnp.float32)
    left_re = jnp.concatenate([own_vals[0], own_vals[1]], axis=0)
    left_im = jnp.concatenate([own_vals[1], -own_vals[0]], axis=0)
    right_side = jnp.concatenate([far_vals[0], far_vals[1]], axis=0)
    high = lax.Precision.HIGHEST
    cross_re = jnp.einsum('kfc,kfd->fcd', left_re, right_side, precision=high)
    cross_im = jnp.einsum('kfc,kfd->fcd', left_im, right_side, precision=high)
    band_re = jnp.einsum('fcd,fb->bcd', cross_re, onehot, precision=high)
    band_im = jnp.einsum('fcd,fb->bcd', cross_im, onehot, precision=high)
    return jnp.stack([band_re, band_im]) / norms[None, :, None, None]

def reference(spectra, band_ids):
    whitened = whiten(spectra)
    onehot = (band_ids[:, None] == jnp.arange(BANDS, dtype=jnp.int32)[None, :]).astype(jnp.float32)
    norms = jnp.sqrt(W * lax.optimization_barrier(jnp.sum(onehot, axis=0)))
    blocks = NCH // C
    own_blocks = jnp.moveaxis(whitened.reshape(2, W, F, blocks, C), 3, 0)
    results = []
    for offset in range(1, ROUNDS + 1):
        partner = jnp.roll(whitened, offset * C, axis=3)
        far_blocks = jnp.moveaxis(partner.reshape(2, W, F, blocks, C), 3, 0)
        mapped = lax.map(lambda pair: band_cross(pair[0], pair[1], onehot, norms), (own_blocks, far_blocks))
        mapped = jnp.transpose(mapped, (1, 2, 0, 3, 4)).reshape(2, BANDS, NCH, C)
        results.append(mapped)
    return jnp.stack(results, axis=1)
```

```python
import functools

import jax
import jax.numpy as jnp
from jax import lax
from jax.experimental import pallas as pl
from jax.experimental.pallas import tpu as pltpu
from jax.sharding import PartitionSpec as P

BANDS = 8
ROUNDS = 4
SMOOTH = 4
EPS = 1e-06

GROUP = 16
CHUNKS = 6
VMEM_LIMIT = 24 * 1024 * 1024


def vmem():
    return pl.BlockSpec(memory_space=pltpu.VMEM)


def smem():
    return pl.BlockSpec(memory_space=pltpu.SMEM)


def params():
    return pltpu.CompilerParams(vmem_limit_bytes=VMEM_LIMIT)


def power_kernel(x_ref, power_ref):
    rows = x_ref.shape[0]

    def step(i, total):
        value = x_ref[i].astype(jnp.float32)
        return total + value * value

    total = lax.fori_loop(0, rows, step, jnp.zeros(power_ref.shape, jnp.float32), unroll=8)
    power_ref[...] = total / (rows // 2)


def left_kernel(where_ref, x_ref, power_ref, halo_ref, scale_ref, left_ref, padded):
    fq, bin_total = where_ref[0], where_ref[1]
    rows, width, channels = x_ref.shape
    padded[...] = jnp.zeros_like(padded)
    padded[8 : 8 + width, :] = power_ref[...]

    @pl.when(fq > 0)
    def _():
        padded[8 - SMOOTH : 8, :] = halo_ref[...]

    @pl.when(fq == 0)
    def _():
        padded[8 + width : 8 + width + SMOOTH, :] = halo_ref[...]

    total = padded[8 - SMOOTH : 8 - SMOOTH + width, :]
    for offset in range(1, 2 * SMOOTH + 1):
        total = total + padded[8 - SMOOTH + offset : 8 - SMOOTH + offset + width, :]
    bins = fq * width + lax.broadcasted_iota(jnp.int32, (width, channels), 0)
    counts = jnp.minimum(bins + SMOOTH, bin_total - 1) - jnp.maximum(bins - SMOOTH, 0) + 1
    scale_ref[...] = lax.rsqrt(total / counts.astype(jnp.float32) + EPS)

    span = 16 * GROUP
    pieces = rows // 16
    for group in range(width // GROUP):
        bins_here = slice(group * GROUP, (group + 1) * GROUP)
        scale = scale_ref[bins_here, :]
        for piece in range(pieces):
            raw = x_ref[piece * 16 : (piece + 1) * 16, bins_here, :].astype(jnp.float32)
            white = (raw * scale[None]).reshape(span, channels)
            turned = white.T
            here = slice(piece * span, (piece + 1) * span)
            left_ref[group, :channels, here] = turned.astype(jnp.bfloat16)
            if piece < pieces // 2:
                there = slice((piece + pieces // 2) * span, (piece + pieces // 2 + 1) * span)
                left_ref[group, channels:, there] = (-turned).astype(jnp.bfloat16)
            else:
                there = slice((piece - pieces // 2) * span, (piece - pieces // 2 + 1) * span)
                left_ref[group, channels:, there] = turned.astype(jnp.bfloat16)


def cross_kernel(
    start, first, last, where_ref, norm_ref, left_ref, bands_ref, scales_ref, *refs
):
    rights = refs[:ROUNDS]
    out_ref = refs[-1]
    if first:
        out_ref[...] = jnp.zeros_like(out_ref)
    else:
        out_ref[...] = refs[ROUNDS][...]
    rows, width, channels = rights[0].shape
    span = rows * GROUP
    core = where_ref[0]
    rounds = (2 - 2 * core, 2 * core, 1, 3)
    for group in range(width // GROUP):
        bins_here = slice(group * GROUP, (group + 1) * GROUP)
        left = left_ref[group, :, start * GROUP : (start + rows) * GROUP]

        def one_band(band, carry):
            inside = bands_ref[bins_here, :] == band
            columns = []
            for index, right in enumerate(rights):
                scale = jnp.where(inside, scales_ref[index, bins_here, :], 0.0)
                raw = right[:, bins_here, :].astype(jnp.float32)
                columns.append((raw * scale[None]).astype(jnp.bfloat16).reshape(span, channels))
            product = jnp.dot(
                left, jnp.concatenate(columns, axis=1), preferred_element_type=jnp.float32
            )
            for index, turn in enumerate(rounds):
                lanes = slice(index * channels, (index + 1) * channels)
                out_ref[0, turn, band] += product[:channels, lanes]
                out_ref[1, turn, band] += product[channels:, lanes]
            return carry

        lax.fori_loop(where_ref[1 + 2 * group], where_ref[2 + 2 * group] + 1, one_band, 0)
    if last:
        for band in range(out_ref.shape[2]):
            out_ref[:, :, band] = out_ref[:, :, band] / norm_ref[band]


def shards(spectra, band_ids):
    parts, windows, width, channels = spectra.shape
    rows = parts * windows
    count = lax.axis_size("ch")
    fq_count = lax.axis_size("fq")
    index = lax.axis_index("ch")
    fq = lax.axis_index("fq")
    core = index % 2
    odd_chip = (index // 2) % 2

    ahead = [(i, (i + 4) % count) for i in range(count)]
    beside = [(i, i ^ 2) for i in range(count)]
    mate = [(i, i ^ 1) for i in range(count)]

    own = spectra.reshape(rows, width, channels)
    size = rows // CHUNKS

    def spread(value):
        two = lax.ppermute(value, "ch", ahead)
        one = lax.ppermute(jnp.where(odd_chip == 1, two, value), "ch", beside)
        mixed = lax.ppermute(jnp.where(core == 0, value, two), "ch", mate)
        other = lax.ppermute(one, "ch", mate)
        return mixed, other, one, two

    chunks = [spread(own[k * size : (k + 1) * size]) for k in range(CHUNKS)]

    power = pl.pallas_call(
        power_kernel,
        out_shape=jax.ShapeDtypeStruct((width, channels), jnp.float32),
        in_specs=[vmem()],
        out_specs=vmem(),
        compiler_params=params(),
        name="power",
    )(own)
    edge = jnp.where(fq == 0, power[width - SMOOTH :], power[:SMOOTH])
    halo = lax.ppermute(edge, "fq", [(0, 1), (1, 0)])
    groups = width // GROUP
    place = jnp.stack([fq, width * fq_count]).astype(jnp.int32)
    scale, left = pl.pallas_call(
        left_kernel,
        out_shape=(
            jax.ShapeDtypeStruct((width, channels), jnp.float32),
            jax.ShapeDtypeStruct((groups, 2 * channels, rows * GROUP), jnp.bfloat16),
        ),
        in_specs=[smem(), vmem(), vmem(), vmem()],
        out_specs=(vmem(), vmem()),
        scratch_shapes=[pltpu.VMEM((width + 16, channels), jnp.float32)],
        compiler_params=params(),
        name="left",
    )(place, own, power, halo)
    scales = jnp.stack(spread(scale))

    band_width = BANDS // fq_count
    local_band = band_ids - fq * band_width
    onehot = (local_band[:, None] == jnp.arange(band_width, dtype=jnp.int32)[None, :]).astype(
        jnp.float32
    )
    norms = jnp.sqrt(windows * jnp.sum(onehot, axis=0))
    bands = jnp.broadcast_to(local_band[:, None], (width, channels))
    ends = jnp.stack([local_band[0::GROUP], local_band[GROUP - 1 :: GROUP]], axis=1)
    where = jnp.concatenate([core[None], ends.reshape(-1)]).astype(jnp.int32)

    shape = jax.ShapeDtypeStruct((2, ROUNDS, band_width, channels, channels), jnp.float32)
    total = None
    for k, rights in enumerate(chunks):
        first, last = k == 0, k == CHUNKS - 1
        operands = [where, norms, left, bands, scales, *rights]
        if not first:
            operands.append(total)
        total = pl.pallas_call(
            functools.partial(cross_kernel, k * size, first, last),
            out_shape=shape,
            in_specs=[smem(), smem()] + [vmem()] * (len(operands) - 2),
            out_specs=vmem(),
            input_output_aliases={} if first else {len(operands) - 1: 0},
            compiler_params=params(),
            name="cross",
        )(*operands)
    return total


def solution(mesh):
    placed = (P(None, None, "fq", "ch"), P("fq"))
    return jax.shard_map(
        shards,
        mesh=mesh,
        in_specs=placed,
        out_specs=P(None, None, "fq", "ch", None),
        check_vma=False,
    )
```

```python
import functools

import jax
import jax.numpy as jnp
from jax import lax
from jax.experimental import pallas as pl
from jax.experimental.pallas import tpu as pltpu
from jax.sharding import PartitionSpec as P

BANDS = 8
ROUNDS = 4
SMOOTH = 4
EPS = 1e-06

GROUP = 16
PIECE = 8
RAW = 3
TERMS = 3
DEPTH = 2
AHEAD = 2
CHAIN = 1
SETS = (4, 4, 2, 1, 1)
SEND_AFTER = (5, 10, 12, 12, 12)
CROSS_BEFORE = (9, 11, 12, 12, 12)
VMEM_LIMIT = 16 * 1024 * 1024


def vmem():
    return pl.BlockSpec(memory_space=pltpu.VMEM)


def smem():
    return pl.BlockSpec(memory_space=pltpu.SMEM)


def call(kernel, name, out_shape, in_specs, flops, moved, **more):
    return pl.pallas_call(
        kernel,
        out_shape=out_shape,
        in_specs=in_specs,
        out_specs=jax.tree.map(lambda _: vmem(), out_shape),
        compiler_params=pltpu.CompilerParams(vmem_limit_bytes=VMEM_LIMIT),
        cost_estimate=pl.CostEstimate(flops=flops, bytes_accessed=moved, transcendentals=0),
        name=name,
        **more,
    )


def power_kernel(x_ref, power_ref, edge_ref, *pieces):
    rows, width, _ = x_ref.shape
    for index, piece in enumerate(pieces):
        piece[...] = x_ref[index * PIECE : (index + 1) * PIECE]

    def step(i, total):
        value = x_ref[i].astype(jnp.float32)
        return total + value * value

    total = lax.fori_loop(0, rows, step, jnp.zeros(power_ref.shape, jnp.float32), unroll=8)
    power = total / (rows // 2)
    power_ref[...] = power
    low = lax.axis_index("fq") == 0
    edge_ref[...] = jnp.where(low, power[width - SMOOTH :], power[:SMOOTH])


def left_kernel(x_ref, power_ref, halo_ref, left_ref, *refs):
    pieces, padded = refs[:-1], refs[-1]
    fq = lax.axis_index("fq")
    rows, width, channels = x_ref.shape
    bin_total = width * lax.axis_size("fq")
    padded[...] = jnp.zeros_like(padded)
    padded[8 : 8 + width, :] = power_ref[...]

    @pl.when(fq > 0)
    def _():
        padded[8 - SMOOTH : 8, :] = halo_ref[...]

    @pl.when(fq == 0)
    def _():
        padded[8 + width : 8 + width + SMOOTH, :] = halo_ref[...]

    total = padded[8 - SMOOTH : 8 - SMOOTH + width, :]
    for offset in range(1, 2 * SMOOTH + 1):
        total = total + padded[8 - SMOOTH + offset : 8 - SMOOTH + offset + width, :]
    bins = fq * width + lax.broadcasted_iota(jnp.int32, (width, channels), 0)
    counts = jnp.minimum(bins + SMOOTH, bin_total - 1) - jnp.maximum(bins - SMOOTH, 0) + 1
    scale = lax.rsqrt(total / counts.astype(jnp.float32) + EPS)
    rest = scale
    for term in range(TERMS):
        part = rest.astype(jnp.bfloat16)
        pieces[0][PIECE + term] = part
        rest = rest - part.astype(jnp.float32)

    step = 2 * PIECE
    span = step * GROUP
    steps = rows // step
    for group in range(width // GROUP):
        here = slice(group * GROUP, (group + 1) * GROUP)
        for index in range(steps):
            raw = x_ref[index * step : (index + 1) * step, here, :].astype(jnp.float32)
            white = (raw * scale[here][None]).astype(jnp.bfloat16)
            for half in range(2):
                piece = 2 * index + half - RAW
                if piece >= 0:
                    pieces[piece][:PIECE, here, :] = white[half * PIECE : (half + 1) * PIECE]
            turned = white.reshape(span, channels).T
            left_ref[group, :channels, index * span : (index + 1) * span] = turned
            if index < steps // 2:
                there = index + steps // 2
                turned = -turned
            else:
                there = index - steps // 2
            left_ref[group, channels:, there * span : (there + 1) * span] = turned


def cross_kernel(start, pieces, first, bounds_ref, norm_ref, left_ref, mate_ref, *refs):
    count = len(pieces)
    ones, twos = refs[:count], refs[count : 2 * count]
    out_ref = refs[-1]
    core = lax.axis_index("ch") % 2
    rounds = (2 - 2 * core, 2 * core, 1, 3)
    offsets = [sum(pieces[:k]) for k in range(count)]
    held = sum(pieces)
    rights = [
        [(mate_ref, offset) for offset in offsets],
        [(mate_ref, held + offset) for offset in offsets],
        [(ref, 0) for ref in ones],
        [(ref, 0) for ref in twos],
    ]
    width, channels = mate_ref.shape[1:]
    lanes = slice(start * GROUP, (start + count * PIECE) * GROUP)
    span = count * PIECE * GROUP

    if first:
        out_ref[...] = jnp.zeros_like(out_ref)
    else:
        out_ref[...] = refs[2 * count][...]

    def column(right, here):
        scale = None
        if first:
            ref, offset = right[RAW]
            for term in range(TERMS):
                part = ref[offset + PIECE + term, here, :].astype(jnp.float32)
                scale = part if scale is None else scale + part
        blocks = []
        for index, (ref, offset) in enumerate(right):
            block = ref[offset : offset + PIECE, here, :]
            if first and index < RAW:
                block = (block.astype(jnp.float32) * scale[None]).astype(jnp.bfloat16)
            blocks.append(block.reshape(PIECE * GROUP, channels))
        return jnp.concatenate(blocks, axis=0)

    def add(group, here, band, low, high):
        bins = group * GROUP + lax.broadcasted_iota(jnp.int32, (1, span), 1) % GROUP
        inside = ((bins >= low) & (bins < high)).astype(jnp.float32).astype(jnp.bfloat16)
        left = left_ref[group, :, lanes] * inside
        columns = jnp.concatenate([column(right, here) for right in rights], axis=1)
        product = jnp.dot(left, columns, preferred_element_type=jnp.float32)
        product = product / norm_ref[band]
        for index, turn in enumerate(rounds):
            part = slice(index * channels, (index + 1) * channels)
            out_ref[0, turn, band] += product[:channels, part]
            out_ref[1, turn, band] += product[channels:, part]

    bands = out_ref.shape[2]
    for group in range(width // GROUP):
        band = sum((bounds_ref[k] <= group * GROUP).astype(jnp.int32) for k in range(1, bands))
        here = slice(group * GROUP, (group + 1) * GROUP)
        add(group, here, band, bounds_ref[band], bounds_ref[band + 1])
    for band in range(1, bands):
        low, high = bounds_ref[band], bounds_ref[band + 1]

        @pl.when(low % GROUP != 0)
        def _():
            group = low // GROUP
            add(group, pl.ds(pl.multiple_of(group * GROUP, GROUP), GROUP), band, low, high)


def shards(spectra, band_ids):
    parts, windows, width, channels = spectra.shape
    rows = parts * windows
    count = lax.axis_size("ch")
    fq_count = lax.axis_size("fq")
    index = lax.axis_index("ch")
    fq = lax.axis_index("fq")
    even_core = index % 2 == 0
    odd_chip = (index // 2) % 2 == 1

    ahead = [(i, (i + 4) % count) for i in range(count)]
    beside = [(i, i ^ 2) for i in range(count)]
    mate = [(i, i ^ 1) for i in range(count)]

    own = spectra.reshape(rows, width, channels)
    total_pieces = rows // PIECE
    heights = [PIECE + (TERMS if k == RAW else 0) for k in range(total_pieces)]
    block = jax.ShapeDtypeStruct((width, channels), jnp.float32)
    edge = jax.ShapeDtypeStruct((SMOOTH, channels), jnp.float32)
    held = [jax.ShapeDtypeStruct((h, width, channels), jnp.bfloat16) for h in heights]
    groups = width // GROUP
    left_shape = jax.ShapeDtypeStruct((groups, 2 * channels, rows * GROUP), jnp.bfloat16)
    nbytes = rows * width * channels * 2

    power, edge, *early = call(
        power_kernel, "power", (block, edge, *held[:RAW]), [vmem()], 3 * nbytes, nbytes
    )(own)
    halo = lax.ppermute(edge, "fq", [(0, 1), (1, 0)])
    left, *late = call(
        left_kernel,
        "left",
        (left_shape, *held[RAW:]),
        [vmem()] * 3,
        3 * nbytes,
        4 * nbytes,
        scratch_shapes=[pltpu.VMEM((width + 16, channels), jnp.float32)],
    )(own, power, halo)
    mine = early + late

    band_width = BANDS // fq_count
    local_band = band_ids - fq * band_width
    below = local_band[:, None] < jnp.arange(band_width + 1, dtype=jnp.int32)[None, :]
    bounds = jnp.sum(below.astype(jnp.int32), axis=0)
    norms = jnp.sqrt(windows * (bounds[1:] - bounds[:-1]).astype(jnp.float32))

    shape = jax.ShapeDtypeStruct((2, ROUNDS, band_width, channels, channels), jnp.float32)

    def after(value, other):
        return lax.optimization_barrier((value, other))

    twos, ones, mixed, others, totals = {}, {}, {}, {}, {}
    sets = [range(sum(SETS[:s]), sum(SETS[: s + 1])) for s in range(len(SETS))]

    def send(s):
        these = sets[s]
        block = jnp.concatenate([mixed[i] for i in these] + [ones[i] for i in these], axis=0)
        if SEND_AFTER[s] < total_pieces:
            block, twos[SEND_AFTER[s]] = after(block, twos[SEND_AFTER[s]])
        others[s] = lax.ppermute(block, "ch", mate)

    def cross(s):
        these = sets[s]
        operands = [bounds, norms, left, others[s], *(ones[i] for i in these)]
        operands += [twos[i] for i in these]
        if s > 0:
            operands.append(totals[s - 1])
        totals[s] = call(
            functools.partial(cross_kernel, these[0] * PIECE, [heights[i] for i in these], s == 0),
            "cross",
            shape,
            [smem(), smem()] + [vmem()] * (len(operands) - 2),
            16 * len(these) * PIECE * width * channels * channels,
            12 * len(these) * PIECE * width * channels,
        )(*operands)

    for k in range(DEPTH):
        twos[k] = lax.ppermute(mine[k], "ch", ahead)
    for k in range(total_pieces):
        for s in range(len(SETS)):
            if CROSS_BEFORE[s] == k:
                cross(s)
                twos[k], totals[s] = after(twos[k], totals[s])
        if k >= AHEAD:
            twos[k], ones[k - AHEAD] = after(twos[k], ones[k - AHEAD])
        if CHAIN and k > 0:
            twos[k], mixed[k - 1] = after(twos[k], mixed[k - 1])
        if k + DEPTH < total_pieces:
            twos[k], later = after(twos[k], mine[k + DEPTH])
            twos[k + DEPTH] = lax.ppermute(later, "ch", ahead)
        ones[k] = lax.ppermute(jnp.where(odd_chip, twos[k], mine[k]), "ch", beside)
        mixed[k] = jnp.where(even_core, mine[k], twos[k])
        for s in range(len(SETS)):
            if SEND_AFTER[s] == k:
                send(s)
    for s in range(len(SETS)):
        if s not in others:
            send(s)
    for s in range(len(SETS)):
        if s not in totals:
            cross(s)
    total = totals[len(SETS) - 1]
    return total


def solution(mesh):
    placed = (P(None, None, "fq", "ch"), P("fq"))
    return jax.shard_map(
        shards,
        mesh=mesh,
        in_specs=placed,
        out_specs=P(None, None, "fq", "ch", None),
        check_vma=False,
    )
```

```python
import functools

import jax
import jax.numpy as jnp
from jax import lax
from jax.experimental import pallas as pl
from jax.experimental.pallas import tpu as pltpu
from jax.sharding import PartitionSpec as P

BANDS = 8
ROUNDS = 4
SMOOTH = 4
EPS = 1e-06

GROUP = 16
PIECE = 8
RAW = 3
TERMS = 3
DEPTH = 3
AHEAD = 2
MATES = (6, 4, 2)
MATE_AFTER = (8, 11, 12)
CROSSES = (1, 2)
CROSS_BEFORE = (12, 12)
VMEM_LIMIT = 16 * 1024 * 1024


def vmem():
    return pl.BlockSpec(memory_space=pltpu.VMEM)


def smem():
    return pl.BlockSpec(memory_space=pltpu.SMEM)


def hbm():
    return pl.BlockSpec(memory_space=pl.ANY)


def call(kernel, name, out_shape, in_specs, out_specs, flops, moved, **more):
    return pl.pallas_call(
        kernel,
        out_shape=out_shape,
        in_specs=in_specs,
        out_specs=out_specs,
        compiler_params=pltpu.CompilerParams(vmem_limit_bytes=VMEM_LIMIT),
        cost_estimate=pl.CostEstimate(flops=flops, bytes_accessed=moved, transcendentals=0),
        name=name,
        **more,
    )


def power_kernel(x_ref, power_ref, edge_ref, *refs):
    pieces, sems = refs[:-1], refs[-1]
    copies = [
        pltpu.make_async_copy(x_ref.at[pl.ds(k * PIECE, PIECE)], piece, sems.at[k])
        for k, piece in enumerate(pieces)
    ]
    for copy in copies:
        copy.start()
    total = jnp.zeros(power_ref.shape, jnp.float32)
    for copy, piece in zip(copies, pieces):
        copy.wait()

        def step(i, total):
            value = piece[i].astype(jnp.float32)
            return total + value * value

        total = lax.fori_loop(0, PIECE, step, total, unroll=8)
    width = power_ref.shape[0]
    power = total / (len(pieces) * PIECE // 2)
    power_ref[...] = power
    low = lax.axis_index("fq") == 0
    edge_ref[...] = jnp.where(low, power[width - SMOOTH :], power[:SMOOTH])


def left_kernel(count, power_ref, halo_ref, *refs):
    raws, left_ref, whites, padded = refs[:count], refs[count], refs[count + 1 : -1], refs[-1]
    fq = lax.axis_index("fq")
    width, channels = power_ref.shape
    bin_total = width * lax.axis_size("fq")
    padded[...] = jnp.zeros_like(padded)
    padded[8 : 8 + width, :] = power_ref[...]

    @pl.when(fq > 0)
    def _():
        padded[8 - SMOOTH : 8, :] = halo_ref[...]

    @pl.when(fq == 0)
    def _():
        padded[8 + width : 8 + width + SMOOTH, :] = halo_ref[...]

    total = padded[8 - SMOOTH : 8 - SMOOTH + width, :]
    for offset in range(1, 2 * SMOOTH + 1):
        total = total + padded[8 - SMOOTH + offset : 8 - SMOOTH + offset + width, :]
    bins = fq * width + lax.broadcasted_iota(jnp.int32, (width, channels), 0)
    counts = jnp.minimum(bins + SMOOTH, bin_total - 1) - jnp.maximum(bins - SMOOTH, 0) + 1
    scale = lax.rsqrt(total / counts.astype(jnp.float32) + EPS)
    rest = scale
    for term in range(TERMS):
        part = rest.astype(jnp.bfloat16)
        whites[0][PIECE + term] = part
        rest = rest - part.astype(jnp.float32)

    span = PIECE * GROUP
    for index in range(count):
        for group in range(width // GROUP):
            here = slice(group * GROUP, (group + 1) * GROUP)
            raw = raws[index][:, here, :].astype(jnp.float32)
            white = (raw * scale[here][None]).astype(jnp.bfloat16)
            if index >= RAW:
                whites[index - RAW][:PIECE, here, :] = white
            turned = white.reshape(span, channels).T
            left_ref[group, :channels, index * span : (index + 1) * span] = turned
            if index < count // 2:
                there = index + count // 2
                turned = -turned
            else:
                there = index - count // 2
            left_ref[group, channels:, there * span : (there + 1) * span] = turned


def cross_kernel(start, sets, first, last, bounds_ref, norm_ref, left_ref, *refs):
    mates, refs = refs[: len(sets)], refs[len(sets) :]
    heights = [height for these in sets for height in these]
    count = len(heights)
    ones, twos, refs = refs[:count], refs[count : 2 * count], refs[2 * count :]
    if not first:
        before_ref, refs = refs[0], refs[1:]
    out_ref = refs[0]
    sums = refs[1] if last else out_ref
    core = lax.axis_index("ch") % 2
    rounds = (2 - 2 * core, 2 * core, 1, 3)
    rights = [[], [], [(ref, 0) for ref in ones], [(ref, 0) for ref in twos]]
    for mate, these in zip(mates, sets):
        for half in range(2):
            for k in range(len(these)):
                rights[half].append((mate, half * sum(these) + sum(these[:k])))
    width, channels = mates[0].shape[1:]
    span = count * PIECE * GROUP
    lanes = slice(start * GROUP, start * GROUP + span)
    bands = sums.shape[2]
    groups = width // GROUP

    if first:
        sums[...] = jnp.zeros_like(sums)
    else:
        sums[...] = before_ref[...]

    def column(right, here):
        scale = None
        if first:
            ref, offset = right[RAW]
            for term in range(TERMS):
                part = ref[offset + PIECE + term, here, :].astype(jnp.float32)
                scale = part if scale is None else scale + part
        blocks = []
        for index, (ref, offset) in enumerate(right):
            block = ref[offset : offset + PIECE, here, :]
            if first and index < RAW:
                block = (block.astype(jnp.float32) * scale[None]).astype(jnp.bfloat16)
            blocks.append(block.reshape(PIECE * GROUP, channels))
        return jnp.concatenate(blocks, axis=0)

    def add(group, band):
        here = slice(group * GROUP, (group + 1) * GROUP)
        bins = group * GROUP + lax.broadcasted_iota(jnp.int32, (1, span), 1) % GROUP
        inside = (bins >= bounds_ref[band]) & (bins < bounds_ref[band + 1])
        left = left_ref[group, :, lanes] * inside.astype(jnp.float32).astype(jnp.bfloat16)
        columns = jnp.concatenate([column(right, here) for right in rights], axis=1)
        product = jnp.dot(left, columns, preferred_element_type=jnp.float32) * norm_ref[band]
        for index, turn in enumerate(rounds):
            part = slice(index * channels, (index + 1) * channels)
            sums[0, turn, band] += product[:channels, part]
            sums[1, turn, band] += product[channels:, part]

    def band_at(bin_index):
        return sum((bounds_ref[k] <= bin_index).astype(jnp.int32) for k in range(1, bands))

    def leave(band):
        return [
            pltpu.make_async_copy(sums.at[part, :, band], out_ref.at[part, :, band], refs[2].at[part, band])
            for part in range(2)
        ]

    for group in range(groups):
        low, high = band_at(group * GROUP), band_at((group + 1) * GROUP - 1)
        add(group, low)
        lax.fori_loop(low + 1, high + 1, lambda band, carry: add(group, band), None)
        if last:
            after = band_at((group + 1) * GROUP) if group + 1 < groups else bands

            def start_copies(band, carry):
                for copy in leave(band):
                    copy.start()

            lax.fori_loop(low, after, start_copies, None)
    if last:
        for band in range(bands):
            for copy in leave(band):
                copy.wait()


def shards(spectra, band_ids):
    parts, windows, width, channels = spectra.shape
    rows = parts * windows
    count = lax.axis_size("ch")
    fq_count = lax.axis_size("fq")
    index = lax.axis_index("ch")
    fq = lax.axis_index("fq")
    even_core = index % 2 == 0
    odd_chip = (index // 2) % 2 == 1

    ahead = [(i, (i + 4) % count) for i in range(count)]
    beside = [(i, i ^ 2) for i in range(count)]
    mate = [(i, i ^ 1) for i in range(count)]

    own = spectra.reshape(rows, width, channels)
    pieces = rows // PIECE
    heights = [PIECE + (TERMS if k == RAW else 0) for k in range(pieces)]
    block = jax.ShapeDtypeStruct((width, channels), jnp.float32)
    edge = jax.ShapeDtypeStruct((SMOOTH, channels), jnp.float32)
    plain = jax.ShapeDtypeStruct((PIECE, width, channels), jnp.bfloat16)
    held = [jax.ShapeDtypeStruct((h, width, channels), jnp.bfloat16) for h in heights]
    groups = width // GROUP
    left_shape = jax.ShapeDtypeStruct((groups, 2 * channels, rows * GROUP), jnp.bfloat16)
    nbytes = rows * width * channels * 2

    power, edge, *raws = call(
        power_kernel,
        "power",
        (block, edge, *[plain] * pieces),
        [hbm()],
        (vmem(),) * (2 + pieces),
        nbytes,
        nbytes,
        scratch_shapes=[pltpu.SemaphoreType.DMA((pieces,))],
    )(own)
    def after(value, other):
        return lax.optimization_barrier((value, other))

    band_width = BANDS // fq_count
    local_band = band_ids - fq * band_width
    below = local_band[:, None] < jnp.arange(band_width + 1, dtype=jnp.int32)[None, :]
    bounds = jnp.sum(below.astype(jnp.int32), axis=0)
    norms = 1.0 / jnp.sqrt(windows * (bounds[1:] - bounds[:-1]).astype(jnp.float32))
    power, norms = after(power, norms)

    halo = lax.ppermute(edge, "fq", [(0, 1), (1, 0)])
    left, *late = call(
        functools.partial(left_kernel, pieces),
        "left",
        (left_shape, *held[RAW:]),
        [vmem()] * (2 + pieces),
        (vmem(),) * (1 + pieces - RAW),
        nbytes,
        nbytes,
        scratch_shapes=[pltpu.VMEM((width + 16, channels), jnp.float32)],
    )(power, halo, *raws)
    mine = raws[:RAW] + late

    shape = jax.ShapeDtypeStruct((2, ROUNDS, band_width, channels, channels), jnp.float32)

    twos, ones, mixed, others, totals = {}, {}, {}, {}, {}
    mate_sets = [range(sum(MATES[:s]), sum(MATES[: s + 1])) for s in range(len(MATES))]
    cross_sets = [range(sum(CROSSES[:s]), sum(CROSSES[: s + 1])) for s in range(len(CROSSES))]

    def send(s):
        these = mate_sets[s]
        value = jnp.concatenate([mixed[i] for i in these] + [ones[i] for i in these], axis=0)
        if MATE_AFTER[s] < pieces:
            value, twos[MATE_AFTER[s]] = after(value, twos[MATE_AFTER[s]])
        others[s] = lax.ppermute(value, "ch", mate)

    def cross(s):
        sets = [mate_sets[t] for t in cross_sets[s]]
        these = [k for some in sets for k in some]
        first, last = s == 0, s == len(CROSSES) - 1
        operands = [bounds, norms, left, *(others[t] for t in cross_sets[s])]
        operands += [ones[k] for k in these] + [twos[k] for k in these]
        if not first:
            operands.append(totals[s - 1])
        scratch = []
        if last:
            scratch = [
                pltpu.VMEM(shape.shape, jnp.float32),
                pltpu.SemaphoreType.DMA((2, band_width)),
            ]
        totals[s] = call(
            functools.partial(
                cross_kernel,
                these[0] * PIECE,
                [[heights[k] for k in some] for some in sets],
                first,
                last,
            ),
            "cross",
            shape,
            [smem(), smem()] + [vmem()] * (len(operands) - 2),
            hbm() if last else vmem(),
            16 * len(these) * PIECE * width * channels * channels,
            12 * len(these) * PIECE * width * channels,
            scratch_shapes=scratch,
        )(*operands)

    for k in range(DEPTH):
        twos[k] = lax.ppermute(mine[k], "ch", ahead)
    for k in range(pieces):
        for s in range(len(CROSSES)):
            if CROSS_BEFORE[s] == k:
                cross(s)
                twos[k], totals[s] = after(twos[k], totals[s])
        if k >= AHEAD:
            twos[k], ones[k - AHEAD] = after(twos[k], ones[k - AHEAD])
        if k > 0:
            twos[k], mixed[k - 1] = after(twos[k], mixed[k - 1])
        if k + DEPTH < pieces:
            twos[k], later = after(twos[k], mine[k + DEPTH])
            twos[k + DEPTH] = lax.ppermute(later, "ch", ahead)
        ones[k] = lax.ppermute(jnp.where(odd_chip, twos[k], mine[k]), "ch", beside)
        mixed[k] = jnp.where(even_core, mine[k], twos[k])
        for s in range(len(MATES)):
            if MATE_AFTER[s] == k:
                send(s)
    for s in range(len(MATES)):
        if s not in others:
            send(s)
    for s in range(len(CROSSES)):
        if s not in totals:
            cross(s)
    return totals[len(CROSSES) - 1]


def solution(mesh):
    placed = (P(None, None, "fq", "ch"), P("fq"))
    return jax.shard_map(
        shards,
        mesh=mesh,
        in_specs=placed,
        out_specs=P(None, None, "fq", "ch", None),
        check_vma=False,
    )
```

```python
import functools

import jax
import jax.numpy as jnp
from jax import lax
from jax.experimental import pallas as pl
from jax.experimental.pallas import tpu as pltpu
from jax.sharding import PartitionSpec as P

BANDS = 8
ROUNDS = 4
SMOOTH = 4
EPS = 1e-06

GROUP = 16
PIECE = 12
RAW = 3
TERMS = 3
DEPTH = 3
AHEAD = 2
SETS = (4, 2, 2)
OTHER_AFTER = 1
NEAR_BEFORE = 7
CROSS_BEFORE = (6, 8)
VMEM_LIMIT = 16 * 1024 * 1024


def vmem():
    return pl.BlockSpec(memory_space=pltpu.VMEM)


def smem():
    return pl.BlockSpec(memory_space=pltpu.SMEM)


def hbm():
    return pl.BlockSpec(memory_space=pltpu.HBM)


def call(kernel, name, out_shape, in_specs, out_specs, flops, moved, **more):
    return pl.pallas_call(
        kernel,
        out_shape=out_shape,
        in_specs=in_specs,
        out_specs=out_specs,
        compiler_params=pltpu.CompilerParams(vmem_limit_bytes=VMEM_LIMIT),
        cost_estimate=pl.CostEstimate(flops=flops, bytes_accessed=moved, transcendentals=0),
        name=name,
        **more,
    )


def power_kernel(x_ref, power_ref, edge_ref, *pieces):
    rows, width, _ = x_ref.shape
    for index, piece in enumerate(pieces):
        piece[...] = x_ref[index * PIECE : (index + 1) * PIECE]

    def step(i, total):
        value = x_ref[i].astype(jnp.float32)
        return total + value * value

    total = lax.fori_loop(0, rows, step, jnp.zeros(power_ref.shape, jnp.float32), unroll=8)
    power = total / (rows // 2)
    power_ref[...] = power
    low = lax.axis_index("fq") == 0
    edge_ref[...] = jnp.where(low, power[width - SMOOTH :], power[:SMOOTH])


def left_kernel(x_ref, power_ref, halo_ref, left_ref, *refs):
    whites, padded = refs[:-1], refs[-1]
    count = x_ref.shape[0] // PIECE
    fq = lax.axis_index("fq")
    width, channels = power_ref.shape
    bin_total = width * lax.axis_size("fq")
    padded[...] = jnp.zeros_like(padded)
    padded[8 : 8 + width, :] = power_ref[...]

    @pl.when(fq > 0)
    def _():
        padded[8 - SMOOTH : 8, :] = halo_ref[...]

    @pl.when(fq == 0)
    def _():
        padded[8 + width : 8 + width + SMOOTH, :] = halo_ref[...]

    total = padded[8 - SMOOTH : 8 - SMOOTH + width, :]
    for offset in range(1, 2 * SMOOTH + 1):
        total = total + padded[8 - SMOOTH + offset : 8 - SMOOTH + offset + width, :]
    bins = fq * width + lax.broadcasted_iota(jnp.int32, (width, channels), 0)
    counts = jnp.minimum(bins + SMOOTH, bin_total - 1) - jnp.maximum(bins - SMOOTH, 0) + 1
    scale = lax.rsqrt(total / counts.astype(jnp.float32) + EPS)
    rest = scale
    for term in range(TERMS):
        part = rest.astype(jnp.bfloat16)
        whites[0][PIECE + term] = part
        rest = rest - part.astype(jnp.float32)

    span = 2 * PIECE * GROUP
    for pair in range(count // 2):
        for group in range(width // GROUP):
            here = slice(group * GROUP, (group + 1) * GROUP)
            blocks = []
            for index in (2 * pair, 2 * pair + 1):
                raw = x_ref[index * PIECE : (index + 1) * PIECE, here, :].astype(jnp.float32)
                white = (raw * scale[here][None]).astype(jnp.bfloat16)
                if index >= RAW:
                    whites[index - RAW][:PIECE, here, :] = white
                blocks.append(white.reshape(PIECE * GROUP, channels))
            turned = jnp.concatenate(blocks, axis=0).T
            left_ref[group, :, pair * span : (pair + 1) * span] = turned


def band_at(bounds_ref, bands, bin_index):
    return sum((bounds_ref[k] <= bin_index).astype(jnp.int32) for k in range(1, bands))


def each_band(bounds_ref, groups, bands, add):
    for group in range(groups):
        low = band_at(bounds_ref, bands, group * GROUP)
        high = band_at(bounds_ref, bands, (group + 1) * GROUP - 1)
        add(group, low)
        lax.fori_loop(low + 1, high + 1, lambda band, carry: add(group, band), None)


def lefts(turned_ref, bounds_ref, group, band, start, stop):
    half = turned_ref.shape[2] // 2
    bins = group * GROUP + lax.broadcasted_iota(jnp.int32, (1, stop - start), 1) % GROUP
    inside = (bins >= bounds_ref[band]) & (bins < bounds_ref[band + 1])
    inside = inside.astype(jnp.float32).astype(jnp.bfloat16)
    real = turned_ref[group, :, start:stop] * inside
    parts = []
    if start < half:
        end = min(stop, half)
        parts.append(turned_ref[group, :, start + half : end + half] * inside[:, : end - start])
    if stop > half:
        begin = max(start, half)
        parts.append(turned_ref[group, :, begin - half : stop - half] * -inside[:, begin - start :])
    return [real, parts[0] if len(parts) == 1 else jnp.concatenate(parts, axis=1)]


def near_kernel(bounds_ref, norm_ref, own_ref, mate_ref, out_ref):
    groups, channels, span = own_ref.shape
    bands = out_ref.shape[1]
    out_ref[...] = jnp.zeros_like(out_ref)

    def add(group, band):
        left = jnp.concatenate(lefts(own_ref, bounds_ref, group, band, 0, span), axis=0)
        product = lax.dot_general(
            left, mate_ref[group], (((1,), (1,)), ((), ())), preferred_element_type=jnp.float32
        )
        product = product * norm_ref[band]
        out_ref[0, band] += product[:channels]
        out_ref[1, band] += product[channels:]

    @pl.when(lax.axis_index("ch") % 2 == 1)
    def _():
        each_band(bounds_ref, groups, bands, add)


def cross_kernel(start, count, kinds, first, last, bounds_ref, norm_ref, own_ref, mate_ref, *refs):
    rights = [refs[k * count : (k + 1) * count] for k in range(kinds)]
    refs = refs[kinds * count :]
    if not first:
        befores, refs = refs[:kinds], refs[kinds:]
    if last:
        beyond_ref, refs = refs[0], refs[1:]
    sums = refs[:kinds]
    width, channels = rights[0][0].shape[1:]
    bands = sums[0].shape[2]
    lanes = start * GROUP, (start + count * PIECE) * GROUP
    for k in range(kinds):
        sums[k][...] = jnp.zeros_like(sums[k]) if first else befores[k][...]

    def column(right, here):
        scale = None
        if first:
            for term in range(TERMS):
                part = right[RAW][PIECE + term, here, :].astype(jnp.float32)
                scale = part if scale is None else scale + part
        blocks = []
        for index, ref in enumerate(right):
            block = ref[:PIECE, here, :]
            if first and index < RAW:
                block = (block.astype(jnp.float32) * scale[None]).astype(jnp.bfloat16)
            blocks.append(block.reshape(PIECE * GROUP, channels))
        return jnp.concatenate(blocks, axis=0)

    def add(group, band):
        here = slice(group * GROUP, (group + 1) * GROUP)
        left = jnp.concatenate(
            lefts(own_ref, bounds_ref, group, band, *lanes)
            + lefts(mate_ref, bounds_ref, group, band, *lanes),
            axis=0,
        )
        right = jnp.concatenate([column(right, here) for right in rights], axis=1)
        product = jnp.dot(left, right, preferred_element_type=jnp.float32) * norm_ref[band]
        for k in range(kinds):
            for owner in range(2):
                for part in range(2):
                    row = (2 * owner + part) * channels
                    sums[k][part, owner, band] += product[
                        row : row + channels, k * channels : (k + 1) * channels
                    ]

    each_band(bounds_ref, width // GROUP, bands, add)
    if last:
        refs[kinds][0] = sums[0][:, 1].astype(jnp.bfloat16)
        refs[kinds][1] = beyond_ref[:, 1].astype(jnp.bfloat16)


def put_own_kernel(one_ref, two_ref, out_ref, sems):
    copies = [
        pltpu.make_async_copy(value.at[:, 0], out_ref.at[:, turn], sems.at[k])
        for k, (turn, value) in enumerate(((1, one_ref), (3, two_ref)))
    ]
    for copy in copies:
        copy.start()
    for copy in copies:
        copy.wait()


def put_got_kernel(got_ref, near_ref, before_ref, out_ref, wide, sems):
    core = lax.axis_index("ch") % 2
    wide[0] = got_ref[0].astype(jnp.float32)
    far = pltpu.make_async_copy(wide.at[0], out_ref.at[:, 2 * core], sems.at[0])
    far.start()
    wide[1] = jnp.where(core == 0, got_ref[1].astype(jnp.float32), near_ref[...])
    near = pltpu.make_async_copy(wide.at[1], out_ref.at[:, 2 - 2 * core], sems.at[1])
    near.start()
    far.wait()
    near.wait()


def after(value, other):
    return lax.optimization_barrier((value, other))


def shards(spectra, band_ids):
    parts, windows, width, channels = spectra.shape
    rows = parts * windows
    count = lax.axis_size("ch")
    fq_count = lax.axis_size("fq")
    index = lax.axis_index("ch")
    fq = lax.axis_index("fq")
    even_core = index % 2 == 0
    odd_chip = (index // 2) % 2 == 1

    ahead = [(i, (i + 4) % count) for i in range(count)]
    beside = [(i, i ^ 2) for i in range(count)]
    mate = [(i, i ^ 1) for i in range(count)]

    own = spectra.reshape(rows, width, channels)
    pieces = rows // PIECE
    heights = [PIECE + (TERMS if k == RAW else 0) for k in range(pieces)]
    block = jax.ShapeDtypeStruct((width, channels), jnp.float32)
    edge = jax.ShapeDtypeStruct((SMOOTH, channels), jnp.float32)
    held = [jax.ShapeDtypeStruct((h, width, channels), jnp.bfloat16) for h in heights]
    groups = width // GROUP
    left_shape = jax.ShapeDtypeStruct((groups, channels, rows * GROUP), jnp.bfloat16)
    nbytes = rows * width * channels * 2

    power, edge, *early = call(
        power_kernel,
        "power",
        (block, edge, *held[:RAW]),
        [vmem()],
        (vmem(),) * (2 + RAW),
        nbytes,
        nbytes,
    )(own)
    band_width = BANDS // fq_count
    local_band = band_ids - fq * band_width
    below = local_band[:, None] < jnp.arange(band_width + 1, dtype=jnp.int32)[None, :]
    bounds = jnp.sum(below.astype(jnp.int32), axis=0)
    norms = 1.0 / jnp.sqrt(windows * (bounds[1:] - bounds[:-1]).astype(jnp.float32))
    power, norms = after(power, norms)

    halo = lax.ppermute(edge, "fq", [(0, 1), (1, 0)])
    left, *late = call(
        left_kernel,
        "left",
        (left_shape, *held[RAW:]),
        [vmem()] * 3,
        (vmem(),) * (1 + pieces - RAW),
        nbytes,
        nbytes,
        scratch_shapes=[pltpu.VMEM((width + 16, channels), jnp.float32)],
    )(own, power, halo)
    mine = early + late

    out_shape = jax.ShapeDtypeStruct((2, ROUNDS, band_width, channels, channels), jnp.float32)
    sum_shape = jax.ShapeDtypeStruct((2, 2, band_width, channels, channels), jnp.float32)
    near_shape = jax.ShapeDtypeStruct((2, band_width, channels, channels), jnp.float32)
    send_shape = jax.ShapeDtypeStruct((2, 2, band_width, channels, channels), jnp.bfloat16)

    sets = [range(sum(SETS[:s]), sum(SETS[: s + 1])) for s in range(len(SETS))]
    twos, ones, onward = {}, {}, {}
    sums = {}

    def cross(these, flights, befores, last=()):
        first = befores is None
        operands = [bounds, norms, left, other]
        for flight in flights:
            operands += [flight[k] for k in these]
        operands += [*([] if first else befores), *last]
        kinds = len(flights)
        return call(
            functools.partial(
                cross_kernel, these[0] * PIECE, len(these), kinds, first, bool(last)
            ),
            "cross",
            (sum_shape,) * kinds + (send_shape,) * len(last),
            [smem(), smem()] + [vmem()] * (len(operands) - 2),
            (vmem(),) * (kinds + len(last)),
            8 * kinds * len(these) * PIECE * width * channels * channels,
            0 * nbytes,
        )(*operands)

    for k in range(DEPTH):
        twos[k] = lax.ppermute(mine[k], "ch", ahead)
    left, twos[OTHER_AFTER] = after(left, twos[OTHER_AFTER])
    other = lax.ppermute(left, "ch", mate)
    near = call(
        near_kernel,
        "near",
        near_shape,
        [smem(), smem(), vmem(), vmem()],
        vmem(),
        1000,
        1000,
    )(bounds, norms, left, other)

    for k in range(pieces):
        if k == NEAR_BEFORE:
            twos[k], near = after(twos[k], near)
        for s in range(len(SETS) - 1):
            if CROSS_BEFORE[s] == k:
                sums[s] = list(cross(sets[s], (ones, twos), sums.get(s - 1)))
                twos[k], sums[s][0] = after(twos[k], sums[s][0])
        if k >= AHEAD:
            twos[k], ones[k - AHEAD] = after(twos[k], ones[k - AHEAD])
        if k > 0:
            twos[k], onward[k - 1] = after(twos[k], onward[k - 1])
        if k + DEPTH < pieces:
            twos[k], later = after(twos[k], mine[k + DEPTH])
            twos[k + DEPTH] = lax.ppermute(later, "ch", ahead)
        onward[k] = jnp.where(odd_chip, twos[k], mine[k])
        if k < pieces - 1:
            ones[k] = lax.ppermute(onward[k], "ch", beside)
    final = pieces - 1
    for s in range(len(SETS) - 1):
        if s not in sums:
            onward[final], twos[sets[s][0]] = after(onward[final], twos[sets[s][0]])
            ones[final - 1], twos[sets[s][0]] = after(ones[final - 1], twos[sets[s][0]])
            sums[s] = list(cross(sets[s], (ones, twos), sums.get(s - 1)))
    one_sum, two_sum = sums[len(SETS) - 2]

    ones[final] = lax.ppermute(onward[final], "ch", beside)
    (two_sum,) = cross(sets[-1], (twos,), [two_sum])
    one_sum, sent = cross(sets[-1], (ones,), [one_sum], (two_sum,))
    got = lax.ppermute(sent, "ch", mate)
    out = call(
        put_own_kernel,
        "put",
        out_shape,
        [vmem()] * 2,
        hbm(),
        1000,
        1000,
        scratch_shapes=[pltpu.SemaphoreType.DMA((2,))],
    )(one_sum, two_sum)
    return call(
        put_got_kernel,
        "put",
        out_shape,
        [vmem(), vmem(), hbm()],
        hbm(),
        1000,
        1000,
        input_output_aliases={2: 0},
        scratch_shapes=[
            pltpu.VMEM((2,) + near_shape.shape, jnp.float32),
            pltpu.SemaphoreType.DMA((2,)),
        ],
    )(got, near, out)


def solution(mesh):
    placed = (P(None, None, "fq", "ch"), P("fq"))
    return jax.shard_map(
        shards,
        mesh=mesh,
        in_specs=placed,
        out_specs=P(None, None, "fq", "ch", None),
        check_vma=False,
    )
```

```python
import functools

import jax
import jax.numpy as jnp
from jax import lax
from jax.experimental import pallas as pl
from jax.experimental.pallas import tpu as pltpu
from jax.sharding import PartitionSpec as P

BANDS = 8
ROUNDS = 4
SMOOTH = 4
EPS = 1e-06

GROUP = 16
PIECE = 12
RAW = 3
TERMS = 3
DEPTH = 3
AHEAD = 2
CHAIN = 1
SETS = (4, 2, 2)
LEFT_AFTER = 0
OTHER_AFTER = 1
NEAR_BEFORE = 8
CROSS_BEFORE = (7, 8)
VMEM_LIMIT = 10 * 1024 * 1024


def vmem():
    return pl.BlockSpec(memory_space=pltpu.VMEM)


def smem():
    return pl.BlockSpec(memory_space=pltpu.SMEM)


def hbm():
    return pl.BlockSpec(memory_space=pltpu.HBM)


def call(kernel, name, out_shape, in_specs, out_specs, flops, moved, **more):
    return pl.pallas_call(
        kernel,
        out_shape=out_shape,
        in_specs=in_specs,
        out_specs=out_specs,
        compiler_params=pltpu.CompilerParams(vmem_limit_bytes=VMEM_LIMIT),
        cost_estimate=pl.CostEstimate(flops=flops, bytes_accessed=moved, transcendentals=0),
        name=name,
        **more,
    )


def power_kernel(x_ref, power_ref, edge_ref, *pieces):
    rows, width, _ = x_ref.shape
    for index, piece in enumerate(pieces):
        piece[...] = x_ref[index * PIECE : (index + 1) * PIECE]

    def step(i, total):
        value = x_ref[i].astype(jnp.float32)
        return total + value * value

    total = lax.fori_loop(0, rows, step, jnp.zeros(power_ref.shape, jnp.float32), unroll=8)
    power = total / (rows // 2)
    power_ref[...] = power
    low = lax.axis_index("fq") == 0
    edge_ref[...] = jnp.where(low, power[width - SMOOTH :], power[:SMOOTH])


def left_kernel(x_ref, power_ref, halo_ref, left_ref, *refs):
    whites, padded = refs[:-1], refs[-1]
    count = x_ref.shape[0] // PIECE
    fq = lax.axis_index("fq")
    width, channels = power_ref.shape
    bin_total = width * lax.axis_size("fq")
    padded[...] = jnp.zeros_like(padded)
    padded[8 : 8 + width, :] = power_ref[...]

    @pl.when(fq > 0)
    def _():
        padded[8 - SMOOTH : 8, :] = halo_ref[...]

    @pl.when(fq == 0)
    def _():
        padded[8 + width : 8 + width + SMOOTH, :] = halo_ref[...]

    total = padded[8 - SMOOTH : 8 - SMOOTH + width, :]
    for offset in range(1, 2 * SMOOTH + 1):
        total = total + padded[8 - SMOOTH + offset : 8 - SMOOTH + offset + width, :]
    bins = fq * width + lax.broadcasted_iota(jnp.int32, (width, channels), 0)
    counts = jnp.minimum(bins + SMOOTH, bin_total - 1) - jnp.maximum(bins - SMOOTH, 0) + 1
    scale = lax.rsqrt(total / counts.astype(jnp.float32) + EPS)
    rest = scale
    for term in range(TERMS):
        part = rest.astype(jnp.bfloat16)
        whites[0][PIECE + term] = part
        rest = rest - part.astype(jnp.float32)

    span = 2 * PIECE * GROUP
    for pair in range(count // 2):
        for group in range(width // GROUP):
            here = slice(group * GROUP, (group + 1) * GROUP)
            blocks = []
            for index in (2 * pair, 2 * pair + 1):
                raw = x_ref[index * PIECE : (index + 1) * PIECE, here, :].astype(jnp.float32)
                white = (raw * scale[here][None]).astype(jnp.bfloat16)
                if index >= RAW:
                    whites[index - RAW][:PIECE, here, :] = white
                blocks.append(white.reshape(PIECE * GROUP, channels))
            turned = jnp.concatenate(blocks, axis=0).T
            left_ref[group, :, pair * span : (pair + 1) * span] = turned


def band_at(bounds_ref, bands, bin_index):
    return sum((bounds_ref[k] <= bin_index).astype(jnp.int32) for k in range(1, bands))


def each_band(bounds_ref, groups, bands, add):
    for group in range(groups):
        low = band_at(bounds_ref, bands, group * GROUP)
        high = band_at(bounds_ref, bands, (group + 1) * GROUP - 1)
        add(group, low)
        lax.fori_loop(low + 1, high + 1, lambda band, carry: add(group, band), None)


def inside(bounds_ref, group, band, shape, dimension):
    bins = group * GROUP + lax.broadcasted_iota(jnp.int32, shape, dimension) % GROUP
    held = (bins >= bounds_ref[band]) & (bins < bounds_ref[band + 1])
    return held.astype(jnp.float32).astype(jnp.bfloat16)


def near_kernel(bounds_ref, norm_ref, own_ref, mate_ref, out_ref):
    groups, channels, span = own_ref.shape
    half = span // 2
    bands = out_ref.shape[1]
    out_ref[...] = jnp.zeros_like(out_ref)

    def add(group, band):
        right = mate_ref[group] * inside(bounds_ref, group, band, (1, span), 1)
        halves = []
        for start in (0, half):
            left = jnp.concatenate(
                [own_ref[group, :, begin : begin + half] for begin in (start, half - start)], axis=0
            )
            halves.append(
                lax.dot_general(
                    left,
                    right[:, start : start + half],
                    (((1,), (1,)), ((), ())),
                    preferred_element_type=jnp.float32,
                )
            )
        low, high = halves
        out_ref[0, band] += (low[:channels] + high[:channels]) * norm_ref[band]
        out_ref[1, band] += (low[channels:] - high[channels:]) * norm_ref[band]

    @pl.when(lax.axis_index("ch") % 2 == 1)
    def _():
        each_band(bounds_ref, groups, bands, add)


def cross_kernel(start, count, kinds, first, last, bounds_ref, norm_ref, own_ref, mate_ref, *refs):
    rights = [refs[k * count : (k + 1) * count] for k in range(kinds)]
    refs = refs[kinds * count :]
    if not first:
        befores, refs = refs[:kinds], refs[kinds:]
    if last:
        beyond_ref, refs = refs[0], refs[1:]
    sums = refs[:kinds]
    width, channels = rights[0][0].shape[1:]
    bands = sums[0].shape[2]
    half = own_ref.shape[2] // 2
    lanes = slice(start * GROUP, (start + count * PIECE) * GROUP)
    turned = lanes.start >= half
    shift = -half if turned else half
    across = slice(lanes.start + shift, lanes.stop + shift)
    for k in range(kinds):
        sums[k][...] = jnp.zeros_like(sums[k]) if first else befores[k][...]

    def column(right, here, held):
        scale = None
        if first:
            for term in range(TERMS):
                part = right[RAW][PIECE + term, here, :].astype(jnp.float32)
                scale = part if scale is None else scale + part
        blocks = []
        for index, ref in enumerate(right):
            block = ref[:PIECE, here, :]
            if first and index < RAW:
                block = (block.astype(jnp.float32) * scale[None]).astype(jnp.bfloat16)
            blocks.append((block * held[None]).reshape(PIECE * GROUP, channels))
        return jnp.concatenate(blocks, axis=0)

    def add(group, band):
        here = slice(group * GROUP, (group + 1) * GROUP)
        held = inside(bounds_ref, group, band, (GROUP, channels), 0)
        left = jnp.concatenate(
            [ref[group, :, part] for ref in (own_ref, mate_ref) for part in (lanes, across)], axis=0
        )
        right = jnp.concatenate([column(right, here, held) for right in rights], axis=1)
        product = jnp.dot(left, right, preferred_element_type=jnp.float32) * norm_ref[band]
        for k in range(kinds):
            for owner in range(2):
                for part in range(2):
                    row = (2 * owner + part) * channels
                    term = product[row : row + channels, k * channels : (k + 1) * channels]
                    sums[k][part, owner, band] += -term if part and turned else term

    each_band(bounds_ref, width // GROUP, bands, add)
    if last:
        refs[kinds][0] = sums[0][:, 1].astype(jnp.bfloat16)
        refs[kinds][1] = beyond_ref[:, 1].astype(jnp.bfloat16)


def put_own_kernel(one_ref, two_ref, out_ref, sems):
    copies = []
    for turn, value in ((1, one_ref), (3, two_ref)):
        for part in range(2):
            for band in range(out_ref.shape[2]):
                copies.append(
                    pltpu.make_async_copy(
                        value.at[part, 0, band], out_ref.at[part, turn, band], sems.at[turn // 2, part, band]
                    )
                )
    for copy in copies:
        copy.start()
    for copy in copies:
        copy.wait()


def put_got_kernel(got_ref, near_ref, before_ref, out_ref, wide, sems):
    core = lax.axis_index("ch") % 2
    copies = []
    for k, turn in enumerate((2 * core, 2 - 2 * core)):
        for part in range(2):
            for band in range(out_ref.shape[2]):
                value = got_ref[k, part, band].astype(jnp.float32)
                if k == 1:
                    value = jnp.where(core == 0, value, near_ref[part, band])
                wide[k, part, band] = value
                copies.append(
                    pltpu.make_async_copy(
                        wide.at[k, part, band], out_ref.at[part, turn, band], sems.at[k, part, band]
                    )
                )
                copies[-1].start()
    for copy in copies:
        copy.wait()


def after(value, other):
    return lax.optimization_barrier((value, other))


def shards(spectra, band_ids):
    parts, windows, width, channels = spectra.shape
    rows = parts * windows
    count = lax.axis_size("ch")
    fq_count = lax.axis_size("fq")
    index = lax.axis_index("ch")
    fq = lax.axis_index("fq")
    even_core = index % 2 == 0
    odd_chip = (index // 2) % 2 == 1

    ahead = [(i, (i + 4) % count) for i in range(count)]
    beside = [(i, i ^ 2) for i in range(count)]
    mate = [(i, i ^ 1) for i in range(count)]

    own = spectra.reshape(rows, width, channels)
    pieces = rows // PIECE
    heights = [PIECE + (TERMS if k == RAW else 0) for k in range(pieces)]
    block = jax.ShapeDtypeStruct((width, channels), jnp.float32)
    edge = jax.ShapeDtypeStruct((SMOOTH, channels), jnp.float32)
    held = [jax.ShapeDtypeStruct((h, width, channels), jnp.bfloat16) for h in heights]
    groups = width // GROUP
    left_shape = jax.ShapeDtypeStruct((groups, channels, rows * GROUP), jnp.bfloat16)
    nbytes = rows * width * channels * 2

    power, edge, *early = call(
        power_kernel,
        "power",
        (block, edge, *held[:RAW]),
        [vmem()],
        (vmem(),) * (2 + RAW),
        nbytes,
        nbytes,
    )(own)
    band_width = BANDS // fq_count
    local_band = band_ids - fq * band_width
    below = local_band[:, None] < jnp.arange(band_width + 1, dtype=jnp.int32)[None, :]
    bounds = jnp.sum(below.astype(jnp.int32), axis=0)
    norms = 1.0 / jnp.sqrt(windows * (bounds[1:] - bounds[:-1]).astype(jnp.float32))
    power, norms = after(power, norms)

    halo = lax.ppermute(edge, "fq", [(0, 1), (1, 0)])
    twos = {k: lax.ppermute(early[k], "ch", ahead) for k in range(RAW)}
    if LEFT_AFTER >= 0:
        twos[LEFT_AFTER], halo = after(twos[LEFT_AFTER], halo)
    left, *late = call(
        left_kernel,
        "left",
        (left_shape, *held[RAW:]),
        [vmem()] * 3,
        (vmem(),) * (1 + pieces - RAW),
        nbytes,
        nbytes,
        scratch_shapes=[pltpu.VMEM((width + 16, channels), jnp.float32)],
    )(own, power, halo)
    mine = early + late

    out_shape = jax.ShapeDtypeStruct((2, ROUNDS, band_width, channels, channels), jnp.float32)
    sum_shape = jax.ShapeDtypeStruct((2, 2, band_width, channels, channels), jnp.float32)
    near_shape = jax.ShapeDtypeStruct((2, band_width, channels, channels), jnp.float32)
    send_shape = jax.ShapeDtypeStruct((2, 2, band_width, channels, channels), jnp.bfloat16)

    sets = [range(sum(SETS[:s]), sum(SETS[: s + 1])) for s in range(len(SETS))]
    ones, onward = {}, {}
    sums = {}

    def cross(these, flights, befores, last=()):
        first = befores is None
        operands = [bounds, norms, left, other]
        for flight in flights:
            operands += [flight[k] for k in these]
        operands += [*([] if first else befores), *last]
        kinds = len(flights)
        return call(
            functools.partial(
                cross_kernel, these[0] * PIECE, len(these), kinds, first, bool(last)
            ),
            "cross",
            (sum_shape,) * kinds + (send_shape,) * len(last),
            [smem(), smem()] + [vmem()] * (len(operands) - 2),
            (vmem(),) * (kinds + len(last)),
            8 * kinds * len(these) * PIECE * width * channels * channels,
            0 * nbytes,
        )(*operands)

    for k in range(RAW, DEPTH):
        twos[k] = lax.ppermute(mine[k], "ch", ahead)
    left, twos[OTHER_AFTER] = after(left, twos[OTHER_AFTER])
    other = lax.ppermute(left, "ch", mate)
    near = call(
        near_kernel,
        "near",
        near_shape,
        [smem(), smem(), vmem(), vmem()],
        vmem(),
        1000,
        1000,
    )(bounds, norms, left, other)

    for k in range(pieces):
        if k == NEAR_BEFORE:
            twos[k], near = after(twos[k], near)
        for s in range(len(SETS) - 1):
            if CROSS_BEFORE[s] == k:
                sums[s] = list(cross(sets[s], (ones, twos), sums.get(s - 1)))
                twos[k], sums[s][0] = after(twos[k], sums[s][0])
        if k >= AHEAD:
            twos[k], ones[k - AHEAD] = after(twos[k], ones[k - AHEAD])
        if CHAIN and k > 0:
            twos[k], onward[k - 1] = after(twos[k], onward[k - 1])
        if k + DEPTH < pieces:
            twos[k], later = after(twos[k], mine[k + DEPTH])
            twos[k + DEPTH] = lax.ppermute(later, "ch", ahead)
        onward[k] = jnp.where(odd_chip, twos[k], mine[k])
        if k < pieces - 1:
            ones[k] = lax.ppermute(onward[k], "ch", beside)
    final = pieces - 1
    for s in range(len(SETS) - 1):
        if s not in sums:
            onward[final], twos[sets[s][0]] = after(onward[final], twos[sets[s][0]])
            ones[final - 1], twos[sets[s][0]] = after(ones[final - 1], twos[sets[s][0]])
            sums[s] = list(cross(sets[s], (ones, twos), sums.get(s - 1)))
    one_sum, two_sum = sums[len(SETS) - 2]

    ones[final] = lax.ppermute(onward[final], "ch", beside)
    (two_sum,) = cross(sets[-1], (twos,), [two_sum])
    one_sum, sent = cross(sets[-1], (ones,), [one_sum], (two_sum,))
    got = lax.ppermute(sent, "ch", mate)
    out = call(
        put_own_kernel,
        "put",
        out_shape,
        [vmem()] * 2,
        hbm(),
        1000,
        1000,
        scratch_shapes=[pltpu.SemaphoreType.DMA((2, 2, band_width))],
    )(one_sum, two_sum)
    return call(
        put_got_kernel,
        "put",
        out_shape,
        [vmem(), vmem(), hbm()],
        hbm(),
        1000,
        1000,
        input_output_aliases={2: 0},
        scratch_shapes=[
            pltpu.VMEM((2,) + near_shape.shape, jnp.float32),
            pltpu.SemaphoreType.DMA((2, 2, band_width)),
        ],
    )(got, near, out)


def solution(mesh):
    placed = (P(None, None, "fq", "ch"), P("fq"))
    return jax.shard_map(
        shards,
        mesh=mesh,
        in_specs=placed,
        out_specs=P(None, None, "fq", "ch", None),
        check_vma=False,
    )
```

```python
import functools

import jax
import jax.numpy as jnp
from jax import lax
from jax.experimental import pallas as pl
from jax.experimental.pallas import tpu as pltpu
from jax.sharding import PartitionSpec as P

BANDS = 8
ROUNDS = 4
SMOOTH = 4
EPS = 1e-06

GROUP = 16
PIECE = 12
RAW = 3
TERMS = 3
Z_AFTER = (-1, -1, -1, 0, 1, 2, 3, 4)
Y_AFTER = (-1, -1, 0, 1, 2, 3, 4, 5)
CHAIN = 1
SETS = (4, 2, 2)
LEFT_AFTER = 0
OTHER_AFTER = 0
NEAR_BEFORE = 7
CROSS_BEFORE = (8, 8)
VMEM_LIMIT = 10 * 1024 * 1024


def vmem():
    return pl.BlockSpec(memory_space=pltpu.VMEM)


def smem():
    return pl.BlockSpec(memory_space=pltpu.SMEM)


def hbm():
    return pl.BlockSpec(memory_space=pltpu.HBM)


def call(kernel, name, out_shape, in_specs, out_specs, flops, moved, **more):
    return pl.pallas_call(
        kernel,
        out_shape=out_shape,
        in_specs=in_specs,
        out_specs=out_specs,
        compiler_params=pltpu.CompilerParams(vmem_limit_bytes=VMEM_LIMIT),
        cost_estimate=pl.CostEstimate(flops=flops, bytes_accessed=moved, transcendentals=0),
        name=name,
        **more,
    )


def power_kernel(x_ref, power_ref, edge_ref, *pieces):
    rows, width, _ = x_ref.shape
    for index, piece in enumerate(pieces):
        piece[...] = x_ref[index * PIECE : (index + 1) * PIECE]

    def step(i, total):
        value = x_ref[i].astype(jnp.float32)
        return total + value * value

    total = lax.fori_loop(0, rows, step, jnp.zeros(power_ref.shape, jnp.float32), unroll=8)
    power = total / (rows // 2)
    power_ref[...] = power
    low = lax.axis_index("fq") == 0
    edge_ref[...] = jnp.where(low, power[width - SMOOTH :], power[:SMOOTH])


def left_kernel(x_ref, power_ref, halo_ref, left_ref, *refs):
    whites, padded = refs[:-1], refs[-1]
    count = x_ref.shape[0] // PIECE
    fq = lax.axis_index("fq")
    width, channels = power_ref.shape
    bin_total = width * lax.axis_size("fq")
    padded[...] = jnp.zeros_like(padded)
    padded[8 : 8 + width, :] = power_ref[...]

    @pl.when(fq > 0)
    def _():
        padded[8 - SMOOTH : 8, :] = halo_ref[...]

    @pl.when(fq == 0)
    def _():
        padded[8 + width : 8 + width + SMOOTH, :] = halo_ref[...]

    total = padded[8 - SMOOTH : 8 - SMOOTH + width, :]
    for offset in range(1, 2 * SMOOTH + 1):
        total = total + padded[8 - SMOOTH + offset : 8 - SMOOTH + offset + width, :]
    bins = fq * width + lax.broadcasted_iota(jnp.int32, (width, channels), 0)
    counts = jnp.minimum(bins + SMOOTH, bin_total - 1) - jnp.maximum(bins - SMOOTH, 0) + 1
    scale = lax.rsqrt(total / counts.astype(jnp.float32) + EPS)
    rest = scale
    for term in range(TERMS):
        part = rest.astype(jnp.bfloat16)
        whites[0][PIECE + term] = part
        rest = rest - part.astype(jnp.float32)

    span = 2 * PIECE * GROUP
    for pair in range(count // 2):
        for group in range(width // GROUP):
            here = slice(group * GROUP, (group + 1) * GROUP)
            blocks = []
            for index in (2 * pair, 2 * pair + 1):
                raw = x_ref[index * PIECE : (index + 1) * PIECE, here, :].astype(jnp.float32)
                white = (raw * scale[here][None]).astype(jnp.bfloat16)
                if index >= RAW:
                    whites[index - RAW][:PIECE, here, :] = white
                blocks.append(white.reshape(PIECE * GROUP, channels))
            turned = jnp.concatenate(blocks, axis=0).T
            left_ref[group, :, pair * span : (pair + 1) * span] = turned


def band_at(bounds_ref, bands, bin_index):
    return sum((bounds_ref[k] <= bin_index).astype(jnp.int32) for k in range(1, bands))


def each_band(bounds_ref, groups, bands, add):
    for group in range(groups):
        band = band_at(bounds_ref, bands, group * GROUP)
        add(group, band, bounds_ref[band], bounds_ref[band + 1])
    for band in range(1, bands):
        low = bounds_ref[band]
        high = jnp.where(low % GROUP == 0, low, bounds_ref[band + 1])
        add(jnp.minimum(low // GROUP, groups - 1), band, low, high)


def inside(group, low, high, shape, dimension):
    bins = group * GROUP + lax.broadcasted_iota(jnp.int32, shape, dimension) % GROUP
    return ((bins >= low) & (bins < high)).astype(jnp.float32).astype(jnp.bfloat16)


def near_kernel(bounds_ref, norm_ref, own_ref, mate_ref, out_ref):
    groups, channels, span = own_ref.shape
    half = span // 2
    bands = out_ref.shape[1]
    out_ref[...] = jnp.zeros_like(out_ref)

    def add(group, band, low, high):
        right = mate_ref[group] * inside(group, low, high, (1, span), 1)
        halves = []
        for start in (0, half):
            left = jnp.concatenate(
                [own_ref[group, :, begin : begin + half] for begin in (start, half - start)], axis=0
            )
            halves.append(
                lax.dot_general(
                    left,
                    right[:, start : start + half],
                    (((1,), (1,)), ((), ())),
                    preferred_element_type=jnp.float32,
                )
            )
        out_ref[0, band] += (halves[0][:channels] + halves[1][:channels]) * norm_ref[band]
        out_ref[1, band] += (halves[0][channels:] - halves[1][channels:]) * norm_ref[band]

    @pl.when(lax.axis_index("ch") % 2 == 1)
    def _():
        each_band(bounds_ref, groups, bands, add)


def cross_kernel(start, count, kinds, first, last, bounds_ref, norm_ref, own_ref, mate_ref, *refs):
    rights = [refs[k * count : (k + 1) * count] for k in range(kinds)]
    refs = refs[kinds * count :]
    if not first:
        befores, refs = refs[:kinds], refs[kinds:]
    if last:
        beyond_ref, refs = refs[0], refs[1:]
    sums = refs[:kinds]
    width, channels = rights[0][0].shape[1:]
    bands = sums[0].shape[2]
    half = own_ref.shape[2] // 2
    lanes = slice(start * GROUP, (start + count * PIECE) * GROUP)
    turned = lanes.start >= half
    shift = -half if turned else half
    across = slice(lanes.start + shift, lanes.stop + shift)
    for k in range(kinds):
        sums[k][...] = jnp.zeros_like(sums[k]) if first else befores[k][...]

    def column(right, here, held):
        scale = None
        if first:
            for term in range(TERMS):
                part = right[RAW][PIECE + term, here, :].astype(jnp.float32)
                scale = part if scale is None else scale + part
        blocks = []
        for index, ref in enumerate(right):
            block = ref[:PIECE, here, :]
            if first and index < RAW:
                block = (block.astype(jnp.float32) * scale[None]).astype(jnp.bfloat16)
            blocks.append((block * held[None]).reshape(PIECE * GROUP, channels))
        return jnp.concatenate(blocks, axis=0)

    def add(group, band, low, high):
        begin = group * GROUP
        here = pl.ds(begin if isinstance(group, int) else pl.multiple_of(begin, GROUP), GROUP)
        held = inside(group, low, high, (GROUP, channels), 0)
        left = jnp.concatenate(
            [ref[group, :, part] for ref in (own_ref, mate_ref) for part in (lanes, across)], axis=0
        )
        right = jnp.concatenate([column(right, here, held) for right in rights], axis=1)
        product = jnp.dot(left, right, preferred_element_type=jnp.float32) * norm_ref[band]
        for k in range(kinds):
            for owner in range(2):
                for part in range(2):
                    row = (2 * owner + part) * channels
                    term = product[row : row + channels, k * channels : (k + 1) * channels]
                    sums[k][part, owner, band] += -term if part and turned else term

    each_band(bounds_ref, width // GROUP, bands, add)
    if last:
        refs[kinds][0] = sums[0][:, 1].astype(jnp.bfloat16)
        refs[kinds][1] = beyond_ref[:, 1].astype(jnp.bfloat16)


def put_own_kernel(one_ref, two_ref, out_ref, sems):
    copies = []
    for turn, value in ((1, one_ref), (3, two_ref)):
        for part in range(2):
            for band in range(out_ref.shape[2]):
                copies.append(
                    pltpu.make_async_copy(
                        value.at[part, 0, band], out_ref.at[part, turn, band], sems.at[turn // 2, part, band]
                    )
                )
    for copy in copies:
        copy.start()
    for copy in copies:
        copy.wait()


def put_got_kernel(got_ref, near_ref, before_ref, out_ref, wide, sems):
    core = lax.axis_index("ch") % 2
    copies = []
    for k, turn in enumerate((2 * core, 2 - 2 * core)):
        for part in range(2):
            for band in range(out_ref.shape[2]):
                value = got_ref[k, part, band].astype(jnp.float32)
                if k == 1:
                    value = jnp.where(core == 0, value, near_ref[part, band])
                wide[k, part, band] = value
                copies.append(
                    pltpu.make_async_copy(
                        wide.at[k, part, band], out_ref.at[part, turn, band], sems.at[k, part, band]
                    )
                )
                copies[-1].start()
    for copy in copies:
        copy.wait()


def after(value, other):
    return lax.optimization_barrier((value, other))


def shards(spectra, band_ids):
    parts, windows, width, channels = spectra.shape
    rows = parts * windows
    count = lax.axis_size("ch")
    fq_count = lax.axis_size("fq")
    index = lax.axis_index("ch")
    fq = lax.axis_index("fq")
    even_core = index % 2 == 0
    odd_chip = (index // 2) % 2 == 1

    ahead = [(i, (i + 4) % count) for i in range(count)]
    beside = [(i, i ^ 2) for i in range(count)]
    mate = [(i, i ^ 1) for i in range(count)]

    own = spectra.reshape(rows, width, channels)
    pieces = rows // PIECE
    heights = [PIECE + (TERMS if k == RAW else 0) for k in range(pieces)]
    block = jax.ShapeDtypeStruct((width, channels), jnp.float32)
    edge = jax.ShapeDtypeStruct((SMOOTH, channels), jnp.float32)
    held = [jax.ShapeDtypeStruct((h, width, channels), jnp.bfloat16) for h in heights]
    groups = width // GROUP
    left_shape = jax.ShapeDtypeStruct((groups, channels, rows * GROUP), jnp.bfloat16)
    nbytes = rows * width * channels * 2

    power, edge, *early = call(
        power_kernel,
        "power",
        (block, edge, *held[:RAW]),
        [vmem()],
        (vmem(),) * (2 + RAW),
        nbytes,
        nbytes,
    )(own)
    band_width = BANDS // fq_count
    local_band = band_ids - fq * band_width
    below = local_band[:, None] < jnp.arange(band_width + 1, dtype=jnp.int32)[None, :]
    bounds = jnp.sum(below.astype(jnp.int32), axis=0)
    norms = 1.0 / jnp.sqrt(windows * (bounds[1:] - bounds[:-1]).astype(jnp.float32))
    power, norms = after(power, norms)

    halo = lax.ppermute(edge, "fq", [(0, 1), (1, 0)])
    twos = {k: lax.ppermute(early[k], "ch", ahead) for k in range(RAW)}
    if LEFT_AFTER >= 0:
        twos[LEFT_AFTER], halo = after(twos[LEFT_AFTER], halo)
    left, *late = call(
        left_kernel,
        "left",
        (left_shape, *held[RAW:]),
        [vmem()] * 3,
        (vmem(),) * (1 + pieces - RAW),
        nbytes,
        nbytes,
        scratch_shapes=[pltpu.VMEM((width + 16, channels), jnp.float32)],
    )(own, power, halo)
    mine = early + late

    out_shape = jax.ShapeDtypeStruct((2, ROUNDS, band_width, channels, channels), jnp.float32)
    sum_shape = jax.ShapeDtypeStruct((2, 2, band_width, channels, channels), jnp.float32)
    near_shape = jax.ShapeDtypeStruct((2, band_width, channels, channels), jnp.float32)
    send_shape = jax.ShapeDtypeStruct((2, 2, band_width, channels, channels), jnp.bfloat16)

    sets = [range(sum(SETS[:s]), sum(SETS[: s + 1])) for s in range(len(SETS))]
    ones, onward = {}, {}
    sums = {}

    def cross(these, flights, befores, last=()):
        first = befores is None
        operands = [bounds, norms, left, other]
        for flight in flights:
            operands += [flight[k] for k in these]
        operands += [*([] if first else befores), *last]
        kinds = len(flights)
        return call(
            functools.partial(
                cross_kernel, these[0] * PIECE, len(these), kinds, first, bool(last)
            ),
            "cross",
            (sum_shape,) * kinds + (send_shape,) * len(last),
            [smem(), smem()] + [vmem()] * (len(operands) - 2),
            (vmem(),) * (kinds + len(last)),
            8 * kinds * len(these) * PIECE * width * channels * channels,
            0 * nbytes,
        )(*operands)

    for k in range(RAW, pieces):
        if Z_AFTER[k] < 0:
            twos[k] = lax.ppermute(mine[k], "ch", ahead)
    left, twos[OTHER_AFTER] = after(left, twos[OTHER_AFTER])
    other = lax.ppermute(left, "ch", mate)
    near = call(
        near_kernel,
        "near",
        near_shape,
        [smem(), smem(), vmem(), vmem()],
        vmem(),
        1000,
        1000,
    )(bounds, norms, left, other)

    for k in range(pieces):
        if k == NEAR_BEFORE:
            twos[k], near = after(twos[k], near)
        for s in range(len(SETS) - 1):
            if CROSS_BEFORE[s] == k:
                sums[s] = list(cross(sets[s], (ones, twos), sums.get(s - 1)))
                twos[k], sums[s][0] = after(twos[k], sums[s][0])
        if Y_AFTER[k] >= 0:
            twos[k], ones[Y_AFTER[k]] = after(twos[k], ones[Y_AFTER[k]])
        if CHAIN and k > 0:
            twos[k], onward[k - 1] = after(twos[k], onward[k - 1])
        for later in range(pieces):
            if Z_AFTER[later] == k:
                twos[k], mine[later] = after(twos[k], mine[later])
                twos[later] = lax.ppermute(mine[later], "ch", ahead)
        onward[k] = jnp.where(odd_chip, twos[k], mine[k])
        if k < pieces - 1:
            ones[k] = lax.ppermute(onward[k], "ch", beside)
    final = pieces - 1
    for s in range(len(SETS) - 1):
        if s not in sums:
            onward[final], twos[sets[s][0]] = after(onward[final], twos[sets[s][0]])
            ones[final - 1], twos[sets[s][0]] = after(ones[final - 1], twos[sets[s][0]])
            sums[s] = list(cross(sets[s], (ones, twos), sums.get(s - 1)))
    one_sum, two_sum = sums[len(SETS) - 2]

    ones[final] = lax.ppermute(onward[final], "ch", beside)
    (two_sum,) = cross(sets[-1], (twos,), [two_sum])
    one_sum, sent = cross(sets[-1], (ones,), [one_sum], (two_sum,))
    got = lax.ppermute(sent, "ch", mate)
    out = call(
        put_own_kernel,
        "put",
        out_shape,
        [vmem()] * 2,
        hbm(),
        1000,
        1000,
        scratch_shapes=[pltpu.SemaphoreType.DMA((2, 2, band_width))],
    )(one_sum, two_sum)
    return call(
        put_got_kernel,
        "put",
        out_shape,
        [vmem(), vmem(), hbm()],
        hbm(),
        1000,
        1000,
        input_output_aliases={2: 0},
        scratch_shapes=[
            pltpu.VMEM((2,) + near_shape.shape, jnp.float32),
            pltpu.SemaphoreType.DMA((2, 2, band_width)),
        ],
    )(got, near, out)


def solution(mesh):
    placed = (P(None, None, "fq", "ch"), P("fq"))
    return jax.shard_map(
        shards,
        mesh=mesh,
        in_specs=placed,
        out_specs=P(None, None, "fq", "ch", None),
        check_vma=False,
    )
```

```python
import functools

import jax
import jax.numpy as jnp
from jax import lax
from jax.experimental import pallas as pl
from jax.experimental.pallas import tpu as pltpu
from jax.sharding import PartitionSpec as P

BANDS = 8
ROUNDS = 4
SMOOTH = 4
EPS = 1e-06

GROUP = 16
PIECE = 12
RAW = 3
TERMS = 3
Z_AFTER = (-1, -1, -1, 0, 2, 2, 3, 4)
Y_AFTER = (-1, -1, 0, 1, 2, 3, 4, 5)
LAST_TIE = 0
CHAIN = 0
SETS = (4, 2, 2)
LEFT_AFTER = -1
OTHER_AFTER = 0
NEAR_BEFORE = 8
CROSS_BEFORE = (7, 8)
VMEM_LIMIT = 10 * 1024 * 1024


def vmem():
    return pl.BlockSpec(memory_space=pltpu.VMEM)


def smem():
    return pl.BlockSpec(memory_space=pltpu.SMEM)


def hbm():
    return pl.BlockSpec(memory_space=pltpu.HBM)


def call(kernel, name, out_shape, in_specs, out_specs, flops, moved, **more):
    return pl.pallas_call(
        kernel,
        out_shape=out_shape,
        in_specs=in_specs,
        out_specs=out_specs,
        compiler_params=pltpu.CompilerParams(vmem_limit_bytes=VMEM_LIMIT),
        cost_estimate=pl.CostEstimate(flops=flops, bytes_accessed=moved, transcendentals=0),
        name=name,
        **more,
    )


def power_kernel(x_ref, power_ref, edge_ref, *pieces):
    rows, width, _ = x_ref.shape
    for index, piece in enumerate(pieces):
        piece[...] = x_ref[index * PIECE : (index + 1) * PIECE]

    def step(i, total):
        value = x_ref[i].astype(jnp.float32)
        return total + value * value

    total = lax.fori_loop(0, rows, step, jnp.zeros(power_ref.shape, jnp.float32), unroll=8)
    power = total / (rows // 2)
    power_ref[...] = power
    low = lax.axis_index("fq") == 0
    edge_ref[...] = jnp.where(low, power[width - SMOOTH :], power[:SMOOTH])


def left_kernel(x_ref, power_ref, halo_ref, left_ref, *refs):
    whites, padded = refs[:-1], refs[-1]
    count = x_ref.shape[0] // PIECE
    fq = lax.axis_index("fq")
    width, channels = power_ref.shape
    bin_total = width * lax.axis_size("fq")
    padded[...] = jnp.zeros_like(padded)
    padded[8 : 8 + width, :] = power_ref[...]

    @pl.when(fq > 0)
    def _():
        padded[8 - SMOOTH : 8, :] = halo_ref[...]

    @pl.when(fq == 0)
    def _():
        padded[8 + width : 8 + width + SMOOTH, :] = halo_ref[...]

    total = padded[8 - SMOOTH : 8 - SMOOTH + width, :]
    for offset in range(1, 2 * SMOOTH + 1):
        total = total + padded[8 - SMOOTH + offset : 8 - SMOOTH + offset + width, :]
    bins = fq * width + lax.broadcasted_iota(jnp.int32, (width, channels), 0)
    counts = jnp.minimum(bins + SMOOTH, bin_total - 1) - jnp.maximum(bins - SMOOTH, 0) + 1
    scale = lax.rsqrt(total / counts.astype(jnp.float32) + EPS)
    rest = scale
    for term in range(TERMS):
        part = rest.astype(jnp.bfloat16)
        whites[0][PIECE + term] = part
        rest = rest - part.astype(jnp.float32)

    span = 2 * PIECE * GROUP
    for pair in range(count // 2):
        for group in range(width // GROUP):
            here = slice(group * GROUP, (group + 1) * GROUP)
            blocks = []
            for index in (2 * pair, 2 * pair + 1):
                raw = x_ref[index * PIECE : (index + 1) * PIECE, here, :].astype(jnp.float32)
                white = (raw * scale[here][None]).astype(jnp.bfloat16)
                if index >= RAW:
                    whites[index - RAW][:PIECE, here, :] = white
                blocks.append(white.reshape(PIECE * GROUP, channels))
            turned = jnp.concatenate(blocks, axis=0).T
            left_ref[group, :, pair * span : (pair + 1) * span] = turned


def band_at(bounds_ref, bands, bin_index):
    return sum((bounds_ref[k] <= bin_index).astype(jnp.int32) for k in range(1, bands))


def each_band(bounds_ref, groups, bands, add):
    for group in range(groups):
        band = band_at(bounds_ref, bands, group * GROUP)
        add(group, band, bounds_ref[band], bounds_ref[band + 1])
    for band in range(1, bands):
        low = bounds_ref[band]
        high = jnp.where(low % GROUP == 0, low, bounds_ref[band + 1])
        add(jnp.minimum(low // GROUP, groups - 1), band, low, high)


def inside(group, low, high, shape, dimension):
    bins = group * GROUP + lax.broadcasted_iota(jnp.int32, shape, dimension) % GROUP
    return ((bins >= low) & (bins < high)).astype(jnp.float32).astype(jnp.bfloat16)


def near_kernel(bounds_ref, norm_ref, own_ref, mate_ref, out_ref):
    groups, channels, span = own_ref.shape
    half = span // 2
    bands = out_ref.shape[1]
    out_ref[...] = jnp.zeros_like(out_ref)

    def add(group, band, low, high):
        right = mate_ref[group] * inside(group, low, high, (1, span), 1)
        halves = []
        for start in (0, half):
            left = jnp.concatenate(
                [own_ref[group, :, begin : begin + half] for begin in (start, half - start)], axis=0
            )
            halves.append(
                lax.dot_general(
                    left,
                    right[:, start : start + half],
                    (((1,), (1,)), ((), ())),
                    preferred_element_type=jnp.float32,
                )
            )
        out_ref[0, band] += (halves[0][:channels] + halves[1][:channels]) * norm_ref[band]
        out_ref[1, band] += (halves[0][channels:] - halves[1][channels:]) * norm_ref[band]

    @pl.when(lax.axis_index("ch") % 2 == 1)
    def _():
        each_band(bounds_ref, groups, bands, add)


def cross_kernel(start, count, kinds, first, last, bounds_ref, norm_ref, own_ref, mate_ref, *refs):
    rights = [refs[k * count : (k + 1) * count] for k in range(kinds)]
    refs = refs[kinds * count :]
    if not first:
        befores, refs = refs[:kinds], refs[kinds:]
    if last:
        beyond_ref, refs = refs[0], refs[1:]
    sums = refs[:kinds]
    width, channels = rights[0][0].shape[1:]
    bands = sums[0].shape[2]
    half = own_ref.shape[2] // 2
    lanes = slice(start * GROUP, (start + count * PIECE) * GROUP)
    turned = lanes.start >= half
    shift = -half if turned else half
    across = slice(lanes.start + shift, lanes.stop + shift)
    for k in range(kinds):
        sums[k][...] = jnp.zeros_like(sums[k]) if first else befores[k][...]

    def column(right, here, held):
        scale = None
        if first:
            for term in range(TERMS):
                part = right[RAW][PIECE + term, here, :].astype(jnp.float32)
                scale = part if scale is None else scale + part
        blocks = []
        for index, ref in enumerate(right):
            block = ref[:PIECE, here, :]
            if first and index < RAW:
                block = (block.astype(jnp.float32) * scale[None]).astype(jnp.bfloat16)
            blocks.append((block * held[None]).reshape(PIECE * GROUP, channels))
        return jnp.concatenate(blocks, axis=0)

    def add(group, band, low, high):
        begin = group * GROUP
        here = pl.ds(begin if isinstance(group, int) else pl.multiple_of(begin, GROUP), GROUP)
        held = inside(group, low, high, (GROUP, channels), 0)
        left = jnp.concatenate(
            [ref[group, :, part] for ref in (own_ref, mate_ref) for part in (lanes, across)], axis=0
        )
        right = jnp.concatenate([column(right, here, held) for right in rights], axis=1)
        product = jnp.dot(left, right, preferred_element_type=jnp.float32) * norm_ref[band]
        for k in range(kinds):
            for owner in range(2):
                for part in range(2):
                    row = (2 * owner + part) * channels
                    term = product[row : row + channels, k * channels : (k + 1) * channels]
                    sums[k][part, owner, band] += -term if part and turned else term

    each_band(bounds_ref, width // GROUP, bands, add)
    if last:
        refs[kinds][0] = sums[0][:, 1].astype(jnp.bfloat16)
        refs[kinds][1] = beyond_ref[:, 1].astype(jnp.bfloat16)


def put_own_kernel(one_ref, two_ref, out_ref, sems):
    copies = []
    for turn, value in ((1, one_ref), (3, two_ref)):
        for part in range(2):
            for band in range(out_ref.shape[2]):
                copies.append(
                    pltpu.make_async_copy(
                        value.at[part, 0, band], out_ref.at[part, turn, band], sems.at[turn // 2, part, band]
                    )
                )
    for copy in copies:
        copy.start()
    for copy in copies:
        copy.wait()


def put_got_kernel(got_ref, near_ref, before_ref, out_ref, wide, sems):
    core = lax.axis_index("ch") % 2
    copies = []
    for k, turn in enumerate((2 * core, 2 - 2 * core)):
        for part in range(2):
            for band in range(out_ref.shape[2]):
                value = got_ref[k, part, band].astype(jnp.float32)
                if k == 1:
                    value = jnp.where(core == 0, value, near_ref[part, band])
                wide[k, part, band] = value
                copies.append(
                    pltpu.make_async_copy(
                        wide.at[k, part, band], out_ref.at[part, turn, band], sems.at[k, part, band]
                    )
                )
                copies[-1].start()
    for copy in copies:
        copy.wait()


def after(value, other):
    return lax.optimization_barrier((value, other))


def shards(spectra, band_ids):
    parts, windows, width, channels = spectra.shape
    rows = parts * windows
    count = lax.axis_size("ch")
    fq_count = lax.axis_size("fq")
    index = lax.axis_index("ch")
    fq = lax.axis_index("fq")
    even_core = index % 2 == 0
    odd_chip = (index // 2) % 2 == 1

    ahead = [(i, (i + 4) % count) for i in range(count)]
    beside = [(i, i ^ 2) for i in range(count)]
    mate = [(i, i ^ 1) for i in range(count)]

    own = spectra.reshape(rows, width, channels)
    pieces = rows // PIECE
    heights = [PIECE + (TERMS if k == RAW else 0) for k in range(pieces)]
    block = jax.ShapeDtypeStruct((width, channels), jnp.float32)
    edge = jax.ShapeDtypeStruct((SMOOTH, channels), jnp.float32)
    held = [jax.ShapeDtypeStruct((h, width, channels), jnp.bfloat16) for h in heights]
    groups = width // GROUP
    left_shape = jax.ShapeDtypeStruct((groups, channels, rows * GROUP), jnp.bfloat16)
    nbytes = rows * width * channels * 2

    power, edge, *early = call(
        power_kernel,
        "power",
        (block, edge, *held[:RAW]),
        [vmem()],
        (vmem(),) * (2 + RAW),
        nbytes,
        nbytes,
    )(own)
    band_width = BANDS // fq_count
    local_band = band_ids - fq * band_width
    below = local_band[:, None] < jnp.arange(band_width + 1, dtype=jnp.int32)[None, :]
    bounds = jnp.sum(below.astype(jnp.int32), axis=0)
    norms = 1.0 / jnp.sqrt(windows * (bounds[1:] - bounds[:-1]).astype(jnp.float32))
    power, norms = after(power, norms)

    twos = {k: lax.ppermute(early[k], "ch", ahead) for k in range(RAW)}
    halo = lax.ppermute(edge, "fq", [(0, 1), (1, 0)])
    if LEFT_AFTER >= 0:
        twos[LEFT_AFTER], halo = after(twos[LEFT_AFTER], halo)
    left, *late = call(
        left_kernel,
        "left",
        (left_shape, *held[RAW:]),
        [vmem()] * 3,
        (vmem(),) * (1 + pieces - RAW),
        nbytes,
        nbytes,
        scratch_shapes=[pltpu.VMEM((width + 16, channels), jnp.float32)],
    )(own, power, halo)
    mine = early + late

    out_shape = jax.ShapeDtypeStruct((2, ROUNDS, band_width, channels, channels), jnp.float32)
    sum_shape = jax.ShapeDtypeStruct((2, 2, band_width, channels, channels), jnp.float32)
    near_shape = jax.ShapeDtypeStruct((2, band_width, channels, channels), jnp.float32)
    send_shape = jax.ShapeDtypeStruct((2, 2, band_width, channels, channels), jnp.bfloat16)

    sets = [range(sum(SETS[:s]), sum(SETS[: s + 1])) for s in range(len(SETS))]
    ones, onward = {}, {}
    sums = {}

    def cross(these, flights, befores, last=()):
        first = befores is None
        operands = [bounds, norms, left, other]
        for flight in flights:
            operands += [flight[k] for k in these]
        operands += [*([] if first else befores), *last]
        kinds = len(flights)
        return call(
            functools.partial(
                cross_kernel, these[0] * PIECE, len(these), kinds, first, bool(last)
            ),
            "cross",
            (sum_shape,) * kinds + (send_shape,) * len(last),
            [smem(), smem()] + [vmem()] * (len(operands) - 2),
            (vmem(),) * (kinds + len(last)),
            8 * kinds * len(these) * PIECE * width * channels * channels,
            0 * nbytes,
        )(*operands)

    for k in range(RAW, pieces):
        if Z_AFTER[k] < 0:
            twos[k] = lax.ppermute(mine[k], "ch", ahead)
    left, twos[OTHER_AFTER] = after(left, twos[OTHER_AFTER])
    other = lax.ppermute(left, "ch", mate)
    near = call(
        near_kernel,
        "near",
        near_shape,
        [smem(), smem(), vmem(), vmem()],
        vmem(),
        1000,
        1000,
    )(bounds, norms, left, other)

    for k in range(pieces):
        if k == NEAR_BEFORE:
            twos[k], near = after(twos[k], near)
        for s in range(len(SETS) - 1):
            if CROSS_BEFORE[s] == k:
                sums[s] = list(cross(sets[s], (ones, twos), sums.get(s - 1)))
                twos[k], sums[s][0] = after(twos[k], sums[s][0])
        if Y_AFTER[k] >= 0:
            twos[k], ones[Y_AFTER[k]] = after(twos[k], ones[Y_AFTER[k]])
        if CHAIN and k > 0:
            twos[k], onward[k - 1] = after(twos[k], onward[k - 1])
        for later in range(pieces):
            if Z_AFTER[later] == k:
                twos[k], mine[later] = after(twos[k], mine[later])
                twos[later] = lax.ppermute(mine[later], "ch", ahead)
        onward[k] = jnp.where(odd_chip, twos[k], mine[k])
        if k < pieces - 1:
            ones[k] = lax.ppermute(onward[k], "ch", beside)
    final = pieces - 1
    for s in range(len(SETS) - 1):
        if s not in sums:
            onward[final], twos[sets[s][0]] = after(onward[final], twos[sets[s][0]])
            if NEAR_BEFORE == pieces:
                twos[sets[s][0]], near = after(twos[sets[s][0]], near)
            if LAST_TIE:
                ones[final - 1], twos[sets[s][0]] = after(ones[final - 1], twos[sets[s][0]])
            sums[s] = list(cross(sets[s], (ones, twos), sums.get(s - 1)))
    one_sum, two_sum = sums[len(SETS) - 2]

    ones[final] = lax.ppermute(onward[final], "ch", beside)
    (two_sum,) = cross(sets[-1], (twos,), [two_sum])
    one_sum, sent = cross(sets[-1], (ones,), [one_sum], (two_sum,))
    got = lax.ppermute(sent, "ch", mate)
    out = call(
        put_own_kernel,
        "put",
        out_shape,
        [vmem()] * 2,
        hbm(),
        1000,
        1000,
        scratch_shapes=[pltpu.SemaphoreType.DMA((2, 2, band_width))],
    )(one_sum, two_sum)
    return call(
        put_got_kernel,
        "put",
        out_shape,
        [vmem(), vmem(), hbm()],
        hbm(),
        1000,
        1000,
        input_output_aliases={2: 0},
        scratch_shapes=[
            pltpu.VMEM((2,) + near_shape.shape, jnp.float32),
            pltpu.SemaphoreType.DMA((2, 2, band_width)),
        ],
    )(got, near, out)


def solution(mesh):
    placed = (P(None, None, "fq", "ch"), P("fq"))
    return jax.shard_map(
        shards,
        mesh=mesh,
        in_specs=placed,
        out_specs=P(None, None, "fq", "ch", None),
        check_vma=False,
    )
```

```python
import functools

import jax
import jax.numpy as jnp
from jax import lax
from jax.experimental import pallas as pl
from jax.experimental.pallas import tpu as pltpu
from jax.sharding import PartitionSpec as P

BANDS = 8
ROUNDS = 4
SMOOTH = 4
EPS = 1e-06

GROUP = 16
SIZES = (8,8,8,12,12,12,12,12,12)
BLOCK = 24
RAW = 3
TERMS = 3
Z_AFTER = (-1, -1, -1, 0, 2, 2, 3, 4, 5)
Y_AFTER = (-1, -1, 0, 1, 2, 3, 4, 5, 6)
LAST_TIE = 0
PUT_TIE = 1
CHAIN = 0
SETS = (5, 2, 2)
LEFT_AFTER = -1
OTHER_AFTER = 0
NEAR_BEFORE = 9
CROSS_BEFORE = (8, 9)
VMEM_LIMIT = 10 * 1024 * 1024


def vmem():
    return pl.BlockSpec(memory_space=pltpu.VMEM)


def smem():
    return pl.BlockSpec(memory_space=pltpu.SMEM)


def hbm():
    return pl.BlockSpec(memory_space=pltpu.HBM)


def call(kernel, name, out_shape, in_specs, out_specs, flops, moved, **more):
    return pl.pallas_call(
        kernel,
        out_shape=out_shape,
        in_specs=in_specs,
        out_specs=out_specs,
        compiler_params=pltpu.CompilerParams(vmem_limit_bytes=VMEM_LIMIT),
        cost_estimate=pl.CostEstimate(flops=flops, bytes_accessed=moved, transcendentals=0),
        name=name,
        **more,
    )


def power_kernel(x_ref, power_ref, edge_ref, *pieces):
    rows, width, _ = x_ref.shape
    for index, piece in enumerate(pieces):
        piece[...] = x_ref[sum(SIZES[:index]) : sum(SIZES[: index + 1])]

    def step(i, total):
        value = x_ref[i].astype(jnp.float32)
        return total + value * value

    total = lax.fori_loop(0, rows, step, jnp.zeros(power_ref.shape, jnp.float32), unroll=8)
    power = total / (rows // 2)
    power_ref[...] = power
    low = lax.axis_index("fq") == 0
    edge_ref[...] = jnp.where(low, power[width - SMOOTH :], power[:SMOOTH])


def left_kernel(x_ref, power_ref, halo_ref, left_ref, *refs):
    whites, padded = refs[:-1], refs[-1]
    rows = x_ref.shape[0]
    fq = lax.axis_index("fq")
    width, channels = power_ref.shape
    bin_total = width * lax.axis_size("fq")
    padded[...] = jnp.zeros_like(padded)
    padded[8 : 8 + width, :] = power_ref[...]

    @pl.when(fq > 0)
    def _():
        padded[8 - SMOOTH : 8, :] = halo_ref[...]

    @pl.when(fq == 0)
    def _():
        padded[8 + width : 8 + width + SMOOTH, :] = halo_ref[...]

    total = padded[8 - SMOOTH : 8 - SMOOTH + width, :]
    for offset in range(1, 2 * SMOOTH + 1):
        total = total + padded[8 - SMOOTH + offset : 8 - SMOOTH + offset + width, :]
    bins = fq * width + lax.broadcasted_iota(jnp.int32, (width, channels), 0)
    counts = jnp.minimum(bins + SMOOTH, bin_total - 1) - jnp.maximum(bins - SMOOTH, 0) + 1
    scale = lax.rsqrt(total / counts.astype(jnp.float32) + EPS)
    rest = scale
    for term in range(TERMS):
        part = rest.astype(jnp.bfloat16)
        whites[0][SIZES[RAW] + term] = part
        rest = rest - part.astype(jnp.float32)

    span = BLOCK * GROUP
    for block in range(rows // BLOCK):
        first = block * BLOCK
        for group in range(width // GROUP):
            here = slice(group * GROUP, (group + 1) * GROUP)
            raw = x_ref[first : first + BLOCK, here, :].astype(jnp.float32)
            white = (raw * scale[here][None]).astype(jnp.bfloat16)
            for index, piece in enumerate(whites):
                start = sum(SIZES[: RAW + index])
                low, high = max(start, first), min(start + SIZES[RAW + index], first + BLOCK)
                if low < high:
                    piece[low - start : high - start, here, :] = white[low - first : high - first]
            turned = white.reshape(span, channels).T
            left_ref[group, :, block * span : (block + 1) * span] = turned


def band_at(bounds_ref, bands, bin_index):
    return sum((bounds_ref[k] <= bin_index).astype(jnp.int32) for k in range(1, bands))


def each_band(bounds_ref, groups, bands, add):
    for group in range(groups):
        band = band_at(bounds_ref, bands, group * GROUP)
        add(group, band, bounds_ref[band], bounds_ref[band + 1])
    for band in range(1, bands):
        low = bounds_ref[band]
        high = jnp.where(low % GROUP == 0, low, bounds_ref[band + 1])
        add(jnp.minimum(low // GROUP, groups - 1), band, low, high)


def inside(group, low, high, shape, dimension):
    bins = group * GROUP + lax.broadcasted_iota(jnp.int32, shape, dimension) % GROUP
    return ((bins >= low) & (bins < high)).astype(jnp.float32).astype(jnp.bfloat16)


def near_kernel(bounds_ref, norm_ref, own_ref, mate_ref, out_ref):
    groups, channels, span = own_ref.shape
    half = span // 2
    bands = out_ref.shape[1]
    out_ref[...] = jnp.zeros_like(out_ref)

    def add(group, band, low, high):
        right = mate_ref[group] * inside(group, low, high, (1, span), 1)
        halves = []
        for start in (0, half):
            left = jnp.concatenate(
                [own_ref[group, :, begin : begin + half] for begin in (start, half - start)], axis=0
            )
            halves.append(
                lax.dot_general(
                    left,
                    right[:, start : start + half],
                    (((1,), (1,)), ((), ())),
                    preferred_element_type=jnp.float32,
                )
            )
        out_ref[0, band] += (halves[0][:channels] + halves[1][:channels]) * norm_ref[band]
        out_ref[1, band] += (halves[0][channels:] - halves[1][channels:]) * norm_ref[band]

    @pl.when(lax.axis_index("ch") % 2 == 1)
    def _():
        each_band(bounds_ref, groups, bands, add)


def cross_kernel(these, kinds, first, last, bounds_ref, norm_ref, own_ref, mate_ref, *refs):
    count, start = len(these), sum(SIZES[: these[0]])
    rights = [refs[k * count : (k + 1) * count] for k in range(kinds)]
    refs = refs[kinds * count :]
    if not first:
        befores, refs = refs[:kinds], refs[kinds:]
    sums = refs[:kinds]
    width, channels = rights[0][0].shape[1:]
    bands = sums[0].shape[2]
    half = own_ref.shape[2] // 2
    lanes = slice(start * GROUP, sum(SIZES[: these[-1] + 1]) * GROUP)
    turned = lanes.start >= half
    shift = -half if turned else half
    across = slice(lanes.start + shift, lanes.stop + shift)
    for k in range(kinds):
        sums[k][...] = jnp.zeros_like(sums[k]) if first else befores[k][...]

    def column(right, here, held):
        scale = None
        if first:
            for term in range(TERMS):
                part = right[RAW][SIZES[RAW] + term, here, :].astype(jnp.float32)
                scale = part if scale is None else scale + part
        blocks = []
        for index, ref in enumerate(right):
            size = SIZES[these[index]]
            block = ref[:size, here, :]
            if first and index < RAW:
                block = (block.astype(jnp.float32) * scale[None]).astype(jnp.bfloat16)
            blocks.append((block * held[None]).reshape(size * GROUP, channels))
        return jnp.concatenate(blocks, axis=0)

    def add(group, band, low, high):
        begin = group * GROUP
        here = pl.ds(begin if isinstance(group, int) else pl.multiple_of(begin, GROUP), GROUP)
        held = inside(group, low, high, (GROUP, channels), 0)
        left = jnp.concatenate(
            [ref[group, :, part] for ref in (own_ref, mate_ref) for part in (lanes, across)], axis=0
        )
        right = jnp.concatenate([column(right, here, held) for right in rights], axis=1)
        product = jnp.dot(left, right, preferred_element_type=jnp.float32) * norm_ref[band]
        for k in range(kinds):
            for owner in range(2):
                for part in range(2):
                    row = (2 * owner + part) * channels
                    term = product[row : row + channels, k * channels : (k + 1) * channels]
                    sums[k][part, owner, band] += -term if part and turned else term

    each_band(bounds_ref, width // GROUP, bands, add)
    if last:
        refs[kinds][...] = sums[0][:, 1].astype(jnp.bfloat16)


def put_kernel(kind, *refs):
    value_ref, refs = refs[0], refs[1:]
    core = lax.axis_index("ch") % 2
    if kind == "near":
        near_ref, refs = refs[0], refs[1:]
    out_ref, wide, sems = refs[-3:]
    turn = {"one": 1, "two": 3, "far": 2 * core, "near": 2 - 2 * core}[kind]
    copies = []
    for part in range(2):
        for band in range(out_ref.shape[2]):
            if kind in ("one", "two"):
                source = value_ref.at[part, 0, band]
            else:
                value = value_ref[part, band].astype(jnp.float32)
                if kind == "near":
                    value = jnp.where(core == 0, value, near_ref[part, band])
                wide[part, band] = value
                source = wide.at[part, band]
            copies.append(
                pltpu.make_async_copy(source, out_ref.at[part, turn, band], sems.at[part, band])
            )
            copies[-1].start()
    for copy in copies:
        copy.wait()


def after(value, other):
    return lax.optimization_barrier((value, other))


def shards(spectra, band_ids):
    parts, windows, width, channels = spectra.shape
    rows = parts * windows
    count = lax.axis_size("ch")
    fq_count = lax.axis_size("fq")
    index = lax.axis_index("ch")
    fq = lax.axis_index("fq")
    even_core = index % 2 == 0
    odd_chip = (index // 2) % 2 == 1

    ahead = [(i, (i + 4) % count) for i in range(count)]
    beside = [(i, i ^ 2) for i in range(count)]
    mate = [(i, i ^ 1) for i in range(count)]

    own = spectra.reshape(rows, width, channels)
    pieces = len(SIZES)
    heights = [size + (TERMS if k == RAW else 0) for k, size in enumerate(SIZES)]
    block = jax.ShapeDtypeStruct((width, channels), jnp.float32)
    edge = jax.ShapeDtypeStruct((SMOOTH, channels), jnp.float32)
    held = [jax.ShapeDtypeStruct((h, width, channels), jnp.bfloat16) for h in heights]
    groups = width // GROUP
    left_shape = jax.ShapeDtypeStruct((groups, channels, rows * GROUP), jnp.bfloat16)
    nbytes = rows * width * channels * 2

    power, edge, *early = call(
        power_kernel,
        "power",
        (block, edge, *held[:RAW]),
        [vmem()],
        (vmem(),) * (2 + RAW),
        nbytes,
        nbytes,
    )(own)
    band_width = BANDS // fq_count
    local_band = band_ids - fq * band_width
    below = local_band[:, None] < jnp.arange(band_width + 1, dtype=jnp.int32)[None, :]
    bounds = jnp.sum(below.astype(jnp.int32), axis=0)
    norms = 1.0 / jnp.sqrt(windows * (bounds[1:] - bounds[:-1]).astype(jnp.float32))
    power, norms = after(power, norms)

    twos = {k: lax.ppermute(early[k], "ch", ahead) for k in range(RAW)}
    halo = lax.ppermute(edge, "fq", [(0, 1), (1, 0)])
    if LEFT_AFTER >= 0:
        twos[LEFT_AFTER], halo = after(twos[LEFT_AFTER], halo)
    left, *late = call(
        left_kernel,
        "left",
        (left_shape, *held[RAW:]),
        [vmem()] * 3,
        (vmem(),) * (1 + pieces - RAW),
        nbytes,
        nbytes,
        scratch_shapes=[pltpu.VMEM((width + 16, channels), jnp.float32)],
    )(own, power, halo)
    mine = early + late

    out_shape = jax.ShapeDtypeStruct((2, ROUNDS, band_width, channels, channels), jnp.float32)
    sum_shape = jax.ShapeDtypeStruct((2, 2, band_width, channels, channels), jnp.float32)
    near_shape = jax.ShapeDtypeStruct((2, band_width, channels, channels), jnp.float32)
    send_shape = jax.ShapeDtypeStruct((2, band_width, channels, channels), jnp.bfloat16)

    sets = [range(sum(SETS[:s]), sum(SETS[: s + 1])) for s in range(len(SETS))]
    ones, onward = {}, {}
    sums = {}

    def cross(these, flights, befores, last=False):
        first = befores is None
        operands = [bounds, norms, left, other]
        for flight in flights:
            operands += [flight[k] for k in these]
        operands += [] if first else befores
        kinds = len(flights)
        return call(
            functools.partial(
                cross_kernel, tuple(these), kinds, first, last
            ),
            "cross",
            (sum_shape,) * kinds + (send_shape,) * last,
            [smem(), smem()] + [vmem()] * (len(operands) - 2),
            (vmem(),) * (kinds + last),
            8 * kinds * sum(SIZES[k] for k in these) * width * channels * channels,
            0 * nbytes,
        )(*operands)

    for k in range(RAW, pieces):
        if Z_AFTER[k] < 0:
            twos[k] = lax.ppermute(mine[k], "ch", ahead)
    left, twos[OTHER_AFTER] = after(left, twos[OTHER_AFTER])
    other = lax.ppermute(left, "ch", mate)
    near = call(
        near_kernel,
        "near",
        near_shape,
        [smem(), smem(), vmem(), vmem()],
        vmem(),
        1000,
        1000,
    )(bounds, norms, left, other)

    for k in range(pieces):
        if k == NEAR_BEFORE:
            twos[k], near = after(twos[k], near)
        for s in range(len(SETS) - 1):
            if CROSS_BEFORE[s] == k:
                sums[s] = list(cross(sets[s], (ones, twos), sums.get(s - 1)))
                twos[k], sums[s][0] = after(twos[k], sums[s][0])
        if Y_AFTER[k] >= 0:
            twos[k], ones[Y_AFTER[k]] = after(twos[k], ones[Y_AFTER[k]])
        if CHAIN and k > 0:
            twos[k], onward[k - 1] = after(twos[k], onward[k - 1])
        for later in range(pieces):
            if Z_AFTER[later] == k:
                twos[k], mine[later] = after(twos[k], mine[later])
                twos[later] = lax.ppermute(mine[later], "ch", ahead)
        onward[k] = jnp.where(odd_chip, twos[k], mine[k])
        if k < pieces - 1:
            ones[k] = lax.ppermute(onward[k], "ch", beside)
    final = pieces - 1
    for s in range(len(SETS) - 1):
        if s not in sums:
            onward[final], twos[sets[s][0]] = after(onward[final], twos[sets[s][0]])
            if NEAR_BEFORE == pieces:
                twos[sets[s][0]], near = after(twos[sets[s][0]], near)
            if LAST_TIE:
                ones[final - 1], twos[sets[s][0]] = after(ones[final - 1], twos[sets[s][0]])
            sums[s] = list(cross(sets[s], (ones, twos), sums.get(s - 1)))
    one_sum, two_sum = sums[len(SETS) - 2]

    def put(kind, out, *values):
        aliased = out is not None
        operands = [*values, out] if aliased else list(values)
        return call(
            functools.partial(put_kernel, kind),
            "put",
            out_shape,
            [vmem()] * len(values) + [hbm()] * aliased,
            hbm(),
            1000,
            4 * nbytes,
            input_output_aliases={len(values): 0} if aliased else {},
            scratch_shapes=[
                pltpu.VMEM(near_shape.shape, jnp.float32),
                pltpu.SemaphoreType.DMA((2, band_width)),
            ],
        )(*operands)

    ones[final] = lax.ppermute(onward[final], "ch", beside)
    two_sum, two_sent = cross(sets[-1], (twos,), [two_sum], True)
    two_got = lax.ppermute(two_sent, "ch", mate)
    out = put("two", None, two_sum)
    if PUT_TIE:
        one_sum, out = after(one_sum, out)
    one_sum, one_sent = cross(sets[-1], (ones,), [one_sum], True)
    one_got = lax.ppermute(one_sent, "ch", mate)
    out = put("one", out, one_sum)
    out = put("near", out, two_got, near)
    return put("far", out, one_got)


def solution(mesh):
    placed = (P(None, None, "fq", "ch"), P("fq"))
    return jax.shard_map(
        shards,
        mesh=mesh,
        in_specs=placed,
        out_specs=P(None, None, "fq", "ch", None),
        check_vma=False,
    )
```

```python
import functools

import jax
import jax.numpy as jnp
from jax import lax
from jax.experimental import pallas as pl
from jax.experimental.pallas import tpu as pltpu
from jax.sharding import PartitionSpec as P

BANDS = 8
ROUNDS = 4
SMOOTH = 4
EPS = 1e-06

GROUP = 16
SIZES = (4,8,12,12,12,12,12,12,12)
BLOCK = 24
RAW = 3
TERMS = 3
Z_AFTER = (-1, -1, -1, 0, 2, 2, 3, 4, 5)
Y_AFTER = (-1, -1, 0, 1, 2, 3, 4, 5, 6)
LAST_TIE = 0
PUT_TIE = 1
CHAIN = 0
SETS = (5, 2, 2)
LEFT_AFTER = -1
OTHER_AFTER = 0
NEAR_BEFORE = 8
CROSS_BEFORE = (7, 9)
VMEM_LIMIT = 10 * 1024 * 1024


def vmem():
    return pl.BlockSpec(memory_space=pltpu.VMEM)


def smem():
    return pl.BlockSpec(memory_space=pltpu.SMEM)


def hbm():
    return pl.BlockSpec(memory_space=pltpu.HBM)


def call(kernel, name, out_shape, in_specs, out_specs, flops, moved, **more):
    return pl.pallas_call(
        kernel,
        out_shape=out_shape,
        in_specs=in_specs,
        out_specs=out_specs,
        compiler_params=pltpu.CompilerParams(vmem_limit_bytes=VMEM_LIMIT),
        cost_estimate=pl.CostEstimate(flops=flops, bytes_accessed=moved, transcendentals=0),
        name=name,
        **more,
    )


def power_kernel(x_ref, power_ref, edge_ref, *pieces):
    rows, width, _ = x_ref.shape
    for index, piece in enumerate(pieces):
        piece[...] = x_ref[sum(SIZES[:index]) : sum(SIZES[: index + 1])]

    def step(i, total):
        value = x_ref[i].astype(jnp.float32)
        return total + value * value

    total = lax.fori_loop(0, rows, step, jnp.zeros(power_ref.shape, jnp.float32), unroll=8)
    power = total / (rows // 2)
    power_ref[...] = power
    low = lax.axis_index("fq") == 0
    edge_ref[...] = jnp.where(low, power[width - SMOOTH :], power[:SMOOTH])


def left_kernel(x_ref, power_ref, halo_ref, left_ref, *refs):
    whites, padded = refs[:-1], refs[-1]
    rows = x_ref.shape[0]
    fq = lax.axis_index("fq")
    width, channels = power_ref.shape
    bin_total = width * lax.axis_size("fq")
    padded[...] = jnp.zeros_like(padded)
    padded[8 : 8 + width, :] = power_ref[...]

    @pl.when(fq > 0)
    def _():
        padded[8 - SMOOTH : 8, :] = halo_ref[...]

    @pl.when(fq == 0)
    def _():
        padded[8 + width : 8 + width + SMOOTH, :] = halo_ref[...]

    total = padded[8 - SMOOTH : 8 - SMOOTH + width, :]
    for offset in range(1, 2 * SMOOTH + 1):
        total = total + padded[8 - SMOOTH + offset : 8 - SMOOTH + offset + width, :]
    bins = fq * width + lax.broadcasted_iota(jnp.int32, (width, channels), 0)
    counts = jnp.minimum(bins + SMOOTH, bin_total - 1) - jnp.maximum(bins - SMOOTH, 0) + 1
    scale = lax.rsqrt(total / counts.astype(jnp.float32) + EPS)
    rest = scale
    for term in range(TERMS):
        part = rest.astype(jnp.bfloat16)
        whites[0][SIZES[RAW] + term] = part
        rest = rest - part.astype(jnp.float32)

    span = BLOCK * GROUP
    for block in range(rows // BLOCK):
        first = block * BLOCK
        for group in range(width // GROUP):
            here = slice(group * GROUP, (group + 1) * GROUP)
            raw = x_ref[first : first + BLOCK, here, :].astype(jnp.float32)
            white = (raw * scale[here][None]).astype(jnp.bfloat16)
            for index, piece in enumerate(whites):
                start = sum(SIZES[: RAW + index])
                low, high = max(start, first), min(start + SIZES[RAW + index], first + BLOCK)
                if low < high:
                    piece[low - start : high - start, here, :] = white[low - first : high - first]
            turned = white.reshape(span, channels).T
            left_ref[group, :, block * span : (block + 1) * span] = turned


def band_at(bounds_ref, bands, bin_index):
    return sum((bounds_ref[k] <= bin_index).astype(jnp.int32) for k in range(1, bands))


def each_band(bounds_ref, groups, bands, add):
    for group in range(groups):
        band = band_at(bounds_ref, bands, group * GROUP)
        add(group, band, bounds_ref[band], bounds_ref[band + 1])
    for band in range(1, bands):
        low = bounds_ref[band]
        high = jnp.where(low % GROUP == 0, low, bounds_ref[band + 1])
        add(jnp.minimum(low // GROUP, groups - 1), band, low, high)


def inside(group, low, high, shape, dimension):
    bins = group * GROUP + lax.broadcasted_iota(jnp.int32, shape, dimension) % GROUP
    return ((bins >= low) & (bins < high)).astype(jnp.float32).astype(jnp.bfloat16)


def near_kernel(bounds_ref, norm_ref, own_ref, mate_ref, out_ref):
    groups, channels, span = own_ref.shape
    half = span // 2
    bands = out_ref.shape[1]
    out_ref[...] = jnp.zeros_like(out_ref)

    def add(group, band, low, high):
        right = mate_ref[group] * inside(group, low, high, (1, span), 1)
        halves = []
        for start in (0, half):
            left = jnp.concatenate(
                [own_ref[group, :, begin : begin + half] for begin in (start, half - start)], axis=0
            )
            halves.append(
                lax.dot_general(
                    left,
                    right[:, start : start + half],
                    (((1,), (1,)), ((), ())),
                    preferred_element_type=jnp.float32,
                )
            )
        out_ref[0, band] += (halves[0][:channels] + halves[1][:channels]) * norm_ref[band]
        out_ref[1, band] += (halves[0][channels:] - halves[1][channels:]) * norm_ref[band]

    @pl.when(lax.axis_index("ch") % 2 == 1)
    def _():
        each_band(bounds_ref, groups, bands, add)


def cross_kernel(these, kinds, first, last, bounds_ref, norm_ref, own_ref, mate_ref, *refs):
    count, start = len(these), sum(SIZES[: these[0]])
    rights = [refs[k * count : (k + 1) * count] for k in range(kinds)]
    refs = refs[kinds * count :]
    if not first:
        befores, refs = refs[:kinds], refs[kinds:]
    sums = refs[:kinds]
    width, channels = rights[0][0].shape[1:]
    bands = sums[0].shape[2]
    half = own_ref.shape[2] // 2
    lanes = slice(start * GROUP, sum(SIZES[: these[-1] + 1]) * GROUP)
    turned = lanes.start >= half
    shift = -half if turned else half
    across = slice(lanes.start + shift, lanes.stop + shift)
    for k in range(kinds):
        sums[k][...] = jnp.zeros_like(sums[k]) if first else befores[k][...]

    def column(right, here, held):
        scale = None
        if first:
            for term in range(TERMS):
                part = right[RAW][SIZES[RAW] + term, here, :].astype(jnp.float32)
                scale = part if scale is None else scale + part
        blocks = []
        for index, ref in enumerate(right):
            size = SIZES[these[index]]
            block = ref[:size, here, :]
            if first and index < RAW:
                block = (block.astype(jnp.float32) * scale[None]).astype(jnp.bfloat16)
            blocks.append((block * held[None]).reshape(size * GROUP, channels))
        return jnp.concatenate(blocks, axis=0)

    def add(group, band, low, high):
        begin = group * GROUP
        here = pl.ds(begin if isinstance(group, int) else pl.multiple_of(begin, GROUP), GROUP)
        held = inside(group, low, high, (GROUP, channels), 0)
        left = jnp.concatenate(
            [ref[group, :, part] for ref in (own_ref, mate_ref) for part in (lanes, across)], axis=0
        )
        right = jnp.concatenate([column(right, here, held) for right in rights], axis=1)
        product = jnp.dot(left, right, preferred_element_type=jnp.float32) * norm_ref[band]
        for k in range(kinds):
            for owner in range(2):
                for part in range(2):
                    row = (2 * owner + part) * channels
                    term = product[row : row + channels, k * channels : (k + 1) * channels]
                    sums[k][part, owner, band] += -term if part and turned else term

    each_band(bounds_ref, width // GROUP, bands, add)
    if last:
        refs[kinds][...] = sums[0][:, 1].astype(jnp.bfloat16)


def put_kernel(kind, *refs):
    value_ref, refs = refs[0], refs[1:]
    core = lax.axis_index("ch") % 2
    if kind == "near":
        near_ref, refs = refs[0], refs[1:]
    out_ref, wide, sems = refs[-3:]
    turn = {"one": 1, "two": 3, "far": 2 * core, "near": 2 - 2 * core}[kind]
    copies = []
    for part in range(2):
        for band in range(out_ref.shape[2]):
            if kind in ("one", "two"):
                source = value_ref.at[part, 0, band]
            else:
                value = value_ref[part, band].astype(jnp.float32)
                if kind == "near":
                    value = jnp.where(core == 0, value, near_ref[part, band])
                wide[part, band] = value
                source = wide.at[part, band]
            copies.append(
                pltpu.make_async_copy(source, out_ref.at[part, turn, band], sems.at[part, band])
            )
            copies[-1].start()
    for copy in copies:
        copy.wait()


def after(value, other):
    return lax.optimization_barrier((value, other))


def shards(spectra, band_ids):
    parts, windows, width, channels = spectra.shape
    rows = parts * windows
    count = lax.axis_size("ch")
    fq_count = lax.axis_size("fq")
    index = lax.axis_index("ch")
    fq = lax.axis_index("fq")
    even_core = index % 2 == 0
    odd_chip = (index // 2) % 2 == 1

    ahead = [(i, (i + 4) % count) for i in range(count)]
    beside = [(i, i ^ 2) for i in range(count)]
    mate = [(i, i ^ 1) for i in range(count)]

    own = spectra.reshape(rows, width, channels)
    pieces = len(SIZES)
    heights = [size + (TERMS if k == RAW else 0) for k, size in enumerate(SIZES)]
    block = jax.ShapeDtypeStruct((width, channels), jnp.float32)
    edge = jax.ShapeDtypeStruct((SMOOTH, channels), jnp.float32)
    held = [jax.ShapeDtypeStruct((h, width, channels), jnp.bfloat16) for h in heights]
    groups = width // GROUP
    left_shape = jax.ShapeDtypeStruct((groups, channels, rows * GROUP), jnp.bfloat16)
    nbytes = rows * width * channels * 2

    power, edge, *early = call(
        power_kernel,
        "power",
        (block, edge, *held[:RAW]),
        [vmem()],
        (vmem(),) * (2 + RAW),
        nbytes,
        nbytes,
    )(own)
    band_width = BANDS // fq_count
    local_band = band_ids - fq * band_width
    below = local_band[:, None] < jnp.arange(band_width + 1, dtype=jnp.int32)[None, :]
    bounds = jnp.sum(below.astype(jnp.int32), axis=0)
    norms = 1.0 / jnp.sqrt(windows * (bounds[1:] - bounds[:-1]).astype(jnp.float32))
    power, norms = after(power, norms)

    twos = {k: lax.ppermute(early[k], "ch", ahead) for k in range(RAW)}
    halo = lax.ppermute(edge, "fq", [(0, 1), (1, 0)])
    if LEFT_AFTER >= 0:
        twos[LEFT_AFTER], halo = after(twos[LEFT_AFTER], halo)
    left, *late = call(
        left_kernel,
        "left",
        (left_shape, *held[RAW:]),
        [vmem()] * 3,
        (vmem(),) * (1 + pieces - RAW),
        nbytes,
        nbytes,
        scratch_shapes=[pltpu.VMEM((width + 16, channels), jnp.float32)],
    )(own, power, halo)
    mine = early + late

    out_shape = jax.ShapeDtypeStruct((2, ROUNDS, band_width, channels, channels), jnp.float32)
    sum_shape = jax.ShapeDtypeStruct((2, 2, band_width, channels, channels), jnp.float32)
    near_shape = jax.ShapeDtypeStruct((2, band_width, channels, channels), jnp.float32)
    send_shape = jax.ShapeDtypeStruct((2, band_width, channels, channels), jnp.bfloat16)

    sets = [range(sum(SETS[:s]), sum(SETS[: s + 1])) for s in range(len(SETS))]
    ones, onward = {}, {}
    sums = {}

    def cross(these, flights, befores, last=False):
        first = befores is None
        operands = [bounds, norms, left, other]
        for flight in flights:
            operands += [flight[k] for k in these]
        operands += [] if first else befores
        kinds = len(flights)
        return call(
            functools.partial(
                cross_kernel, tuple(these), kinds, first, last
            ),
            "cross",
            (sum_shape,) * kinds + (send_shape,) * last,
            [smem(), smem()] + [vmem()] * (len(operands) - 2),
            (vmem(),) * (kinds + last),
            8 * kinds * sum(SIZES[k] for k in these) * width * channels * channels,
            0 * nbytes,
        )(*operands)

    for k in range(RAW, pieces):
        if Z_AFTER[k] < 0:
            twos[k] = lax.ppermute(mine[k], "ch", ahead)
    left, twos[OTHER_AFTER] = after(left, twos[OTHER_AFTER])
    other = lax.ppermute(left, "ch", mate)
    near = call(
        near_kernel,
        "near",
        near_shape,
        [smem(), smem(), vmem(), vmem()],
        vmem(),
        1000,
        1000,
    )(bounds, norms, left, other)

    for k in range(pieces):
        if k == NEAR_BEFORE:
            twos[k], near = after(twos[k], near)
        for s in range(len(SETS) - 1):
            if CROSS_BEFORE[s] == k:
                sums[s] = list(cross(sets[s], (ones, twos), sums.get(s - 1)))
                twos[k], sums[s][0] = after(twos[k], sums[s][0])
        if Y_AFTER[k] >= 0:
            twos[k], ones[Y_AFTER[k]] = after(twos[k], ones[Y_AFTER[k]])
        if CHAIN and k > 0:
            twos[k], onward[k - 1] = after(twos[k], onward[k - 1])
        for later in range(pieces):
            if Z_AFTER[later] == k:
                twos[k], mine[later] = after(twos[k], mine[later])
                twos[later] = lax.ppermute(mine[later], "ch", ahead)
        onward[k] = jnp.where(odd_chip, twos[k], mine[k])
        if k < pieces - 1:
            ones[k] = lax.ppermute(onward[k], "ch", beside)
    final = pieces - 1
    for s in range(len(SETS) - 1):
        if s not in sums:
            onward[final], twos[sets[s][0]] = after(onward[final], twos[sets[s][0]])
            if NEAR_BEFORE == pieces:
                twos[sets[s][0]], near = after(twos[sets[s][0]], near)
            if LAST_TIE:
                ones[final - 1], twos[sets[s][0]] = after(ones[final - 1], twos[sets[s][0]])
            sums[s] = list(cross(sets[s], (ones, twos), sums.get(s - 1)))
    one_sum, two_sum = sums[len(SETS) - 2]

    def put(kind, out, *values):
        aliased = out is not None
        operands = [*values, out] if aliased else list(values)
        return call(
            functools.partial(put_kernel, kind),
            "put",
            out_shape,
            [vmem()] * len(values) + [hbm()] * aliased,
            hbm(),
            1000,
            4 * nbytes,
            input_output_aliases={len(values): 0} if aliased else {},
            scratch_shapes=[
                pltpu.VMEM(near_shape.shape, jnp.float32),
                pltpu.SemaphoreType.DMA((2, band_width)),
            ],
        )(*operands)

    ones[final] = lax.ppermute(onward[final], "ch", beside)
    two_sum, two_sent = cross(sets[-1], (twos,), [two_sum], True)
    two_got = lax.ppermute(two_sent, "ch", mate)
    out = put("two", None, two_sum)
    if PUT_TIE:
        one_sum, out = after(one_sum, out)
    one_sum, one_sent = cross(sets[-1], (ones,), [one_sum], True)
    one_got = lax.ppermute(one_sent, "ch", mate)
    out = put("one", out, one_sum)
    out = put("near", out, two_got, near)
    return put("far", out, one_got)


def solution(mesh):
    placed = (P(None, None, "fq", "ch"), P("fq"))
    return jax.shard_map(
        shards,
        mesh=mesh,
        in_specs=placed,
        out_specs=P(None, None, "fq", "ch", None),
        check_vma=False,
    )
```

```python
import functools

import jax
import jax.numpy as jnp
from jax import lax
from jax.experimental import pallas as pl
from jax.experimental.pallas import tpu as pltpu
from jax.sharding import PartitionSpec as P

BANDS = 8
ROUNDS = 4
SMOOTH = 4
EPS = 1e-06

GROUP = 16
SIZES = (4,8,12,12,12,12,12,12,12)
BLOCK = 24
RAW = 3
TERMS = 3
Z_AFTER = (-1, -1, -1, 0, 2, 2, 3, 4, 5)
Y_AFTER = (-1, -1, 0, 1, 2, 3, 4, 5, 6)
LAST_TIE = 0
PUT_TIE = 1
CHAIN = 0
SETS = (5, 2, 2)
LEFT_AFTER = -1
OTHER_AFTER = 0
NEAR_BEFORE = 8
CROSS_BEFORE = 7
VMEM_LIMIT = 10 * 1024 * 1024


def vmem():
    return pl.BlockSpec(memory_space=pltpu.VMEM)


def smem():
    return pl.BlockSpec(memory_space=pltpu.SMEM)


def hbm():
    return pl.BlockSpec(memory_space=pltpu.HBM)


def call(kernel, name, out_shape, in_specs, out_specs, flops, moved, **more):
    return pl.pallas_call(
        kernel,
        out_shape=out_shape,
        in_specs=in_specs,
        out_specs=out_specs,
        compiler_params=pltpu.CompilerParams(vmem_limit_bytes=VMEM_LIMIT),
        cost_estimate=pl.CostEstimate(flops=flops, bytes_accessed=moved, transcendentals=0),
        name=name,
        **more,
    )


def power_kernel(x_ref, power_ref, edge_ref, *pieces):
    rows, width, _ = x_ref.shape
    for index, piece in enumerate(pieces):
        piece[...] = x_ref[sum(SIZES[:index]) : sum(SIZES[: index + 1])]

    def step(i, total):
        value = x_ref[i].astype(jnp.float32)
        return total + value * value

    total = lax.fori_loop(0, rows, step, jnp.zeros(power_ref.shape, jnp.float32), unroll=8)
    power = total / (rows // 2)
    power_ref[...] = power
    low = lax.axis_index("fq") == 0
    edge_ref[...] = jnp.where(low, power[width - SMOOTH :], power[:SMOOTH])


def left_kernel(x_ref, power_ref, halo_ref, left_ref, *refs):
    whites, padded = refs[:-1], refs[-1]
    rows = x_ref.shape[0]
    fq = lax.axis_index("fq")
    width, channels = power_ref.shape
    bin_total = width * lax.axis_size("fq")
    padded[...] = jnp.zeros_like(padded)
    padded[8 : 8 + width, :] = power_ref[...]

    @pl.when(fq > 0)
    def _():
        padded[8 - SMOOTH : 8, :] = halo_ref[...]

    @pl.when(fq == 0)
    def _():
        padded[8 + width : 8 + width + SMOOTH, :] = halo_ref[...]

    total = padded[8 - SMOOTH : 8 - SMOOTH + width, :]
    for offset in range(1, 2 * SMOOTH + 1):
        total = total + padded[8 - SMOOTH + offset : 8 - SMOOTH + offset + width, :]
    bins = fq * width + lax.broadcasted_iota(jnp.int32, (width, channels), 0)
    counts = jnp.minimum(bins + SMOOTH, bin_total - 1) - jnp.maximum(bins - SMOOTH, 0) + 1
    scale = lax.rsqrt(total / counts.astype(jnp.float32) + EPS)
    rest = scale
    for term in range(TERMS):
        part = rest.astype(jnp.bfloat16)
        whites[0][SIZES[RAW] + term] = part
        rest = rest - part.astype(jnp.float32)

    span = BLOCK * GROUP
    for block in range(rows // BLOCK):
        first = block * BLOCK
        for group in range(width // GROUP):
            here = slice(group * GROUP, (group + 1) * GROUP)
            raw = x_ref[first : first + BLOCK, here, :].astype(jnp.float32)
            white = (raw * scale[here][None]).astype(jnp.bfloat16)
            for index, piece in enumerate(whites):
                start = sum(SIZES[: RAW + index])
                low, high = max(start, first), min(start + SIZES[RAW + index], first + BLOCK)
                if low < high:
                    piece[low - start : high - start, here, :] = white[low - first : high - first]
            turned = white.reshape(span, channels).T
            left_ref[group, :, block * span : (block + 1) * span] = turned


def band_at(bounds_ref, bands, bin_index):
    return sum((bounds_ref[k] <= bin_index).astype(jnp.int32) for k in range(1, bands))


def each_band(bounds_ref, groups, bands, add):
    for group in range(groups):
        band = band_at(bounds_ref, bands, group * GROUP)
        add(group, band, bounds_ref[band], bounds_ref[band + 1])
    for band in range(1, bands):
        low = bounds_ref[band]
        high = jnp.where(low % GROUP == 0, low, bounds_ref[band + 1])
        add(jnp.minimum(low // GROUP, groups - 1), band, low, high)


def inside(group, low, high, shape, dimension):
    bins = group * GROUP + lax.broadcasted_iota(jnp.int32, shape, dimension) % GROUP
    return ((bins >= low) & (bins < high)).astype(jnp.float32).astype(jnp.bfloat16)


def near_kernel(bounds_ref, norm_ref, own_ref, mate_ref, out_ref):
    groups, channels, span = own_ref.shape
    half = span // 2
    bands = out_ref.shape[1]
    out_ref[...] = jnp.zeros_like(out_ref)

    def add(group, band, low, high):
        right = mate_ref[group] * inside(group, low, high, (1, span), 1)
        halves = []
        for start in (0, half):
            left = jnp.concatenate(
                [own_ref[group, :, begin : begin + half] for begin in (start, half - start)], axis=0
            )
            halves.append(
                lax.dot_general(
                    left,
                    right[:, start : start + half],
                    (((1,), (1,)), ((), ())),
                    preferred_element_type=jnp.float32,
                )
            )
        out_ref[0, band] += (halves[0][:channels] + halves[1][:channels]) * norm_ref[band]
        out_ref[1, band] += (halves[0][channels:] - halves[1][channels:]) * norm_ref[band]

    @pl.when(lax.axis_index("ch") % 2 == 1)
    def _():
        each_band(bounds_ref, groups, bands, add)


def cross_kernel(jobs, first, sent, bounds_ref, norm_ref, own_ref, mate_ref, *refs):
    present = sorted({kind for kinds, _ in jobs for kind in kinds})
    work = []
    for kinds, these in jobs:
        taken = []
        for _ in kinds:
            taken.append(refs[: len(these)])
            refs = refs[len(these) :]
        work.append((kinds, these, taken))
    if not first:
        befores, refs = refs[: len(present)], refs[len(present) :]
    sums = dict(zip(present, refs))
    width, channels = work[0][2][0][0].shape[1:]
    bands = refs[0].shape[2]
    half = own_ref.shape[2] // 2
    for index, kind in enumerate(present):
        sums[kind][...] = jnp.zeros_like(refs[0]) if first else befores[index][...]

    def column(right, these, here, held):
        scale = None
        if first:
            for term in range(TERMS):
                part = right[RAW][SIZES[RAW] + term, here, :].astype(jnp.float32)
                scale = part if scale is None else scale + part
        blocks = []
        for ref, number in zip(right, these):
            size = SIZES[number]
            block = ref[:size, here, :]
            if number < RAW:
                block = (block.astype(jnp.float32) * scale[None]).astype(jnp.bfloat16)
            blocks.append((block * held[None]).reshape(size * GROUP, channels))
        return jnp.concatenate(blocks, axis=0)

    def multiply(kinds, these, taken, owners):
        start, stop = sum(SIZES[: these[0]]) * GROUP, sum(SIZES[: these[-1] + 1]) * GROUP
        turned = start >= half
        shift = -half if turned else half
        parts = slice(start, stop), slice(start + shift, stop + shift)

        def add(group, band, low, high):
            begin = group * GROUP
            here = pl.ds(begin if isinstance(group, int) else pl.multiple_of(begin, GROUP), GROUP)
            held = inside(group, low, high, (GROUP, channels), 0)
            left = jnp.concatenate(
                [ref[group, :, part] for ref in (own_ref, mate_ref)[:owners] for part in parts], axis=0
            )
            right = jnp.concatenate([column(right, these, here, held) for right in taken], axis=1)
            product = jnp.dot(left, right, preferred_element_type=jnp.float32) * norm_ref[band]
            for k, kind in enumerate(kinds):
                for owner in range(owners):
                    for part in range(2):
                        row = (2 * owner + part) * channels
                        term = product[row : row + channels, k * channels : (k + 1) * channels]
                        sums[kind][part, owner, band] += -term if part and turned else term

        each_band(bounds_ref, width // GROUP, bands, add)

    core = lax.axis_index("ch") % 2
    for kinds, these, taken in work:
        if kinds == (1,):
            pl.when(core == 0)(functools.partial(multiply, kinds, these, taken, 1))
            pl.when(core == 1)(functools.partial(multiply, kinds, these, taken, 2))
        else:
            multiply(kinds, these, taken, 2)
    if sent is not None:
        refs[-1][...] = sums[sent][:, 1].astype(jnp.bfloat16)


def put_kernel(kind, *refs):
    value_ref, refs = refs[0], refs[1:]
    core = lax.axis_index("ch") % 2
    if kind == "near":
        near_ref, refs = refs[0], refs[1:]
    out_ref, wide, sems = refs[-3:]
    turn = {"one": 1, "two": 3, "far": 2 * core, "near": 2 - 2 * core}[kind]
    copies = []
    for part in range(2):
        for band in range(out_ref.shape[2]):
            if kind in ("one", "two"):
                source = value_ref.at[part, 0, band]
            else:
                value = value_ref[part, band].astype(jnp.float32)
                if kind == "near":
                    value = jnp.where(core == 0, value, near_ref[part, band])
                wide[part, band] = value
                source = wide.at[part, band]
            copies.append(
                pltpu.make_async_copy(source, out_ref.at[part, turn, band], sems.at[part, band])
            )
            copies[-1].start()
    for copy in copies:
        copy.wait()


def after(value, other):
    return lax.optimization_barrier((value, other))


def shards(spectra, band_ids):
    parts, windows, width, channels = spectra.shape
    rows = parts * windows
    count = lax.axis_size("ch")
    fq_count = lax.axis_size("fq")
    index = lax.axis_index("ch")
    fq = lax.axis_index("fq")
    even_core = index % 2 == 0
    odd_chip = (index // 2) % 2 == 1

    ahead = [(i, (i + 4) % count) for i in range(count)]
    beside = [(i, i ^ 2) for i in range(count)]
    mate = [(i, i ^ 1) for i in range(count)]

    own = spectra.reshape(rows, width, channels)
    pieces = len(SIZES)
    heights = [size + (TERMS if k == RAW else 0) for k, size in enumerate(SIZES)]
    block = jax.ShapeDtypeStruct((width, channels), jnp.float32)
    edge = jax.ShapeDtypeStruct((SMOOTH, channels), jnp.float32)
    held = [jax.ShapeDtypeStruct((h, width, channels), jnp.bfloat16) for h in heights]
    groups = width // GROUP
    left_shape = jax.ShapeDtypeStruct((groups, channels, rows * GROUP), jnp.bfloat16)
    nbytes = rows * width * channels * 2

    power, edge, *early = call(
        power_kernel,
        "power",
        (block, edge, *held[:RAW]),
        [vmem()],
        (vmem(),) * (2 + RAW),
        nbytes,
        nbytes,
    )(own)
    band_width = BANDS // fq_count
    local_band = band_ids - fq * band_width
    below = local_band[:, None] < jnp.arange(band_width + 1, dtype=jnp.int32)[None, :]
    bounds = jnp.sum(below.astype(jnp.int32), axis=0)
    norms = 1.0 / jnp.sqrt(windows * (bounds[1:] - bounds[:-1]).astype(jnp.float32))
    power, norms = after(power, norms)

    twos = {k: lax.ppermute(early[k], "ch", ahead) for k in range(RAW)}
    halo = lax.ppermute(edge, "fq", [(0, 1), (1, 0)])
    if LEFT_AFTER >= 0:
        twos[LEFT_AFTER], halo = after(twos[LEFT_AFTER], halo)
    left, *late = call(
        left_kernel,
        "left",
        (left_shape, *held[RAW:]),
        [vmem()] * 3,
        (vmem(),) * (1 + pieces - RAW),
        nbytes,
        nbytes,
        scratch_shapes=[pltpu.VMEM((width + 16, channels), jnp.float32)],
    )(own, power, halo)
    mine = early + late

    out_shape = jax.ShapeDtypeStruct((2, ROUNDS, band_width, channels, channels), jnp.float32)
    sum_shape = jax.ShapeDtypeStruct((2, 2, band_width, channels, channels), jnp.float32)
    near_shape = jax.ShapeDtypeStruct((2, band_width, channels, channels), jnp.float32)
    send_shape = jax.ShapeDtypeStruct((2, band_width, channels, channels), jnp.bfloat16)

    sets = [tuple(range(sum(SETS[:s]), sum(SETS[: s + 1]))) for s in range(len(SETS))]
    ones, onward = {}, {}

    def cross(jobs, befores=(), sent=None):
        operands = [bounds, norms, left, other]
        for kinds, these in jobs:
            for kind in kinds:
                operands += [(ones, twos)[kind][k] for k in these]
        operands += befores
        count = len({kind for kinds, _ in jobs for kind in kinds})
        products = sum(len(kinds) * SIZES[k] for kinds, these in jobs for k in these)
        return call(
            functools.partial(cross_kernel, jobs, not befores, sent),
            "cross",
            (sum_shape,) * count + (send_shape,) * (sent is not None),
            [smem(), smem()] + [vmem()] * (len(operands) - 2),
            (vmem(),) * (count + (sent is not None)),
            8 * products * width * channels * channels,
            0 * nbytes,
        )(*operands)

    left, twos[OTHER_AFTER] = after(left, twos[OTHER_AFTER])
    other = lax.ppermute(left, "ch", mate)
    near = call(
        near_kernel,
        "near",
        near_shape,
        [smem(), smem(), vmem(), vmem()],
        vmem(),
        1000,
        1000,
    )(bounds, norms, left, other)

    for k in range(pieces):
        if k == NEAR_BEFORE:
            twos[k], near = after(twos[k], near)
        if k == CROSS_BEFORE:
            one_sum, two_sum = cross((((0, 1), sets[0]),))
            twos[k], one_sum = after(twos[k], one_sum)
        if Y_AFTER[k] >= 0:
            twos[k], ones[Y_AFTER[k]] = after(twos[k], ones[Y_AFTER[k]])
        if CHAIN and k > 0:
            twos[k], onward[k - 1] = after(twos[k], onward[k - 1])
        for later in range(pieces):
            if Z_AFTER[later] == k:
                twos[k], mine[later] = after(twos[k], mine[later])
                twos[later] = lax.ppermute(mine[later], "ch", ahead)
        onward[k] = jnp.where(odd_chip, twos[k], mine[k])
        if k < pieces - 1:
            ones[k] = lax.ppermute(onward[k], "ch", beside)
    final = pieces - 1
    middle = sets[1][0]
    onward[final], twos[middle] = after(onward[final], twos[middle])
    if NEAR_BEFORE == pieces:
        twos[middle], near = after(twos[middle], near)
    if LAST_TIE:
        ones[final - 1], twos[middle] = after(ones[final - 1], twos[middle])

    def put(kind, out, *values):
        aliased = out is not None
        operands = [*values, out] if aliased else list(values)
        return call(
            functools.partial(put_kernel, kind),
            "put",
            out_shape,
            [vmem()] * len(values) + [hbm()] * aliased,
            hbm(),
            1000,
            4 * nbytes,
            input_output_aliases={len(values): 0} if aliased else {},
            scratch_shapes=[
                pltpu.VMEM(near_shape.shape, jnp.float32),
                pltpu.SemaphoreType.DMA((2, band_width)),
            ],
        )(*operands)

    ones[final] = lax.ppermute(onward[final], "ch", beside)
    one_sum, two_sum, two_sent = cross(
        (((0,), sets[1]), ((1,), sets[1] + sets[2])), (one_sum, two_sum), 1
    )
    two_got = lax.ppermute(two_sent, "ch", mate)
    out = put("two", None, two_sum)
    if PUT_TIE:
        one_sum, out = after(one_sum, out)
    one_sum, one_sent = cross((((0,), sets[2]),), (one_sum,), 0)
    one_got = lax.ppermute(one_sent, "ch", mate)
    out = put("one", out, one_sum)
    out = put("near", out, two_got, near)
    return put("far", out, one_got)


def solution(mesh):
    placed = (P(None, None, "fq", "ch"), P("fq"))
    return jax.shard_map(
        shards,
        mesh=mesh,
        in_specs=placed,
        out_specs=P(None, None, "fq", "ch", None),
        check_vma=False,
    )
```

```python
import functools

import jax
import jax.numpy as jnp
from jax import lax
from jax.experimental import pallas as pl
from jax.experimental.pallas import tpu as pltpu
from jax.sharding import PartitionSpec as P

BANDS = 8
ROUNDS = 4
SMOOTH = 4
EPS = 1e-06

GROUP = 16
SIZES = (4,8,12,12,12,12,12,12,12)
BLOCK = 24
RAW = 3
TERMS = 3
Z_AFTER = (-1, -1, -1, 0, 2, 2, 3, 5, 6)
Z_BEHIND = (0,0,0,0,0,0,0,1,0)
Y_AFTER = (-1, -1, 0, 1, 2, 3, 4, 5, 6)
LAST_TIE = 0
PUT_TIE = 1
CHAIN = 0
SETS = (5, 2, 2)
LEFT_AFTER = -1
OTHER_AFTER = 0
NEAR_BEFORE = 8
CROSS_BEFORE = 7
VMEM_LIMIT = 10 * 1024 * 1024


def vmem():
    return pl.BlockSpec(memory_space=pltpu.VMEM)


def smem():
    return pl.BlockSpec(memory_space=pltpu.SMEM)


def hbm():
    return pl.BlockSpec(memory_space=pltpu.HBM)


def call(kernel, name, out_shape, in_specs, out_specs, flops, moved, **more):
    return pl.pallas_call(
        kernel,
        out_shape=out_shape,
        in_specs=in_specs,
        out_specs=out_specs,
        compiler_params=pltpu.CompilerParams(vmem_limit_bytes=VMEM_LIMIT),
        cost_estimate=pl.CostEstimate(flops=flops, bytes_accessed=moved, transcendentals=0),
        name=name,
        **more,
    )


def power_kernel(x_ref, power_ref, edge_ref, *pieces):
    rows, width, _ = x_ref.shape
    for index, piece in enumerate(pieces):
        piece[...] = x_ref[sum(SIZES[:index]) : sum(SIZES[: index + 1])]

    def step(i, total):
        value = x_ref[i].astype(jnp.float32)
        return total + value * value

    total = lax.fori_loop(0, rows, step, jnp.zeros(power_ref.shape, jnp.float32), unroll=8)
    power = total / (rows // 2)
    power_ref[...] = power
    low = lax.axis_index("fq") == 0
    edge_ref[...] = jnp.where(low, power[width - SMOOTH :], power[:SMOOTH])


def left_kernel(x_ref, power_ref, halo_ref, left_ref, *refs):
    whites, padded = refs[:-1], refs[-1]
    rows = x_ref.shape[0]
    fq = lax.axis_index("fq")
    width, channels = power_ref.shape
    bin_total = width * lax.axis_size("fq")
    padded[...] = jnp.zeros_like(padded)
    padded[8 : 8 + width, :] = power_ref[...]

    @pl.when(fq > 0)
    def _():
        padded[8 - SMOOTH : 8, :] = halo_ref[...]

    @pl.when(fq == 0)
    def _():
        padded[8 + width : 8 + width + SMOOTH, :] = halo_ref[...]

    total = padded[8 - SMOOTH : 8 - SMOOTH + width, :]
    for offset in range(1, 2 * SMOOTH + 1):
        total = total + padded[8 - SMOOTH + offset : 8 - SMOOTH + offset + width, :]
    bins = fq * width + lax.broadcasted_iota(jnp.int32, (width, channels), 0)
    counts = jnp.minimum(bins + SMOOTH, bin_total - 1) - jnp.maximum(bins - SMOOTH, 0) + 1
    scale = lax.rsqrt(total / counts.astype(jnp.float32) + EPS)
    rest = scale
    for term in range(TERMS):
        part = rest.astype(jnp.bfloat16)
        whites[0][SIZES[RAW] + term] = part
        rest = rest - part.astype(jnp.float32)

    span = BLOCK * GROUP
    for block in range(rows // BLOCK):
        first = block * BLOCK
        for group in range(width // GROUP):
            here = slice(group * GROUP, (group + 1) * GROUP)
            raw = x_ref[first : first + BLOCK, here, :].astype(jnp.float32)
            white = (raw * scale[here][None]).astype(jnp.bfloat16)
            for index, piece in enumerate(whites):
                start = sum(SIZES[: RAW + index])
                low, high = max(start, first), min(start + SIZES[RAW + index], first + BLOCK)
                if low < high:
                    piece[low - start : high - start, here, :] = white[low - first : high - first]
            turned = white.reshape(span, channels).T
            left_ref[group, :, block * span : (block + 1) * span] = turned


def band_at(bounds_ref, bands, bin_index):
    return sum((bounds_ref[k] <= bin_index).astype(jnp.int32) for k in range(1, bands))


def each_band(bounds_ref, groups, bands, add):
    for group in range(groups):
        band = band_at(bounds_ref, bands, group * GROUP)
        add(group, band, bounds_ref[band], bounds_ref[band + 1])
    for band in range(1, bands):
        low = bounds_ref[band]
        high = jnp.where(low % GROUP == 0, low, bounds_ref[band + 1])
        add(jnp.minimum(low // GROUP, groups - 1), band, low, high)


def inside(group, low, high, shape, dimension):
    bins = group * GROUP + lax.broadcasted_iota(jnp.int32, shape, dimension) % GROUP
    return ((bins >= low) & (bins < high)).astype(jnp.float32).astype(jnp.bfloat16)


def near_kernel(bounds_ref, norm_ref, own_ref, mate_ref, out_ref):
    groups, channels, span = own_ref.shape
    half = span // 2
    bands = out_ref.shape[1]
    out_ref[...] = jnp.zeros_like(out_ref)

    def add(group, band, low, high):
        right = mate_ref[group] * inside(group, low, high, (1, span), 1)
        halves = []
        for start in (0, half):
            left = jnp.concatenate(
                [own_ref[group, :, begin : begin + half] for begin in (start, half - start)], axis=0
            )
            halves.append(
                lax.dot_general(
                    left,
                    right[:, start : start + half],
                    (((1,), (1,)), ((), ())),
                    preferred_element_type=jnp.float32,
                )
            )
        out_ref[0, band] += (halves[0][:channels] + halves[1][:channels]) * norm_ref[band]
        out_ref[1, band] += (halves[0][channels:] - halves[1][channels:]) * norm_ref[band]

    @pl.when(lax.axis_index("ch") % 2 == 1)
    def _():
        each_band(bounds_ref, groups, bands, add)


def cross_kernel(jobs, first, sent, bounds_ref, norm_ref, own_ref, mate_ref, *refs):
    present = sorted({kind for kinds, _ in jobs for kind in kinds})
    work = []
    for kinds, these in jobs:
        taken = []
        for _ in kinds:
            taken.append(refs[: len(these)])
            refs = refs[len(these) :]
        work.append((kinds, these, taken))
    if not first:
        befores, refs = refs[: len(present)], refs[len(present) :]
    sums = dict(zip(present, refs))
    width, channels = work[0][2][0][0].shape[1:]
    bands = refs[0].shape[2]
    half = own_ref.shape[2] // 2
    for index, kind in enumerate(present):
        sums[kind][...] = jnp.zeros_like(refs[0]) if first else befores[index][...]

    def column(right, these, here, held):
        scale = None
        if first:
            for term in range(TERMS):
                part = right[RAW][SIZES[RAW] + term, here, :].astype(jnp.float32)
                scale = part if scale is None else scale + part
        blocks = []
        for ref, number in zip(right, these):
            size = SIZES[number]
            block = ref[:size, here, :]
            if number < RAW:
                block = (block.astype(jnp.float32) * scale[None]).astype(jnp.bfloat16)
            blocks.append((block * held[None]).reshape(size * GROUP, channels))
        return jnp.concatenate(blocks, axis=0)

    def multiply(kinds, these, taken, owners):
        start, stop = sum(SIZES[: these[0]]) * GROUP, sum(SIZES[: these[-1] + 1]) * GROUP
        turned = start >= half
        shift = -half if turned else half
        parts = slice(start, stop), slice(start + shift, stop + shift)

        def add(group, band, low, high):
            begin = group * GROUP
            here = pl.ds(begin if isinstance(group, int) else pl.multiple_of(begin, GROUP), GROUP)
            held = inside(group, low, high, (GROUP, channels), 0)
            left = jnp.concatenate(
                [ref[group, :, part] for ref in (own_ref, mate_ref)[:owners] for part in parts], axis=0
            )
            right = jnp.concatenate([column(right, these, here, held) for right in taken], axis=1)
            product = jnp.dot(left, right, preferred_element_type=jnp.float32) * norm_ref[band]
            for k, kind in enumerate(kinds):
                for owner in range(owners):
                    for part in range(2):
                        row = (2 * owner + part) * channels
                        term = product[row : row + channels, k * channels : (k + 1) * channels]
                        sums[kind][part, owner, band] += -term if part and turned else term

        each_band(bounds_ref, width // GROUP, bands, add)

    core = lax.axis_index("ch") % 2
    for kinds, these, taken in work:
        if kinds == (1,):
            pl.when(core == 0)(functools.partial(multiply, kinds, these, taken, 1))
            pl.when(core == 1)(functools.partial(multiply, kinds, these, taken, 2))
        else:
            multiply(kinds, these, taken, 2)
    if sent is not None:
        refs[-1][...] = sums[sent][:, 1].astype(jnp.bfloat16)


def put_kernel(kind, *refs):
    value_ref, refs = refs[0], refs[1:]
    core = lax.axis_index("ch") % 2
    if kind == "near":
        near_ref, refs = refs[0], refs[1:]
    out_ref, wide, sems = refs[-3:]
    turn = {"one": 1, "two": 3, "far": 2 * core, "near": 2 - 2 * core}[kind]
    copies = []
    for part in range(2):
        for band in range(out_ref.shape[2]):
            if kind in ("one", "two"):
                source = value_ref.at[part, 0, band]
            else:
                value = value_ref[part, band].astype(jnp.float32)
                if kind == "near":
                    value = jnp.where(core == 0, value, near_ref[part, band])
                wide[part, band] = value
                source = wide.at[part, band]
            copies.append(
                pltpu.make_async_copy(source, out_ref.at[part, turn, band], sems.at[part, band])
            )
            copies[-1].start()
    for copy in copies:
        copy.wait()


def after(value, other):
    return lax.optimization_barrier((value, other))


def shards(spectra, band_ids):
    parts, windows, width, channels = spectra.shape
    rows = parts * windows
    count = lax.axis_size("ch")
    fq_count = lax.axis_size("fq")
    index = lax.axis_index("ch")
    fq = lax.axis_index("fq")
    even_core = index % 2 == 0
    odd_chip = (index // 2) % 2 == 1

    ahead = [(i, (i + 4) % count) for i in range(count)]
    beside = [(i, i ^ 2) for i in range(count)]
    mate = [(i, i ^ 1) for i in range(count)]

    own = spectra.reshape(rows, width, channels)
    pieces = len(SIZES)
    heights = [size + (TERMS if k == RAW else 0) for k, size in enumerate(SIZES)]
    block = jax.ShapeDtypeStruct((width, channels), jnp.float32)
    edge = jax.ShapeDtypeStruct((SMOOTH, channels), jnp.float32)
    held = [jax.ShapeDtypeStruct((h, width, channels), jnp.bfloat16) for h in heights]
    groups = width // GROUP
    left_shape = jax.ShapeDtypeStruct((groups, channels, rows * GROUP), jnp.bfloat16)
    nbytes = rows * width * channels * 2

    power, edge, *early = call(
        power_kernel,
        "power",
        (block, edge, *held[:RAW]),
        [vmem()],
        (vmem(),) * (2 + RAW),
        nbytes,
        nbytes,
    )(own)
    band_width = BANDS // fq_count
    local_band = band_ids - fq * band_width
    below = local_band[:, None] < jnp.arange(band_width + 1, dtype=jnp.int32)[None, :]
    bounds = jnp.sum(below.astype(jnp.int32), axis=0)
    norms = 1.0 / jnp.sqrt(windows * (bounds[1:] - bounds[:-1]).astype(jnp.float32))
    power, norms = after(power, norms)

    twos = {k: lax.ppermute(early[k], "ch", ahead) for k in range(RAW)}
    halo = lax.ppermute(edge, "fq", [(0, 1), (1, 0)])
    if LEFT_AFTER >= 0:
        twos[LEFT_AFTER], halo = after(twos[LEFT_AFTER], halo)
    left, *late = call(
        left_kernel,
        "left",
        (left_shape, *held[RAW:]),
        [vmem()] * 3,
        (vmem(),) * (1 + pieces - RAW),
        nbytes,
        nbytes,
        scratch_shapes=[pltpu.VMEM((width + 16, channels), jnp.float32)],
    )(own, power, halo)
    mine = early + late

    out_shape = jax.ShapeDtypeStruct((2, ROUNDS, band_width, channels, channels), jnp.float32)
    sum_shape = jax.ShapeDtypeStruct((2, 2, band_width, channels, channels), jnp.float32)
    near_shape = jax.ShapeDtypeStruct((2, band_width, channels, channels), jnp.float32)
    send_shape = jax.ShapeDtypeStruct((2, band_width, channels, channels), jnp.bfloat16)

    sets = [tuple(range(sum(SETS[:s]), sum(SETS[: s + 1]))) for s in range(len(SETS))]
    ones, onward = {}, {}

    def cross(jobs, befores=(), sent=None):
        operands = [bounds, norms, left, other]
        for kinds, these in jobs:
            for kind in kinds:
                operands += [(ones, twos)[kind][k] for k in these]
        operands += befores
        count = len({kind for kinds, _ in jobs for kind in kinds})
        products = sum(len(kinds) * SIZES[k] for kinds, these in jobs for k in these)
        return call(
            functools.partial(cross_kernel, jobs, not befores, sent),
            "cross",
            (sum_shape,) * count + (send_shape,) * (sent is not None),
            [smem(), smem()] + [vmem()] * (len(operands) - 2),
            (vmem(),) * (count + (sent is not None)),
            8 * products * width * channels * channels,
            0 * nbytes,
        )(*operands)

    left, twos[OTHER_AFTER] = after(left, twos[OTHER_AFTER])
    other = lax.ppermute(left, "ch", mate)
    near = call(
        near_kernel,
        "near",
        near_shape,
        [smem(), smem(), vmem(), vmem()],
        vmem(),
        1000,
        1000,
    )(bounds, norms, left, other)

    for k in range(pieces):
        if k == NEAR_BEFORE:
            twos[k], near = after(twos[k], near)
        if k == CROSS_BEFORE:
            one_sum, two_sum = cross((((0, 1), sets[0]),))
            twos[k], one_sum = after(twos[k], one_sum)
        if Y_AFTER[k] >= 0:
            twos[k], ones[Y_AFTER[k]] = after(twos[k], ones[Y_AFTER[k]])
        if CHAIN and k > 0:
            twos[k], onward[k - 1] = after(twos[k], onward[k - 1])
        for later in range(pieces):
            if Z_AFTER[later] == k and not Z_BEHIND[later]:
                twos[k], mine[later] = after(twos[k], mine[later])
                twos[later] = lax.ppermute(mine[later], "ch", ahead)
        onward[k] = jnp.where(odd_chip, twos[k], mine[k])
        for later in range(pieces):
            if Z_AFTER[later] == k and Z_BEHIND[later]:
                onward[k], mine[later] = after(onward[k], mine[later])
                twos[later] = lax.ppermute(mine[later], "ch", ahead)
        if k < pieces - 1:
            ones[k] = lax.ppermute(onward[k], "ch", beside)
    final = pieces - 1
    middle = sets[1][0]
    onward[final], twos[middle] = after(onward[final], twos[middle])
    if NEAR_BEFORE == pieces:
        twos[middle], near = after(twos[middle], near)
    if LAST_TIE:
        ones[final - 1], twos[middle] = after(ones[final - 1], twos[middle])

    def put(kind, out, *values):
        aliased = out is not None
        operands = [*values, out] if aliased else list(values)
        return call(
            functools.partial(put_kernel, kind),
            "put",
            out_shape,
            [vmem()] * len(values) + [hbm()] * aliased,
            hbm(),
            1000,
            4 * nbytes,
            input_output_aliases={len(values): 0} if aliased else {},
            scratch_shapes=[
                pltpu.VMEM(near_shape.shape, jnp.float32),
                pltpu.SemaphoreType.DMA((2, band_width)),
            ],
        )(*operands)

    ones[final] = lax.ppermute(onward[final], "ch", beside)
    one_sum, two_sum, two_sent = cross(
        (((0,), sets[1]), ((1,), sets[1] + sets[2])), (one_sum, two_sum), 1
    )
    two_got = lax.ppermute(two_sent, "ch", mate)
    out = put("two", None, two_sum)
    if PUT_TIE:
        one_sum, out = after(one_sum, out)
    one_sum, one_sent = cross((((0,), sets[2]),), (one_sum,), 0)
    one_got = lax.ppermute(one_sent, "ch", mate)
    out = put("one", out, one_sum)
    out = put("near", out, two_got, near)
    return put("far", out, one_got)


def solution(mesh):
    placed = (P(None, None, "fq", "ch"), P("fq"))
    return jax.shard_map(
        shards,
        mesh=mesh,
        in_specs=placed,
        out_specs=P(None, None, "fq", "ch", None),
        check_vma=False,
    )
```

```python
import functools

import jax
import jax.numpy as jnp
from jax import lax
from jax.experimental import pallas as pl
from jax.experimental.pallas import tpu as pltpu
from jax.sharding import PartitionSpec as P

BANDS = 8
ROUNDS = 4
SMOOTH = 4
EPS = 1e-06

GROUP = 16
SIZES = (4,8,12,12,12,12,12,12,12)
BLOCK = 24
RAW = 4
TERMS = 3
Z_AFTER = (-1, -1, -1, -1, 2, 2, 3, 5, 6)
Z_BEHIND = (0,0,0,0,0,0,0,1,0)
Y_AFTER = (-1, -1, 0, 1, 2, 3, 4, 5, 6)
LAST_TIE = 0
PUT_TIE = 1
CHAIN = 0
SETS = (5, 2, 2)
EDGE_AFTER = 0
LEFT_AFTER = -1
OTHER_AFTER = 0
NEAR_BEFORE = 8
CROSS_BEFORE = 7
VMEM_LIMIT = 10 * 1024 * 1024


def vmem():
    return pl.BlockSpec(memory_space=pltpu.VMEM)


def smem():
    return pl.BlockSpec(memory_space=pltpu.SMEM)


def hbm():
    return pl.BlockSpec(memory_space=pltpu.HBM)


def call(kernel, name, out_shape, in_specs, out_specs, flops, moved, **more):
    return pl.pallas_call(
        kernel,
        out_shape=out_shape,
        in_specs=in_specs,
        out_specs=out_specs,
        compiler_params=pltpu.CompilerParams(vmem_limit_bytes=VMEM_LIMIT),
        cost_estimate=pl.CostEstimate(flops=flops, bytes_accessed=moved, transcendentals=0),
        name=name,
        **more,
    )


def power_kernel(x_ref, power_ref, edge_ref, *pieces):
    rows, width, _ = x_ref.shape
    for index, piece in enumerate(pieces):
        piece[...] = x_ref[sum(SIZES[:index]) : sum(SIZES[: index + 1])]

    def step(i, total):
        value = x_ref[i].astype(jnp.float32)
        return total + value * value

    total = lax.fori_loop(0, rows, step, jnp.zeros(power_ref.shape, jnp.float32), unroll=8)
    power = total / (rows // 2)
    power_ref[...] = power
    low = lax.axis_index("fq") == 0
    edge_ref[...] = jnp.where(low, power[width - SMOOTH :], power[:SMOOTH])


def left_kernel(x_ref, power_ref, halo_ref, left_ref, *refs):
    whites, padded = refs[:-1], refs[-1]
    rows = x_ref.shape[0]
    fq = lax.axis_index("fq")
    width, channels = power_ref.shape
    bin_total = width * lax.axis_size("fq")
    padded[...] = jnp.zeros_like(padded)
    padded[8 : 8 + width, :] = power_ref[...]

    @pl.when(fq > 0)
    def _():
        padded[8 - SMOOTH : 8, :] = halo_ref[...]

    @pl.when(fq == 0)
    def _():
        padded[8 + width : 8 + width + SMOOTH, :] = halo_ref[...]

    total = padded[8 - SMOOTH : 8 - SMOOTH + width, :]
    for offset in range(1, 2 * SMOOTH + 1):
        total = total + padded[8 - SMOOTH + offset : 8 - SMOOTH + offset + width, :]
    bins = fq * width + lax.broadcasted_iota(jnp.int32, (width, channels), 0)
    counts = jnp.minimum(bins + SMOOTH, bin_total - 1) - jnp.maximum(bins - SMOOTH, 0) + 1
    scale = lax.rsqrt(total / counts.astype(jnp.float32) + EPS)
    rest = scale
    for term in range(TERMS):
        part = rest.astype(jnp.bfloat16)
        whites[0][SIZES[RAW] + term] = part
        rest = rest - part.astype(jnp.float32)

    span = BLOCK * GROUP
    for block in range(rows // BLOCK):
        first = block * BLOCK
        for group in range(width // GROUP):
            here = slice(group * GROUP, (group + 1) * GROUP)
            raw = x_ref[first : first + BLOCK, here, :].astype(jnp.float32)
            white = (raw * scale[here][None]).astype(jnp.bfloat16)
            for index, piece in enumerate(whites):
                start = sum(SIZES[: RAW + index])
                low, high = max(start, first), min(start + SIZES[RAW + index], first + BLOCK)
                if low < high:
                    piece[low - start : high - start, here, :] = white[low - first : high - first]
            turned = white.reshape(span, channels).T
            left_ref[group, :, block * span : (block + 1) * span] = turned


def band_at(bounds_ref, bands, bin_index):
    return sum((bounds_ref[k] <= bin_index).astype(jnp.int32) for k in range(1, bands))


def each_band(bounds_ref, groups, bands, add):
    for group in range(groups):
        band = band_at(bounds_ref, bands, group * GROUP)
        add(group, band, bounds_ref[band], bounds_ref[band + 1])
    for band in range(1, bands):
        low = bounds_ref[band]
        high = jnp.where(low % GROUP == 0, low, bounds_ref[band + 1])
        add(jnp.minimum(low // GROUP, groups - 1), band, low, high)


def inside(group, low, high, shape, dimension):
    bins = group * GROUP + lax.broadcasted_iota(jnp.int32, shape, dimension) % GROUP
    return ((bins >= low) & (bins < high)).astype(jnp.float32).astype(jnp.bfloat16)


def near_kernel(bounds_ref, norm_ref, own_ref, mate_ref, out_ref):
    groups, channels, span = own_ref.shape
    half = span // 2
    bands = out_ref.shape[1]
    out_ref[...] = jnp.zeros_like(out_ref)

    def add(group, band, low, high):
        right = mate_ref[group] * inside(group, low, high, (1, span), 1)
        halves = []
        for start in (0, half):
            left = jnp.concatenate(
                [own_ref[group, :, begin : begin + half] for begin in (start, half - start)], axis=0
            )
            halves.append(
                lax.dot_general(
                    left,
                    right[:, start : start + half],
                    (((1,), (1,)), ((), ())),
                    preferred_element_type=jnp.float32,
                )
            )
        out_ref[0, band] += (halves[0][:channels] + halves[1][:channels]) * norm_ref[band]
        out_ref[1, band] += (halves[0][channels:] - halves[1][channels:]) * norm_ref[band]

    @pl.when(lax.axis_index("ch") % 2 == 1)
    def _():
        each_band(bounds_ref, groups, bands, add)


def cross_kernel(jobs, first, sent, bounds_ref, norm_ref, own_ref, mate_ref, *refs):
    present = sorted({kind for kinds, _ in jobs for kind in kinds})
    work = []
    for kinds, these in jobs:
        taken = []
        for _ in kinds:
            taken.append(refs[: len(these)])
            refs = refs[len(these) :]
        work.append((kinds, these, taken))
    if not first:
        befores, refs = refs[: len(present)], refs[len(present) :]
    sums = dict(zip(present, refs))
    width, channels = work[0][2][0][0].shape[1:]
    bands = refs[0].shape[2]
    half = own_ref.shape[2] // 2
    for index, kind in enumerate(present):
        sums[kind][...] = jnp.zeros_like(refs[0]) if first else befores[index][...]

    def column(right, these, here, held):
        scale = None
        if first:
            for term in range(TERMS):
                part = right[RAW][SIZES[RAW] + term, here, :].astype(jnp.float32)
                scale = part if scale is None else scale + part
        blocks = []
        for ref, number in zip(right, these):
            size = SIZES[number]
            block = ref[:size, here, :]
            if number < RAW:
                block = (block.astype(jnp.float32) * scale[None]).astype(jnp.bfloat16)
            blocks.append((block * held[None]).reshape(size * GROUP, channels))
        return jnp.concatenate(blocks, axis=0)

    def multiply(kinds, these, taken, owners):
        start, stop = sum(SIZES[: these[0]]) * GROUP, sum(SIZES[: these[-1] + 1]) * GROUP
        turned = start >= half
        shift = -half if turned else half
        parts = slice(start, stop), slice(start + shift, stop + shift)

        def add(group, band, low, high):
            begin = group * GROUP
            here = pl.ds(begin if isinstance(group, int) else pl.multiple_of(begin, GROUP), GROUP)
            held = inside(group, low, high, (GROUP, channels), 0)
            left = jnp.concatenate(
                [ref[group, :, part] for ref in (own_ref, mate_ref)[:owners] for part in parts], axis=0
            )
            right = jnp.concatenate([column(right, these, here, held) for right in taken], axis=1)
            product = jnp.dot(left, right, preferred_element_type=jnp.float32) * norm_ref[band]
            for k, kind in enumerate(kinds):
                for owner in range(owners):
                    for part in range(2):
                        row = (2 * owner + part) * channels
                        term = product[row : row + channels, k * channels : (k + 1) * channels]
                        sums[kind][part, owner, band] += -term if part and turned else term

        each_band(bounds_ref, width // GROUP, bands, add)

    core = lax.axis_index("ch") % 2
    for kinds, these, taken in work:
        if kinds == (1,):
            pl.when(core == 0)(functools.partial(multiply, kinds, these, taken, 1))
            pl.when(core == 1)(functools.partial(multiply, kinds, these, taken, 2))
        else:
            multiply(kinds, these, taken, 2)
    if sent is not None:
        refs[-1][...] = sums[sent][:, 1].astype(jnp.bfloat16)


def put_kernel(kinds, *refs):
    out_ref, wide, sems = refs[-3:]
    core = lax.axis_index("ch") % 2
    turns = {"one": 1, "two": 3, "far": 2 * core, "near": 2 - 2 * core}
    copies = []
    for kind in kinds:
        value_ref, refs = refs[0], refs[1:]
        if kind == "near":
            near_ref, refs = refs[0], refs[1:]
        for part in range(2):
            for band in range(out_ref.shape[2]):
                if kind in ("one", "two"):
                    source = value_ref.at[part, 0, band]
                else:
                    value = value_ref[part, band].astype(jnp.float32)
                    if kind == "near":
                        value = jnp.where(core == 0, value, near_ref[part, band])
                    wide[part, band] = value
                    source = wide.at[part, band]
                turn = turns[kind]
                sem = sems.at[kinds.index(kind), part, band]
                copies.append(pltpu.make_async_copy(source, out_ref.at[part, turn, band], sem))
                copies[-1].start()
    for copy in copies:
        copy.wait()


def after(value, other):
    return lax.optimization_barrier((value, other))


def shards(spectra, band_ids):
    parts, windows, width, channels = spectra.shape
    rows = parts * windows
    count = lax.axis_size("ch")
    fq_count = lax.axis_size("fq")
    index = lax.axis_index("ch")
    fq = lax.axis_index("fq")
    even_core = index % 2 == 0
    odd_chip = (index // 2) % 2 == 1

    ahead = [(i, (i + 4) % count) for i in range(count)]
    beside = [(i, i ^ 2) for i in range(count)]
    mate = [(i, i ^ 1) for i in range(count)]

    own = spectra.reshape(rows, width, channels)
    pieces = len(SIZES)
    heights = [size + (TERMS if k == RAW else 0) for k, size in enumerate(SIZES)]
    block = jax.ShapeDtypeStruct((width, channels), jnp.float32)
    edge = jax.ShapeDtypeStruct((SMOOTH, channels), jnp.float32)
    held = [jax.ShapeDtypeStruct((h, width, channels), jnp.bfloat16) for h in heights]
    groups = width // GROUP
    left_shape = jax.ShapeDtypeStruct((groups, channels, rows * GROUP), jnp.bfloat16)
    nbytes = rows * width * channels * 2

    power, edge, *early = call(
        power_kernel,
        "power",
        (block, edge, *held[:RAW]),
        [vmem()],
        (vmem(),) * (2 + RAW),
        nbytes,
        nbytes,
    )(own)
    band_width = BANDS // fq_count
    local_band = band_ids - fq * band_width
    below = local_band[:, None] < jnp.arange(band_width + 1, dtype=jnp.int32)[None, :]
    bounds = jnp.sum(below.astype(jnp.int32), axis=0)
    norms = 1.0 / jnp.sqrt(windows * (bounds[1:] - bounds[:-1]).astype(jnp.float32))
    power, norms = after(power, norms)

    twos = {k: lax.ppermute(early[k], "ch", ahead) for k in range(RAW)}
    if EDGE_AFTER >= 0:
        twos[EDGE_AFTER], edge = after(twos[EDGE_AFTER], edge)
    halo = lax.ppermute(edge, "fq", [(0, 1), (1, 0)])
    if LEFT_AFTER >= 0:
        twos[LEFT_AFTER], halo = after(twos[LEFT_AFTER], halo)
    left, *late = call(
        left_kernel,
        "left",
        (left_shape, *held[RAW:]),
        [vmem()] * 3,
        (vmem(),) * (1 + pieces - RAW),
        nbytes,
        nbytes,
        scratch_shapes=[pltpu.VMEM((width + 16, channels), jnp.float32)],
    )(own, power, halo)
    mine = early + late

    out_shape = jax.ShapeDtypeStruct((2, ROUNDS, band_width, channels, channels), jnp.float32)
    sum_shape = jax.ShapeDtypeStruct((2, 2, band_width, channels, channels), jnp.float32)
    near_shape = jax.ShapeDtypeStruct((2, band_width, channels, channels), jnp.float32)
    send_shape = jax.ShapeDtypeStruct((2, band_width, channels, channels), jnp.bfloat16)

    sets = [tuple(range(sum(SETS[:s]), sum(SETS[: s + 1]))) for s in range(len(SETS))]
    ones, onward = {}, {}

    def cross(jobs, befores=(), sent=None):
        operands = [bounds, norms, left, other]
        for kinds, these in jobs:
            for kind in kinds:
                operands += [(ones, twos)[kind][k] for k in these]
        operands += befores
        count = len({kind for kinds, _ in jobs for kind in kinds})
        products = sum(len(kinds) * SIZES[k] for kinds, these in jobs for k in these)
        return call(
            functools.partial(cross_kernel, jobs, not befores, sent),
            "cross",
            (sum_shape,) * count + (send_shape,) * (sent is not None),
            [smem(), smem()] + [vmem()] * (len(operands) - 2),
            (vmem(),) * (count + (sent is not None)),
            8 * products * width * channels * channels,
            0 * nbytes,
        )(*operands)

    left, twos[OTHER_AFTER] = after(left, twos[OTHER_AFTER])
    other = lax.ppermute(left, "ch", mate)
    near = call(
        near_kernel,
        "near",
        near_shape,
        [smem(), smem(), vmem(), vmem()],
        vmem(),
        1000,
        1000,
    )(bounds, norms, left, other)

    for k in range(pieces):
        if k == NEAR_BEFORE:
            twos[k], near = after(twos[k], near)
        if k == CROSS_BEFORE:
            one_sum, two_sum = cross((((0, 1), sets[0]),))
            twos[k], one_sum = after(twos[k], one_sum)
        if Y_AFTER[k] >= 0:
            twos[k], ones[Y_AFTER[k]] = after(twos[k], ones[Y_AFTER[k]])
        if CHAIN and k > 0:
            twos[k], onward[k - 1] = after(twos[k], onward[k - 1])
        for later in range(pieces):
            if Z_AFTER[later] == k and not Z_BEHIND[later]:
                twos[k], mine[later] = after(twos[k], mine[later])
                twos[later] = lax.ppermute(mine[later], "ch", ahead)
        onward[k] = jnp.where(odd_chip, twos[k], mine[k])
        for later in range(pieces):
            if Z_AFTER[later] == k and Z_BEHIND[later]:
                onward[k], mine[later] = after(onward[k], mine[later])
                twos[later] = lax.ppermute(mine[later], "ch", ahead)
        if k < pieces - 1:
            ones[k] = lax.ppermute(onward[k], "ch", beside)
    final = pieces - 1
    middle = sets[1][0]
    onward[final], twos[middle] = after(onward[final], twos[middle])
    if NEAR_BEFORE == pieces:
        twos[middle], near = after(twos[middle], near)
    if LAST_TIE:
        ones[final - 1], twos[middle] = after(ones[final - 1], twos[middle])

    def put(kinds, out, *values):
        aliased = out is not None
        operands = [*values, out] if aliased else list(values)
        return call(
            functools.partial(put_kernel, kinds),
            "put",
            out_shape,
            [vmem()] * len(values) + [hbm()] * aliased,
            hbm(),
            1000,
            4 * nbytes,
            input_output_aliases={len(values): 0} if aliased else {},
            scratch_shapes=[
                pltpu.VMEM(near_shape.shape, jnp.float32),
                pltpu.SemaphoreType.DMA((len(kinds), 2, band_width)),
            ],
        )(*operands)

    ones[final] = lax.ppermute(onward[final], "ch", beside)
    one_sum, two_sum, two_sent = cross(
        (((0,), sets[1]), ((1,), sets[1] + sets[2])), (one_sum, two_sum), 1
    )
    two_got = lax.ppermute(two_sent, "ch", mate)
    out = put(("two",), None, two_sum)
    if PUT_TIE:
        one_sum, out = after(one_sum, out)
    one_sum, one_sent = cross((((0,), sets[2]),), (one_sum,), 0)
    one_got = lax.ppermute(one_sent, "ch", mate)
    out = put(("one", "near"), out, one_sum, two_got, near)
    return put(("far",), out, one_got)


def solution(mesh):
    placed = (P(None, None, "fq", "ch"), P("fq"))
    return jax.shard_map(
        shards,
        mesh=mesh,
        in_specs=placed,
        out_specs=P(None, None, "fq", "ch", None),
        check_vma=False,
    )
```

```python
import functools

import jax
import jax.numpy as jnp
from jax import lax
from jax.experimental import pallas as pl
from jax.experimental.pallas import tpu as pltpu
from jax.sharding import PartitionSpec as P

BANDS = 8
ROUNDS = 4
SMOOTH = 4
EPS = 1e-06

GROUP = 16
SIZES = (4,8,12,12,12,12,12,12,12)
BLOCK = 24
RAW = 3
TERMS = 3
Z_AFTER = (-1, -1, -1, 0, 2, 2, 3, 5, 6)
Z_BEHIND = (0,0,0,0,0,0,0,1,0)
Y_AFTER = (-1, -1, 0, 1, 2, 3, 4, 5, 6)
LAST_TIE = 0
PUT_TIE = 1
CHAIN = 0
SETS = (5, 2, 2)
EDGE_AFTER = -1
LEFT_AFTER = -1
OTHER_AFTER = 0
NEAR_BEFORE = 8
CROSS_BEFORE = 7
VMEM_LIMIT = 10 * 1024 * 1024


def vmem():
    return pl.BlockSpec(memory_space=pltpu.VMEM)


def smem():
    return pl.BlockSpec(memory_space=pltpu.SMEM)


def hbm():
    return pl.BlockSpec(memory_space=pltpu.HBM)


def call(kernel, name, out_shape, in_specs, out_specs, flops, moved, **more):
    return pl.pallas_call(
        kernel,
        out_shape=out_shape,
        in_specs=in_specs,
        out_specs=out_specs,
        compiler_params=pltpu.CompilerParams(vmem_limit_bytes=VMEM_LIMIT),
        cost_estimate=pl.CostEstimate(flops=flops, bytes_accessed=moved, transcendentals=0),
        name=name,
        **more,
    )


def power_kernel(x_ref, power_ref, edge_ref, *pieces):
    rows, width, _ = x_ref.shape
    for index, piece in enumerate(pieces):
        piece[...] = x_ref[sum(SIZES[:index]) : sum(SIZES[: index + 1])]

    def step(i, total):
        value = x_ref[i].astype(jnp.float32)
        return total + value * value

    total = lax.fori_loop(0, rows, step, jnp.zeros(power_ref.shape, jnp.float32), unroll=8)
    power = total / (rows // 2)
    power_ref[...] = power
    low = lax.axis_index("fq") == 0
    edge_ref[...] = jnp.where(low, power[width - SMOOTH :], power[:SMOOTH])


def left_kernel(x_ref, power_ref, halo_ref, left_ref, *refs):
    whites, padded = refs[:-1], refs[-1]
    rows = x_ref.shape[0]
    fq = lax.axis_index("fq")
    width, channels = power_ref.shape
    bin_total = width * lax.axis_size("fq")
    padded[...] = jnp.zeros_like(padded)
    padded[8 : 8 + width, :] = power_ref[...]

    @pl.when(fq > 0)
    def _():
        padded[8 - SMOOTH : 8, :] = halo_ref[...]

    @pl.when(fq == 0)
    def _():
        padded[8 + width : 8 + width + SMOOTH, :] = halo_ref[...]

    total = padded[8 - SMOOTH : 8 - SMOOTH + width, :]
    for offset in range(1, 2 * SMOOTH + 1):
        total = total + padded[8 - SMOOTH + offset : 8 - SMOOTH + offset + width, :]
    bins = fq * width + lax.broadcasted_iota(jnp.int32, (width, channels), 0)
    counts = jnp.minimum(bins + SMOOTH, bin_total - 1) - jnp.maximum(bins - SMOOTH, 0) + 1
    scale = lax.rsqrt(total / counts.astype(jnp.float32) + EPS)
    rest = scale
    for term in range(TERMS):
        part = rest.astype(jnp.bfloat16)
        whites[0][SIZES[RAW] + term] = part
        rest = rest - part.astype(jnp.float32)

    span = BLOCK * GROUP
    for block in range(rows // BLOCK):
        first = block * BLOCK
        for group in range(width // GROUP):
            here = slice(group * GROUP, (group + 1) * GROUP)
            raw = x_ref[first : first + BLOCK, here, :].astype(jnp.float32)
            white = (raw * scale[here][None]).astype(jnp.bfloat16)
            for index, piece in enumerate(whites):
                start = sum(SIZES[: RAW + index])
                low, high = max(start, first), min(start + SIZES[RAW + index], first + BLOCK)
                if low < high:
                    piece[low - start : high - start, here, :] = white[low - first : high - first]
            turned = white.reshape(span, channels).T
            left_ref[group, :, block * span : (block + 1) * span] = turned


def band_at(bounds_ref, bands, bin_index):
    return sum((bounds_ref[k] <= bin_index).astype(jnp.int32) for k in range(1, bands))


def each_band(bounds_ref, groups, bands, add):
    for group in range(groups):
        band = band_at(bounds_ref, bands, group * GROUP)
        add(group, band, bounds_ref[band], bounds_ref[band + 1])
    for band in range(1, bands):
        low = bounds_ref[band]
        high = jnp.where(low % GROUP == 0, low, bounds_ref[band + 1])
        add(jnp.minimum(low // GROUP, groups - 1), band, low, high)


def inside(group, low, high, shape, dimension):
    bins = group * GROUP + lax.broadcasted_iota(jnp.int32, shape, dimension) % GROUP
    return ((bins >= low) & (bins < high)).astype(jnp.float32).astype(jnp.bfloat16)


def near_kernel(bounds_ref, norm_ref, own_ref, mate_ref, out_ref):
    groups, channels, span = own_ref.shape
    half = span // 2
    bands = out_ref.shape[1]
    out_ref[...] = jnp.zeros_like(out_ref)

    def add(group, band, low, high):
        right = mate_ref[group] * inside(group, low, high, (1, span), 1)
        halves = []
        for start in (0, half):
            left = jnp.concatenate(
                [own_ref[group, :, begin : begin + half] for begin in (start, half - start)], axis=0
            )
            halves.append(
                lax.dot_general(
                    left,
                    right[:, start : start + half],
                    (((1,), (1,)), ((), ())),
                    preferred_element_type=jnp.float32,
                )
            )
        out_ref[0, band] += (halves[0][:channels] + halves[1][:channels]) * norm_ref[band]
        out_ref[1, band] += (halves[0][channels:] - halves[1][channels:]) * norm_ref[band]

    @pl.when(lax.axis_index("ch") % 2 == 1)
    def _():
        each_band(bounds_ref, groups, bands, add)


def cross_kernel(jobs, first, sent, bounds_ref, norm_ref, own_ref, mate_ref, *refs):
    present = sorted({kind for kinds, _ in jobs for kind in kinds})
    work = []
    for kinds, these in jobs:
        taken = []
        for _ in kinds:
            taken.append(refs[: len(these)])
            refs = refs[len(these) :]
        work.append((kinds, these, taken))
    if not first:
        befores, refs = refs[: len(present)], refs[len(present) :]
    sums = dict(zip(present, refs))
    width, channels = work[0][2][0][0].shape[1:]
    bands = refs[0].shape[2]
    half = own_ref.shape[2] // 2
    for index, kind in enumerate(present):
        sums[kind][...] = jnp.zeros_like(refs[0]) if first else befores[index][...]

    def column(right, these, here, held):
        scale = None
        if first:
            for term in range(TERMS):
                part = right[RAW][SIZES[RAW] + term, here, :].astype(jnp.float32)
                scale = part if scale is None else scale + part
        blocks = []
        for ref, number in zip(right, these):
            size = SIZES[number]
            block = ref[:size, here, :]
            if number < RAW:
                block = (block.astype(jnp.float32) * scale[None]).astype(jnp.bfloat16)
            blocks.append((block * held[None]).reshape(size * GROUP, channels))
        return jnp.concatenate(blocks, axis=0)

    def multiply(kinds, these, taken, owners):
        start, stop = sum(SIZES[: these[0]]) * GROUP, sum(SIZES[: these[-1] + 1]) * GROUP
        turned = start >= half
        shift = -half if turned else half
        parts = slice(start, stop), slice(start + shift, stop + shift)

        def add(group, band, low, high):
            begin = group * GROUP
            here = pl.ds(begin if isinstance(group, int) else pl.multiple_of(begin, GROUP), GROUP)
            held = inside(group, low, high, (GROUP, channels), 0)
            left = jnp.concatenate(
                [ref[group, :, part] for ref in (own_ref, mate_ref)[:owners] for part in parts], axis=0
            )
            right = jnp.concatenate([column(right, these, here, held) for right in taken], axis=1)
            product = jnp.dot(left, right, preferred_element_type=jnp.float32) * norm_ref[band]
            for k, kind in enumerate(kinds):
                for owner in range(owners):
                    for part in range(2):
                        row = (2 * owner + part) * channels
                        term = product[row : row + channels, k * channels : (k + 1) * channels]
                        sums[kind][part, owner, band] += -term if part and turned else term

        each_band(bounds_ref, width // GROUP, bands, add)

    core = lax.axis_index("ch") % 2
    for kinds, these, taken in work:
        if kinds == (1,):
            pl.when(core == 0)(functools.partial(multiply, kinds, these, taken, 1))
            pl.when(core == 1)(functools.partial(multiply, kinds, these, taken, 2))
        else:
            multiply(kinds, these, taken, 2)
    if sent is not None:
        refs[-1][...] = sums[sent][:, 1].astype(jnp.bfloat16)


def put_kernel(kinds, *refs):
    out_ref, wide, sems = refs[-3:]
    core = lax.axis_index("ch") % 2
    turns = {"one": 1, "two": 3, "far": 2 * core, "near": 2 - 2 * core}
    copies = []
    for kind in kinds:
        value_ref, refs = refs[0], refs[1:]
        if kind == "near":
            near_ref, refs = refs[0], refs[1:]
        for part in range(2):
            for band in range(out_ref.shape[2]):
                if kind in ("one", "two"):
                    source = value_ref.at[part, 0, band]
                else:
                    value = value_ref[part, band].astype(jnp.float32)
                    if kind == "near":
                        value = jnp.where(core == 0, value, near_ref[part, band])
                    wide[part, band] = value
                    source = wide.at[part, band]
                turn = turns[kind]
                sem = sems.at[kinds.index(kind), part, band]
                copies.append(pltpu.make_async_copy(source, out_ref.at[part, turn, band], sem))
                copies[-1].start()
    for copy in copies:
        copy.wait()


def after(value, other):
    return lax.optimization_barrier((value, other))


def shards(spectra, band_ids):
    parts, windows, width, channels = spectra.shape
    rows = parts * windows
    count = lax.axis_size("ch")
    fq_count = lax.axis_size("fq")
    index = lax.axis_index("ch")
    fq = lax.axis_index("fq")
    even_core = index % 2 == 0
    odd_chip = (index // 2) % 2 == 1

    ahead = [(i, (i + 4) % count) for i in range(count)]
    beside = [(i, i ^ 2) for i in range(count)]
    mate = [(i, i ^ 1) for i in range(count)]

    own = spectra.reshape(rows, width, channels)
    pieces = len(SIZES)
    heights = [size + (TERMS if k == RAW else 0) for k, size in enumerate(SIZES)]
    block = jax.ShapeDtypeStruct((width, channels), jnp.float32)
    edge = jax.ShapeDtypeStruct((SMOOTH, channels), jnp.float32)
    held = [jax.ShapeDtypeStruct((h, width, channels), jnp.bfloat16) for h in heights]
    groups = width // GROUP
    left_shape = jax.ShapeDtypeStruct((groups, channels, rows * GROUP), jnp.bfloat16)
    nbytes = rows * width * channels * 2

    power, edge, *early = call(
        power_kernel,
        "power",
        (block, edge, *held[:RAW]),
        [vmem()],
        (vmem(),) * (2 + RAW),
        nbytes,
        nbytes,
    )(own)
    band_width = BANDS // fq_count
    local_band = band_ids - fq * band_width
    below = local_band[:, None] < jnp.arange(band_width + 1, dtype=jnp.int32)[None, :]
    bounds = jnp.sum(below.astype(jnp.int32), axis=0)
    norms = 1.0 / jnp.sqrt(windows * (bounds[1:] - bounds[:-1]).astype(jnp.float32))
    power, norms = after(power, norms)

    twos = {k: lax.ppermute(early[k], "ch", ahead) for k in range(RAW)}
    if EDGE_AFTER >= 0:
        twos[EDGE_AFTER], edge = after(twos[EDGE_AFTER], edge)
    halo = lax.ppermute(edge, "fq", [(0, 1), (1, 0)])
    if LEFT_AFTER >= 0:
        twos[LEFT_AFTER], halo = after(twos[LEFT_AFTER], halo)
    left, *late = call(
        left_kernel,
        "left",
        (left_shape, *held[RAW:]),
        [vmem()] * 3,
        (vmem(),) * (1 + pieces - RAW),
        nbytes,
        nbytes,
        scratch_shapes=[pltpu.VMEM((width + 16, channels), jnp.float32)],
    )(own, power, halo)
    mine = early + late

    out_shape = jax.ShapeDtypeStruct((2, ROUNDS, band_width, channels, channels), jnp.float32)
    sum_shape = jax.ShapeDtypeStruct((2, 2, band_width, channels, channels), jnp.float32)
    near_shape = jax.ShapeDtypeStruct((2, band_width, channels, channels), jnp.float32)
    send_shape = jax.ShapeDtypeStruct((2, band_width, channels, channels), jnp.bfloat16)

    sets = [tuple(range(sum(SETS[:s]), sum(SETS[: s + 1]))) for s in range(len(SETS))]
    ones, onward = {}, {}

    def cross(jobs, befores=(), sent=None):
        operands = [bounds, norms, left, other]
        for kinds, these in jobs:
            for kind in kinds:
                operands += [(ones, twos)[kind][k] for k in these]
        operands += befores
        count = len({kind for kinds, _ in jobs for kind in kinds})
        products = sum(len(kinds) * SIZES[k] for kinds, these in jobs for k in these)
        return call(
            functools.partial(cross_kernel, jobs, not befores, sent),
            "cross",
            (sum_shape,) * count + (send_shape,) * (sent is not None),
            [smem(), smem()] + [vmem()] * (len(operands) - 2),
            (vmem(),) * (count + (sent is not None)),
            8 * products * width * channels * channels,
            0 * nbytes,
        )(*operands)

    left, twos[OTHER_AFTER] = after(left, twos[OTHER_AFTER])
    other = lax.ppermute(left, "ch", mate)
    near = call(
        near_kernel,
        "near",
        near_shape,
        [smem(), smem(), vmem(), vmem()],
        vmem(),
        1000,
        1000,
    )(bounds, norms, left, other)

    for k in range(pieces):
        if k == NEAR_BEFORE:
            twos[k], near = after(twos[k], near)
        if k == CROSS_BEFORE:
            one_sum, two_sum = cross((((0, 1), sets[0]),))
            twos[k], one_sum = after(twos[k], one_sum)
        if Y_AFTER[k] >= 0:
            twos[k], ones[Y_AFTER[k]] = after(twos[k], ones[Y_AFTER[k]])
        if CHAIN and k > 0:
            twos[k], onward[k - 1] = after(twos[k], onward[k - 1])
        for later in range(pieces):
            if Z_AFTER[later] == k and not Z_BEHIND[later]:
                twos[k], mine[later] = after(twos[k], mine[later])
                twos[later] = lax.ppermute(mine[later], "ch", ahead)
        onward[k] = jnp.where(odd_chip, twos[k], mine[k])
        for later in range(pieces):
            if Z_AFTER[later] == k and Z_BEHIND[later]:
                onward[k], mine[later] = after(onward[k], mine[later])
                twos[later] = lax.ppermute(mine[later], "ch", ahead)
        if k < pieces - 1:
            ones[k] = lax.ppermute(onward[k], "ch", beside)
    final = pieces - 1
    middle = sets[1][0]
    onward[final], twos[middle] = after(onward[final], twos[middle])
    if NEAR_BEFORE == pieces:
        twos[middle], near = after(twos[middle], near)
    if LAST_TIE:
        ones[final - 1], twos[middle] = after(ones[final - 1], twos[middle])

    def put(kinds, out, *values):
        aliased = out is not None
        operands = [*values, out] if aliased else list(values)
        return call(
            functools.partial(put_kernel, kinds),
            "put",
            out_shape,
            [vmem()] * len(values) + [hbm()] * aliased,
            hbm(),
            1000,
            4 * nbytes,
            input_output_aliases={len(values): 0} if aliased else {},
            scratch_shapes=[
                pltpu.VMEM(near_shape.shape, jnp.float32),
                pltpu.SemaphoreType.DMA((len(kinds), 2, band_width)),
            ],
        )(*operands)

    ones[final] = lax.ppermute(onward[final], "ch", beside)
    one_sum, two_sum, two_sent = cross(
        (((0,), sets[1]), ((1,), sets[1] + sets[2])), (one_sum, two_sum), 1
    )
    two_got = lax.ppermute(two_sent, "ch", mate)
    out = put(("two",), None, two_sum)
    if PUT_TIE:
        one_sum, out = after(one_sum, out)
    one_sum, one_sent = cross((((0,), sets[2]),), (one_sum,), 0)
    one_got = lax.ppermute(one_sent, "ch", mate)
    out = put(("one", "near"), out, one_sum, two_got, near)
    return put(("far",), out, one_got)


def solution(mesh):
    placed = (P(None, None, "fq", "ch"), P("fq"))
    return jax.shard_map(
        shards,
        mesh=mesh,
        in_specs=placed,
        out_specs=P(None, None, "fq", "ch", None),
        check_vma=False,
    )
```

```python
import functools

import jax
import jax.numpy as jnp
from jax import lax
from jax.experimental import pallas as pl
from jax.experimental.pallas import tpu as pltpu
from jax.sharding import PartitionSpec as P

BANDS = 8
ROUNDS = 4
SMOOTH = 4
EPS = 1e-06

GROUP = 16
SIZES = (4,8,12,12,12,12,12,12,12)
BLOCK = 24
RAW = 4
TERMS = 3
Z_AFTER = (-1, -1, -1, -1, 2, 2, 3, 5, 6)
Z_BEHIND = (0, 0, 0, 0, 0, 1, 0, 1, 0)
Y_AFTER = (-1, -1, 0, 1, 2, 3, 4, 5, 6)
LAST_TIE = 0
PUT_TIE = 1
CHAIN = 0
SETS = (5, 2, 2)
EDGE_AFTER = -1
LEFT_AFTER = -1
OTHER_AFTER = 0
NEAR_BEFORE = 8
CROSS_BEFORE = 7
VMEM_LIMIT = 10 * 1024 * 1024


def vmem():
    return pl.BlockSpec(memory_space=pltpu.VMEM)


def smem():
    return pl.BlockSpec(memory_space=pltpu.SMEM)


def hbm():
    return pl.BlockSpec(memory_space=pltpu.HBM)


def call(kernel, name, out_shape, in_specs, out_specs, flops, moved, **more):
    return pl.pallas_call(
        kernel,
        out_shape=out_shape,
        in_specs=in_specs,
        out_specs=out_specs,
        compiler_params=pltpu.CompilerParams(vmem_limit_bytes=VMEM_LIMIT),
        cost_estimate=pl.CostEstimate(flops=flops, bytes_accessed=moved, transcendentals=0),
        name=name,
        **more,
    )


def power_kernel(x_ref, power_ref, edge_ref, *pieces):
    rows, width, _ = x_ref.shape
    for index, piece in enumerate(pieces):
        piece[...] = x_ref[sum(SIZES[:index]) : sum(SIZES[: index + 1])]

    def step(i, total):
        value = x_ref[i].astype(jnp.float32)
        return total + value * value

    total = lax.fori_loop(0, rows, step, jnp.zeros(power_ref.shape, jnp.float32), unroll=8)
    power = total / (rows // 2)
    power_ref[...] = power
    low = lax.axis_index("fq") == 0
    edge_ref[...] = jnp.where(low, power[width - SMOOTH :], power[:SMOOTH])


def left_kernel(x_ref, power_ref, halo_ref, left_ref, *refs):
    whites, padded = refs[:-1], refs[-1]
    rows = x_ref.shape[0]
    fq = lax.axis_index("fq")
    width, channels = power_ref.shape
    bin_total = width * lax.axis_size("fq")
    padded[...] = jnp.zeros_like(padded)
    padded[8 : 8 + width, :] = power_ref[...]

    @pl.when(fq > 0)
    def _():
        padded[8 - SMOOTH : 8, :] = halo_ref[...]

    @pl.when(fq == 0)
    def _():
        padded[8 + width : 8 + width + SMOOTH, :] = halo_ref[...]

    total = padded[8 - SMOOTH : 8 - SMOOTH + width, :]
    for offset in range(1, 2 * SMOOTH + 1):
        total = total + padded[8 - SMOOTH + offset : 8 - SMOOTH + offset + width, :]
    bins = fq * width + lax.broadcasted_iota(jnp.int32, (width, channels), 0)
    counts = jnp.minimum(bins + SMOOTH, bin_total - 1) - jnp.maximum(bins - SMOOTH, 0) + 1
    scale = lax.rsqrt(total / counts.astype(jnp.float32) + EPS)
    rest = scale
    for term in range(TERMS):
        part = rest.astype(jnp.bfloat16)
        whites[0][SIZES[RAW] + term] = part
        rest = rest - part.astype(jnp.float32)

    span = BLOCK * GROUP
    for block in range(rows // BLOCK):
        first = block * BLOCK
        for group in range(width // GROUP):
            here = slice(group * GROUP, (group + 1) * GROUP)
            raw = x_ref[first : first + BLOCK, here, :].astype(jnp.float32)
            white = (raw * scale[here][None]).astype(jnp.bfloat16)
            for index, piece in enumerate(whites):
                start = sum(SIZES[: RAW + index])
                low, high = max(start, first), min(start + SIZES[RAW + index], first + BLOCK)
                if low < high:
                    piece[low - start : high - start, here, :] = white[low - first : high - first]
            turned = white.reshape(span, channels).T
            left_ref[group, :, block * span : (block + 1) * span] = turned


def band_at(bounds_ref, bands, bin_index):
    return sum((bounds_ref[k] <= bin_index).astype(jnp.int32) for k in range(1, bands))


def each_band(bounds_ref, groups, bands, add):
    for group in range(groups):
        band = band_at(bounds_ref, bands, group * GROUP)
        add(group, band, bounds_ref[band], bounds_ref[band + 1])
    for band in range(1, bands):
        low = bounds_ref[band]
        high = jnp.where(low % GROUP == 0, low, bounds_ref[band + 1])
        add(jnp.minimum(low // GROUP, groups - 1), band, low, high)


def inside(group, low, high, shape, dimension):
    bins = group * GROUP + lax.broadcasted_iota(jnp.int32, shape, dimension) % GROUP
    return ((bins >= low) & (bins < high)).astype(jnp.float32).astype(jnp.bfloat16)


def near_kernel(bounds_ref, norm_ref, own_ref, mate_ref, out_ref):
    groups, channels, span = own_ref.shape
    half = span // 2
    bands = out_ref.shape[1]
    out_ref[...] = jnp.zeros_like(out_ref)

    def add(group, band, low, high):
        right = mate_ref[group] * inside(group, low, high, (1, span), 1)
        halves = []
        for start in (0, half):
            left = jnp.concatenate(
                [own_ref[group, :, begin : begin + half] for begin in (start, half - start)], axis=0
            )
            halves.append(
                lax.dot_general(
                    left,
                    right[:, start : start + half],
                    (((1,), (1,)), ((), ())),
                    preferred_element_type=jnp.float32,
                )
            )
        out_ref[0, band] += (halves[0][:channels] + halves[1][:channels]) * norm_ref[band]
        out_ref[1, band] += (halves[0][channels:] - halves[1][channels:]) * norm_ref[band]

    @pl.when(lax.axis_index("ch") % 2 == 1)
    def _():
        each_band(bounds_ref, groups, bands, add)


def cross_kernel(jobs, first, sent, bounds_ref, norm_ref, own_ref, mate_ref, *refs):
    present = sorted({kind for kinds, _ in jobs for kind in kinds})
    work = []
    for kinds, these in jobs:
        taken = []
        for _ in kinds:
            taken.append(refs[: len(these)])
            refs = refs[len(these) :]
        work.append((kinds, these, taken))
    if not first:
        befores, refs = refs[: len(present)], refs[len(present) :]
    sums = dict(zip(present, refs))
    width, channels = work[0][2][0][0].shape[1:]
    bands = refs[0].shape[2]
    half = own_ref.shape[2] // 2
    for index, kind in enumerate(present):
        sums[kind][...] = jnp.zeros_like(refs[0]) if first else befores[index][...]

    def column(right, these, here, held):
        scale = None
        if first:
            for term in range(TERMS):
                part = right[RAW][SIZES[RAW] + term, here, :].astype(jnp.float32)
                scale = part if scale is None else scale + part
        blocks = []
        for ref, number in zip(right, these):
            size = SIZES[number]
            block = ref[:size, here, :]
            if number < RAW:
                block = (block.astype(jnp.float32) * scale[None]).astype(jnp.bfloat16)
            blocks.append((block * held[None]).reshape(size * GROUP, channels))
        return jnp.concatenate(blocks, axis=0)

    def multiply(kinds, these, taken, owners):
        start, stop = sum(SIZES[: these[0]]) * GROUP, sum(SIZES[: these[-1] + 1]) * GROUP
        turned = start >= half
        shift = -half if turned else half
        parts = slice(start, stop), slice(start + shift, stop + shift)

        def add(group, band, low, high):
            begin = group * GROUP
            here = pl.ds(begin if isinstance(group, int) else pl.multiple_of(begin, GROUP), GROUP)
            held = inside(group, low, high, (GROUP, channels), 0)
            left = jnp.concatenate(
                [ref[group, :, part] for ref in (own_ref, mate_ref)[:owners] for part in parts], axis=0
            )
            right = jnp.concatenate([column(right, these, here, held) for right in taken], axis=1)
            product = jnp.dot(left, right, preferred_element_type=jnp.float32) * norm_ref[band]
            for k, kind in enumerate(kinds):
                for owner in range(owners):
                    for part in range(2):
                        row = (2 * owner + part) * channels
                        term = product[row : row + channels, k * channels : (k + 1) * channels]
                        sums[kind][part, owner, band] += -term if part and turned else term

        each_band(bounds_ref, width // GROUP, bands, add)

    core = lax.axis_index("ch") % 2
    for kinds, these, taken in work:
        if kinds == (1,):
            pl.when(core == 0)(functools.partial(multiply, kinds, these, taken, 1))
            pl.when(core == 1)(functools.partial(multiply, kinds, these, taken, 2))
        else:
            multiply(kinds, these, taken, 2)
    if sent is not None:
        refs[-1][...] = sums[sent][:, 1].astype(jnp.bfloat16)


def put_kernel(kinds, *refs):
    out_ref, wide, sems = refs[-3:]
    core = lax.axis_index("ch") % 2
    turns = {"one": 1, "two": 3, "far": 2 * core, "near": 2 - 2 * core}
    copies = []
    for kind in kinds:
        value_ref, refs = refs[0], refs[1:]
        if kind == "near":
            near_ref, refs = refs[0], refs[1:]
        for part in range(2):
            for band in range(out_ref.shape[2]):
                if kind in ("one", "two"):
                    source = value_ref.at[part, 0, band]
                else:
                    value = value_ref[part, band].astype(jnp.float32)
                    if kind == "near":
                        value = jnp.where(core == 0, value, near_ref[part, band])
                    wide[part, band] = value
                    source = wide.at[part, band]
                turn = turns[kind]
                sem = sems.at[kinds.index(kind), part, band]
                copies.append(pltpu.make_async_copy(source, out_ref.at[part, turn, band], sem))
                copies[-1].start()
    for copy in copies:
        copy.wait()


def after(value, other):
    return lax.optimization_barrier((value, other))


def shards(spectra, band_ids):
    parts, windows, width, channels = spectra.shape
    rows = parts * windows
    count = lax.axis_size("ch")
    fq_count = lax.axis_size("fq")
    index = lax.axis_index("ch")
    fq = lax.axis_index("fq")
    even_core = index % 2 == 0
    odd_chip = (index // 2) % 2 == 1

    ahead = [(i, (i + 4) % count) for i in range(count)]
    beside = [(i, i ^ 2) for i in range(count)]
    mate = [(i, i ^ 1) for i in range(count)]

    own = spectra.reshape(rows, width, channels)
    pieces = len(SIZES)
    heights = [size + (TERMS if k == RAW else 0) for k, size in enumerate(SIZES)]
    block = jax.ShapeDtypeStruct((width, channels), jnp.float32)
    edge = jax.ShapeDtypeStruct((SMOOTH, channels), jnp.float32)
    held = [jax.ShapeDtypeStruct((h, width, channels), jnp.bfloat16) for h in heights]
    groups = width // GROUP
    left_shape = jax.ShapeDtypeStruct((groups, channels, rows * GROUP), jnp.bfloat16)
    nbytes = rows * width * channels * 2

    power, edge, *early = call(
        power_kernel,
        "power",
        (block, edge, *held[:RAW]),
        [vmem()],
        (vmem(),) * (2 + RAW),
        nbytes,
        nbytes,
    )(own)
    band_width = BANDS // fq_count
    local_band = band_ids - fq * band_width
    below = local_band[:, None] < jnp.arange(band_width + 1, dtype=jnp.int32)[None, :]
    bounds = jnp.sum(below.astype(jnp.int32), axis=0)
    norms = 1.0 / jnp.sqrt(windows * (bounds[1:] - bounds[:-1]).astype(jnp.float32))
    power, norms = after(power, norms)

    twos = {k: lax.ppermute(early[k], "ch", ahead) for k in range(RAW)}
    if EDGE_AFTER >= 0:
        twos[EDGE_AFTER], edge = after(twos[EDGE_AFTER], edge)
    halo = lax.ppermute(edge, "fq", [(0, 1), (1, 0)])
    if LEFT_AFTER >= 0:
        twos[LEFT_AFTER], halo = after(twos[LEFT_AFTER], halo)
    left, *late = call(
        left_kernel,
        "left",
        (left_shape, *held[RAW:]),
        [vmem()] * 3,
        (vmem(),) * (1 + pieces - RAW),
        nbytes,
        nbytes,
        scratch_shapes=[pltpu.VMEM((width + 16, channels), jnp.float32)],
    )(own, power, halo)
    mine = early + late

    out_shape = jax.ShapeDtypeStruct((2, ROUNDS, band_width, channels, channels), jnp.float32)
    sum_shape = jax.ShapeDtypeStruct((2, 2, band_width, channels, channels), jnp.float32)
    near_shape = jax.ShapeDtypeStruct((2, band_width, channels, channels), jnp.float32)
    send_shape = jax.ShapeDtypeStruct((2, band_width, channels, channels), jnp.bfloat16)

    sets = [tuple(range(sum(SETS[:s]), sum(SETS[: s + 1]))) for s in range(len(SETS))]
    ones, onward = {}, {}

    def cross(jobs, befores=(), sent=None):
        operands = [bounds, norms, left, other]
        for kinds, these in jobs:
            for kind in kinds:
                operands += [(ones, twos)[kind][k] for k in these]
        operands += befores
        count = len({kind for kinds, _ in jobs for kind in kinds})
        products = sum(len(kinds) * SIZES[k] for kinds, these in jobs for k in these)
        return call(
            functools.partial(cross_kernel, jobs, not befores, sent),
            "cross",
            (sum_shape,) * count + (send_shape,) * (sent is not None),
            [smem(), smem()] + [vmem()] * (len(operands) - 2),
            (vmem(),) * (count + (sent is not None)),
            8 * products * width * channels * channels,
            0 * nbytes,
        )(*operands)

    left, twos[OTHER_AFTER] = after(left, twos[OTHER_AFTER])
    other = lax.ppermute(left, "ch", mate)
    near = call(
        near_kernel,
        "near",
        near_shape,
        [smem(), smem(), vmem(), vmem()],
        vmem(),
        1000,
        1000,
    )(bounds, norms, left, other)

    for k in range(pieces):
        if k == NEAR_BEFORE:
            twos[k], near = after(twos[k], near)
        if k == CROSS_BEFORE:
            one_sum, two_sum = cross((((0, 1), sets[0]),))
            twos[k], one_sum = after(twos[k], one_sum)
        if Y_AFTER[k] >= 0:
            twos[k], ones[Y_AFTER[k]] = after(twos[k], ones[Y_AFTER[k]])
        if CHAIN and k > 0:
            twos[k], onward[k - 1] = after(twos[k], onward[k - 1])
        for later in range(pieces):
            if Z_AFTER[later] == k and not Z_BEHIND[later]:
                twos[k], mine[later] = after(twos[k], mine[later])
                twos[later] = lax.ppermute(mine[later], "ch", ahead)
        onward[k] = jnp.where(odd_chip, twos[k], mine[k])
        for later in range(pieces):
            if Z_AFTER[later] == k and Z_BEHIND[later]:
                onward[k], mine[later] = after(onward[k], mine[later])
                twos[later] = lax.ppermute(mine[later], "ch", ahead)
        if k < pieces - 1:
            ones[k] = lax.ppermute(onward[k], "ch", beside)
    final = pieces - 1
    middle = sets[1][0]
    onward[final], twos[middle] = after(onward[final], twos[middle])
    if NEAR_BEFORE == pieces:
        twos[middle], near = after(twos[middle], near)
    if LAST_TIE:
        ones[final - 1], twos[middle] = after(ones[final - 1], twos[middle])

    def put(kinds, out, *values):
        aliased = out is not None
        operands = [*values, out] if aliased else list(values)
        return call(
            functools.partial(put_kernel, kinds),
            "put",
            out_shape,
            [vmem()] * len(values) + [hbm()] * aliased,
            hbm(),
            1000,
            4 * nbytes,
            input_output_aliases={len(values): 0} if aliased else {},
            scratch_shapes=[
                pltpu.VMEM(near_shape.shape, jnp.float32),
                pltpu.SemaphoreType.DMA((len(kinds), 2, band_width)),
            ],
        )(*operands)

    ones[final] = lax.ppermute(onward[final], "ch", beside)
    one_sum, two_sum, two_sent = cross(
        (((0,), sets[1]), ((1,), sets[1] + sets[2])), (one_sum, two_sum), 1
    )
    two_got = lax.ppermute(two_sent, "ch", mate)
    out = put(("two",), None, two_sum)
    if PUT_TIE:
        one_sum, out = after(one_sum, out)
    one_sum, one_sent = cross((((0,), sets[2]),), (one_sum,), 0)
    one_got = lax.ppermute(one_sent, "ch", mate)
    out = put(("one", "near"), out, one_sum, two_got, near)
    return put(("far",), out, one_got)


def solution(mesh):
    placed = (P(None, None, "fq", "ch"), P("fq"))
    return jax.shard_map(
        shards,
        mesh=mesh,
        in_specs=placed,
        out_specs=P(None, None, "fq", "ch", None),
        check_vma=False,
    )
```

```python
import functools

import jax
import jax.numpy as jnp
from jax import lax
from jax.experimental import pallas as pl
from jax.experimental.pallas import tpu as pltpu
from jax.sharding import PartitionSpec as P

BANDS = 8
ROUNDS = 4
SMOOTH = 4
EPS = 1e-06

GROUP = 16
SIZES = (4,8,12,12,12,12,12,12,12)
BLOCK = 24
RAW = 3
TERMS = 3
Z_AFTER = (-1, -1, -1, 0, 1, 2, 3, 5, 6)
Z_BEHIND = (0, 0, 0, 0, 0, 0, 0, 1, 0)
Y_AFTER = (-1, -1, 0, 1, 2, 3, 4, 5, 6)
LAST_TIE = 0
PUT_TIE = 1
CHAIN = 1
SETS = (5, 2, 2)
EDGE_AFTER = -1
LEFT_AFTER = -1
OTHER_AFTER = 0
NEAR_BEFORE = 8
CROSS_BEFORE = 7
VMEM_LIMIT = 10 * 1024 * 1024


def vmem():
    return pl.BlockSpec(memory_space=pltpu.VMEM)


def smem():
    return pl.BlockSpec(memory_space=pltpu.SMEM)


def hbm():
    return pl.BlockSpec(memory_space=pltpu.HBM)


def call(kernel, name, out_shape, in_specs, out_specs, flops, moved, **more):
    return pl.pallas_call(
        kernel,
        out_shape=out_shape,
        in_specs=in_specs,
        out_specs=out_specs,
        compiler_params=pltpu.CompilerParams(vmem_limit_bytes=VMEM_LIMIT),
        cost_estimate=pl.CostEstimate(flops=flops, bytes_accessed=moved, transcendentals=0),
        name=name,
        **more,
    )


def power_kernel(x_ref, power_ref, edge_ref, *pieces):
    rows, width, _ = x_ref.shape
    for index, piece in enumerate(pieces):
        piece[...] = x_ref[sum(SIZES[:index]) : sum(SIZES[: index + 1])]

    def step(i, total):
        value = x_ref[i].astype(jnp.float32)
        return total + value * value

    total = lax.fori_loop(0, rows, step, jnp.zeros(power_ref.shape, jnp.float32), unroll=8)
    power = total / (rows // 2)
    power_ref[...] = power
    low = lax.axis_index("fq") == 0
    edge_ref[...] = jnp.where(low, power[width - SMOOTH :], power[:SMOOTH])


def left_kernel(x_ref, power_ref, halo_ref, left_ref, *refs):
    whites, padded = refs[:-1], refs[-1]
    rows = x_ref.shape[0]
    fq = lax.axis_index("fq")
    width, channels = power_ref.shape
    bin_total = width * lax.axis_size("fq")
    padded[...] = jnp.zeros_like(padded)
    padded[8 : 8 + width, :] = power_ref[...]

    @pl.when(fq > 0)
    def _():
        padded[8 - SMOOTH : 8, :] = halo_ref[...]

    @pl.when(fq == 0)
    def _():
        padded[8 + width : 8 + width + SMOOTH, :] = halo_ref[...]

    total = padded[8 - SMOOTH : 8 - SMOOTH + width, :]
    for offset in range(1, 2 * SMOOTH + 1):
        total = total + padded[8 - SMOOTH + offset : 8 - SMOOTH + offset + width, :]
    bins = fq * width + lax.broadcasted_iota(jnp.int32, (width, channels), 0)
    counts = jnp.minimum(bins + SMOOTH, bin_total - 1) - jnp.maximum(bins - SMOOTH, 0) + 1
    scale = lax.rsqrt(total / counts.astype(jnp.float32) + EPS)
    rest = scale
    for term in range(TERMS):
        part = rest.astype(jnp.bfloat16)
        whites[0][SIZES[RAW] + term] = part
        rest = rest - part.astype(jnp.float32)

    span = BLOCK * GROUP
    for block in range(rows // BLOCK):
        first = block * BLOCK
        for group in range(width // GROUP):
            here = slice(group * GROUP, (group + 1) * GROUP)
            raw = x_ref[first : first + BLOCK, here, :].astype(jnp.float32)
            white = (raw * scale[here][None]).astype(jnp.bfloat16)
            for index, piece in enumerate(whites):
                start = sum(SIZES[: RAW + index])
                low, high = max(start, first), min(start + SIZES[RAW + index], first + BLOCK)
                if low < high:
                    piece[low - start : high - start, here, :] = white[low - first : high - first]
            turned = white.reshape(span, channels).T
            left_ref[group, :, block * span : (block + 1) * span] = turned


def band_at(bounds_ref, bands, bin_index):
    return sum((bounds_ref[k] <= bin_index).astype(jnp.int32) for k in range(1, bands))


def each_band(bounds_ref, groups, bands, add):
    for group in range(groups):
        band = band_at(bounds_ref, bands, group * GROUP)
        add(group, band, bounds_ref[band], bounds_ref[band + 1])
    for band in range(1, bands):
        low = bounds_ref[band]
        high = jnp.where(low % GROUP == 0, low, bounds_ref[band + 1])
        add(jnp.minimum(low // GROUP, groups - 1), band, low, high)


def inside(group, low, high, shape, dimension):
    bins = group * GROUP + lax.broadcasted_iota(jnp.int32, shape, dimension) % GROUP
    return ((bins >= low) & (bins < high)).astype(jnp.float32).astype(jnp.bfloat16)


def near_kernel(bounds_ref, norm_ref, own_ref, mate_ref, out_ref):
    groups, channels, span = own_ref.shape
    half = span // 2
    bands = out_ref.shape[1]
    out_ref[...] = jnp.zeros_like(out_ref)

    def add(group, band, low, high):
        right = mate_ref[group] * inside(group, low, high, (1, span), 1)
        halves = []
        for start in (0, half):
            left = jnp.concatenate(
                [own_ref[group, :, begin : begin + half] for begin in (start, half - start)], axis=0
            )
            halves.append(
                lax.dot_general(
                    left,
                    right[:, start : start + half],
                    (((1,), (1,)), ((), ())),
                    preferred_element_type=jnp.float32,
                )
            )
        out_ref[0, band] += (halves[0][:channels] + halves[1][:channels]) * norm_ref[band]
        out_ref[1, band] += (halves[0][channels:] - halves[1][channels:]) * norm_ref[band]

    @pl.when(lax.axis_index("ch") % 2 == 1)
    def _():
        each_band(bounds_ref, groups, bands, add)


def cross_kernel(jobs, first, sent, bounds_ref, norm_ref, own_ref, mate_ref, *refs):
    present = sorted({kind for kinds, _ in jobs for kind in kinds})
    work = []
    for kinds, these in jobs:
        taken = []
        for _ in kinds:
            taken.append(refs[: len(these)])
            refs = refs[len(these) :]
        work.append((kinds, these, taken))
    if not first:
        befores, refs = refs[: len(present)], refs[len(present) :]
    sums = dict(zip(present, refs))
    width, channels = work[0][2][0][0].shape[1:]
    bands = refs[0].shape[2]
    half = own_ref.shape[2] // 2
    for index, kind in enumerate(present):
        sums[kind][...] = jnp.zeros_like(refs[0]) if first else befores[index][...]

    def column(right, these, here, held):
        scale = None
        if first:
            for term in range(TERMS):
                part = right[RAW][SIZES[RAW] + term, here, :].astype(jnp.float32)
                scale = part if scale is None else scale + part
        blocks = []
        for ref, number in zip(right, these):
            size = SIZES[number]
            block = ref[:size, here, :]
            if number < RAW:
                block = (block.astype(jnp.float32) * scale[None]).astype(jnp.bfloat16)
            blocks.append((block * held[None]).reshape(size * GROUP, channels))
        return jnp.concatenate(blocks, axis=0)

    def multiply(kinds, these, taken, owners):
        start, stop = sum(SIZES[: these[0]]) * GROUP, sum(SIZES[: these[-1] + 1]) * GROUP
        turned = start >= half
        shift = -half if turned else half
        parts = slice(start, stop), slice(start + shift, stop + shift)

        def add(group, band, low, high):
            begin = group * GROUP
            here = pl.ds(begin if isinstance(group, int) else pl.multiple_of(begin, GROUP), GROUP)
            held = inside(group, low, high, (GROUP, channels), 0)
            left = jnp.concatenate(
                [ref[group, :, part] for ref in (own_ref, mate_ref)[:owners] for part in parts], axis=0
            )
            right = jnp.concatenate([column(right, these, here, held) for right in taken], axis=1)
            product = jnp.dot(left, right, preferred_element_type=jnp.float32) * norm_ref[band]
            for k, kind in enumerate(kinds):
                for owner in range(owners):
                    for part in range(2):
                        row = (2 * owner + part) * channels
                        term = product[row : row + channels, k * channels : (k + 1) * channels]
                        sums[kind][part, owner, band] += -term if part and turned else term

        each_band(bounds_ref, width // GROUP, bands, add)

    core = lax.axis_index("ch") % 2
    for kinds, these, taken in work:
        if kinds == (1,):
            pl.when(core == 0)(functools.partial(multiply, kinds, these, taken, 1))
            pl.when(core == 1)(functools.partial(multiply, kinds, these, taken, 2))
        else:
            multiply(kinds, these, taken, 2)
    if sent is not None:
        refs[-1][...] = sums[sent][:, 1].astype(jnp.bfloat16)


def put_kernel(kinds, *refs):
    out_ref, wide, sems = refs[-3:]
    core = lax.axis_index("ch") % 2
    turns = {"one": 1, "two": 3, "far": 2 * core, "near": 2 - 2 * core}
    copies = []
    for kind in kinds:
        value_ref, refs = refs[0], refs[1:]
        if kind == "near":
            near_ref, refs = refs[0], refs[1:]
        for part in range(2):
            for band in range(out_ref.shape[2]):
                if kind in ("one", "two"):
                    source = value_ref.at[part, 0, band]
                else:
                    value = value_ref[part, band].astype(jnp.float32)
                    if kind == "near":
                        value = jnp.where(core == 0, value, near_ref[part, band])
                    wide[part, band] = value
                    source = wide.at[part, band]
                turn = turns[kind]
                sem = sems.at[kinds.index(kind), part, band]
                copies.append(pltpu.make_async_copy(source, out_ref.at[part, turn, band], sem))
                copies[-1].start()
    for copy in copies:
        copy.wait()


def after(value, other):
    return lax.optimization_barrier((value, other))


def shards(spectra, band_ids):
    parts, windows, width, channels = spectra.shape
    rows = parts * windows
    count = lax.axis_size("ch")
    fq_count = lax.axis_size("fq")
    index = lax.axis_index("ch")
    fq = lax.axis_index("fq")
    even_core = index % 2 == 0
    odd_chip = (index // 2) % 2 == 1

    ahead = [(i, (i + 4) % count) for i in range(count)]
    beside = [(i, i ^ 2) for i in range(count)]
    mate = [(i, i ^ 1) for i in range(count)]

    own = spectra.reshape(rows, width, channels)
    pieces = len(SIZES)
    heights = [size + (TERMS if k == RAW else 0) for k, size in enumerate(SIZES)]
    block = jax.ShapeDtypeStruct((width, channels), jnp.float32)
    edge = jax.ShapeDtypeStruct((SMOOTH, channels), jnp.float32)
    held = [jax.ShapeDtypeStruct((h, width, channels), jnp.bfloat16) for h in heights]
    groups = width // GROUP
    left_shape = jax.ShapeDtypeStruct((groups, channels, rows * GROUP), jnp.bfloat16)
    nbytes = rows * width * channels * 2

    power, edge, *early = call(
        power_kernel,
        "power",
        (block, edge, *held[:RAW]),
        [vmem()],
        (vmem(),) * (2 + RAW),
        nbytes,
        nbytes,
    )(own)
    band_width = BANDS // fq_count
    local_band = band_ids - fq * band_width
    below = local_band[:, None] < jnp.arange(band_width + 1, dtype=jnp.int32)[None, :]
    bounds = jnp.sum(below.astype(jnp.int32), axis=0)
    norms = 1.0 / jnp.sqrt(windows * (bounds[1:] - bounds[:-1]).astype(jnp.float32))
    power, norms = after(power, norms)

    twos = {k: lax.ppermute(early[k], "ch", ahead) for k in range(RAW)}
    if EDGE_AFTER >= 0:
        twos[EDGE_AFTER], edge = after(twos[EDGE_AFTER], edge)
    halo = lax.ppermute(edge, "fq", [(0, 1), (1, 0)])
    if LEFT_AFTER >= 0:
        twos[LEFT_AFTER], halo = after(twos[LEFT_AFTER], halo)
    left, *late = call(
        left_kernel,
        "left",
        (left_shape, *held[RAW:]),
        [vmem()] * 3,
        (vmem(),) * (1 + pieces - RAW),
        nbytes,
        nbytes,
        scratch_shapes=[pltpu.VMEM((width + 16, channels), jnp.float32)],
    )(own, power, halo)
    mine = early + late

    out_shape = jax.ShapeDtypeStruct((2, ROUNDS, band_width, channels, channels), jnp.float32)
    sum_shape = jax.ShapeDtypeStruct((2, 2, band_width, channels, channels), jnp.float32)
    near_shape = jax.ShapeDtypeStruct((2, band_width, channels, channels), jnp.float32)
    send_shape = jax.ShapeDtypeStruct((2, band_width, channels, channels), jnp.bfloat16)

    sets = [tuple(range(sum(SETS[:s]), sum(SETS[: s + 1]))) for s in range(len(SETS))]
    ones, onward = {}, {}

    def cross(jobs, befores=(), sent=None):
        operands = [bounds, norms, left, other]
        for kinds, these in jobs:
            for kind in kinds:
                operands += [(ones, twos)[kind][k] for k in these]
        operands += befores
        count = len({kind for kinds, _ in jobs for kind in kinds})
        products = sum(len(kinds) * SIZES[k] for kinds, these in jobs for k in these)
        return call(
            functools.partial(cross_kernel, jobs, not befores, sent),
            "cross",
            (sum_shape,) * count + (send_shape,) * (sent is not None),
            [smem(), smem()] + [vmem()] * (len(operands) - 2),
            (vmem(),) * (count + (sent is not None)),
            8 * products * width * channels * channels,
            0 * nbytes,
        )(*operands)

    left, twos[OTHER_AFTER] = after(left, twos[OTHER_AFTER])
    other = lax.ppermute(left, "ch", mate)
    near = call(
        near_kernel,
        "near",
        near_shape,
        [smem(), smem(), vmem(), vmem()],
        vmem(),
        1000,
        1000,
    )(bounds, norms, left, other)

    for k in range(pieces):
        if k == NEAR_BEFORE:
            twos[k], near = after(twos[k], near)
        if k == CROSS_BEFORE:
            one_sum, two_sum = cross((((0, 1), sets[0]),))
            twos[k], one_sum = after(twos[k], one_sum)
        if Y_AFTER[k] >= 0:
            twos[k], ones[Y_AFTER[k]] = after(twos[k], ones[Y_AFTER[k]])
        if CHAIN and k > 0:
            twos[k], onward[k - 1] = after(twos[k], onward[k - 1])
        for later in range(pieces):
            if Z_AFTER[later] == k and not Z_BEHIND[later]:
                twos[k], mine[later] = after(twos[k], mine[later])
                twos[later] = lax.ppermute(mine[later], "ch", ahead)
        onward[k] = jnp.where(odd_chip, twos[k], mine[k])
        for later in range(pieces):
            if Z_AFTER[later] == k and Z_BEHIND[later]:
                onward[k], mine[later] = after(onward[k], mine[later])
                twos[later] = lax.ppermute(mine[later], "ch", ahead)
        if k < pieces - 1:
            ones[k] = lax.ppermute(onward[k], "ch", beside)
    final = pieces - 1
    middle = sets[1][0]
    onward[final], twos[middle] = after(onward[final], twos[middle])
    if NEAR_BEFORE == pieces:
        twos[middle], near = after(twos[middle], near)
    if LAST_TIE:
        ones[final - 1], twos[middle] = after(ones[final - 1], twos[middle])

    def put(kinds, out, *values):
        aliased = out is not None
        operands = [*values, out] if aliased else list(values)
        return call(
            functools.partial(put_kernel, kinds),
            "put",
            out_shape,
            [vmem()] * len(values) + [hbm()] * aliased,
            hbm(),
            1000,
            4 * nbytes,
            input_output_aliases={len(values): 0} if aliased else {},
            scratch_shapes=[
                pltpu.VMEM(near_shape.shape, jnp.float32),
                pltpu.SemaphoreType.DMA((len(kinds), 2, band_width)),
            ],
        )(*operands)

    ones[final] = lax.ppermute(onward[final], "ch", beside)
    one_sum, two_sum, two_sent = cross(
        (((0,), sets[1]), ((1,), sets[1] + sets[2])), (one_sum, two_sum), 1
    )
    two_got = lax.ppermute(two_sent, "ch", mate)
    out = put(("two",), None, two_sum)
    if PUT_TIE:
        one_sum, out = after(one_sum, out)
    one_sum, one_sent = cross((((0,), sets[2]),), (one_sum,), 0)
    one_got = lax.ppermute(one_sent, "ch", mate)
    out = put(("one", "near"), out, one_sum, two_got, near)
    return put(("far",), out, one_got)


def solution(mesh):
    placed = (P(None, None, "fq", "ch"), P("fq"))
    return jax.shard_map(
        shards,
        mesh=mesh,
        in_specs=placed,
        out_specs=P(None, None, "fq", "ch", None),
        check_vma=False,
    )
```
